32 devices in a mesh: groups: 2 (over x), band: 16 (over z, y, core).
Axes of the slice: x: 2, y: 2, z: 4, core: 2. Of those that a mesh axis runs over, the one named last changes fastest.
Arguments:
- grid_features: bfloat16 [131072, 227], P(('groups', 'band')), parts along dimension 0, may hold values from -6 to 6
- mesh_latent: bfloat16 [8192, 512], P(('groups', 'band')), parts along dimension 0, may hold values from -6 to 6
- embed_in: bfloat16 [227, 512], replicated, may hold values from -0.375 to 0.375
- embed_out: bfloat16 [512, 512], replicated, may hold values from -0.25 to 0.25
- embed_gain: float32 [512], replicated, may hold values from 0.1 to 1.9
- interp: bfloat16 [256, 4, 32, 256], P('band'), may hold values from -0.375 to 0.375
- block_mask: int32 [256, 4], replicated, may hold values 0 or 1
- tile_list: int32 [256, 4], replicated, may hold values from 0 to 127, as said below
- mesh_up: bfloat16 [512, 512], replicated, may hold values from -0.25 to 0.25
- mesh_down: bfloat16 [512, 512], replicated, may hold values from -0.25 to 0.25
- mesh_gain: float32 [512], replicated, may hold values from 0.1 to 1.9
Outputs:
- grid_out: bfloat16 [131072, 512], P(('groups', 'band')), parts along dimension 0
- mesh_out: bfloat16 [8192, 512], P(('groups', 'band')), parts along dimension 0
The draws below stay inside these ranges and needn't reach their ends.
There are 2 independent parts, one for each index of `groups`. The reference program is written for one: setup_inputs(seed, part) draws one part's arguments, and reference() takes and returns one part's arrays. A program takes and returns all parts, laid end to end along the dimension named above; an argument that names none is the same for every part. Nothing has to cross between parts.
Inputs may be any that keep to these rules, and one draw needn't show every extreme that they name: `tile_list`: tile t is owned by band index t // 8. Number the 64 entries of one band index's rows in row order as p; no two entries with equal p // 16 name tiles of one owner, so at most 4 entries of one band index name one owner's tiles, and exactly 4 do for some owner.
All inputs are finite; a program needn't handle non-finite values.
Results may differ from the reference program's by a relative error of at most 0.007.
Values may be sent and summed in bfloat16 or wider, within the bound.
No kernel may reach another device: no remote copies, remote signals or barrier semaphores. Data moves between devices by JAX's collectives and lax.ppermute only.
A program may use at most 128 MiB of HBM per device.

```python
import jax
import jax.numpy as jnp
from jax import lax

D = 512
CHANNELS = 227
R = 256
K = 4
TILE_M = 32
TILES_DEV = 8
BLK_DEV = 16
BLOCKS = 256
GRID = 65536
TILES = 128
NODES = 4096
N_BAND = 16


def draw_tile_list(key, part):
    key = jax.random.fold_in(key, 11)

    def one_band(band_key):
        first_key, second_key = jax.random.split(band_key)
        owners = jax.random.permutation(first_key, N_BAND)
        number = jnp.arange(BLK_DEV * K)
        owner = owners[number % N_BAND]
        local = jax.random.randint(second_key, (BLK_DEV * K,), 0, TILES_DEV)
        return (owner * TILES_DEV + local).astype(jnp.int32).reshape(BLK_DEV, K)
    band_keys = jax.random.split(key, N_BAND)
    return jax.vmap(one_band)(band_keys).reshape(BLOCKS, K)


def set_ends(entries, key, least, top_value):
    longest = entries.shape.index(max(entries.shape))
    spots = []
    for shift in (0, 1):
        where = [jax.random.randint(jax.random.fold_in(key, axis), (), 0, length) for axis, length in enumerate(entries.shape)]
        where[longest] = (where[longest] + shift) % entries.shape[longest]
        spots.append(tuple(where))
    return entries.at[spots[0]].set(least).at[spots[1]].set(top_value)


def block_scale(stream_key, extent, cuts, low, largest):
    def one(axis_at, shards_of):
        draws = jax.random.uniform(jax.random.fold_in(jax.random.fold_in(stream_key, 6), axis_at), (shards_of,), jnp.float32, low / len(cuts), largest / len(cuts))
        return jnp.repeat(jnp.exp(draws), extent[axis_at] // shards_of).reshape((-1,) + (1,) * (len(extent) - axis_at - 1))

    loudness = one(*cuts[0])
    for cut in cuts[1:]:
        loudness = loudness * one(*cut)
    return loudness


def scatter_about(key, extent, width, limit, cuts=(), kind=jnp.bfloat16):
    array = width * jax.random.normal(key, extent, jnp.float32)
    if cuts:
        array = array * block_scale(key, extent, cuts, -0.22, 0.18)
    return jnp.clip(array, -limit, limit).astype(kind)


def setup_inputs(seed: int = 0, part: int = 0) -> dict:
    key_of = jax.random.split(jax.random.key(seed), 12)
    part_splits = jax.random.split(jax.random.fold_in(key_of[11], part), 12)
    return {
        "grid_features": scatter_about(part_splits[0], (GRID, CHANNELS), 1.0, 6.0, ((0, 16),)),
        "mesh_latent": scatter_about(part_splits[1], (NODES, D), 1.0, 6.0, ((0, 16),)),
        "embed_in": scatter_about(key_of[2], (CHANNELS, D), CHANNELS ** -0.5, 0.375),
        "embed_out": scatter_about(key_of[3], (D, D), D ** -0.5, 0.25),
        "embed_gain": jnp.clip(1.0 + 0.18 * jax.random.normal(key_of[4], (D,), jnp.float32), 0.1, 1.9),
        "interp": scatter_about(key_of[5], (BLOCKS, K, TILE_M, R), R ** -0.5, 0.375, ((0, 16),)),
        "block_mask": set_ends((jax.random.randint(key_of[6], (BLOCKS, K), 0, 4) < 3).astype(jnp.int32), jax.random.fold_in(key_of[6], 1), 0, 1),
        "tile_list": draw_tile_list(jax.random.fold_in(key_of[11], 71), part),
        "mesh_up": scatter_about(key_of[8], (D, D), D ** -0.5, 0.25),
        "mesh_down": scatter_about(key_of[9], (D, D), D ** -0.5, 0.25),
        "mesh_gain": jnp.clip(1.0 + 0.18 * jax.random.normal(key_of[10], (D,), jnp.float32), 0.1, 1.9),
    }


def layer_norm(values, gain):
    centred = values - lax.optimization_barrier(jnp.mean(values, axis=-1, keepdims=True))
    spread = lax.optimization_barrier(jnp.mean(centred * centred, axis=-1, keepdims=True))
    return centred * lax.rsqrt(spread + 1e-05) * gain.astype(jnp.float32)

def reference(grid_features, mesh_latent, embed_in, embed_out, embed_gain, interp, block_mask, tile_list, mesh_up, mesh_down, mesh_gain):
    w_first = embed_in.astype(jnp.float32)
    w_second = embed_out.astype(jnp.float32)

    def embed(rows):
        hidden_grid = jax.nn.silu(jnp.dot(rows.astype(jnp.float32), w_first)).astype(jnp.bfloat16)
        before = jnp.dot(hidden_grid.astype(jnp.float32), w_second)
        return layer_norm(before, embed_gain).astype(jnp.bfloat16)
    latent = lax.map(embed, grid_features.reshape(N_BAND, BLK_DEV * R, CHANNELS)).reshape(BLOCKS, R, D)
    weights = interp.astype(jnp.float32)
    maskf = block_mask.astype(jnp.float32)
    partial_value = (jnp.einsum('bkmr,brd->bkmd', weights, latent.astype(jnp.float32)) * maskf[:, :, None, None]).astype(jnp.bfloat16)
    aggregate = jax.ops.segment_sum(partial_value.astype(jnp.float32).reshape(BLOCKS * K, TILE_M, D), tile_list.reshape(-1).astype(jnp.int32), num_segments=TILES)
    mesh_in = (mesh_latent.astype(jnp.float32).reshape(TILES, TILE_M, D) + aggregate).reshape(NODES, D)
    normed = layer_norm(mesh_in, mesh_gain).astype(jnp.bfloat16)
    mesh_hidden = jax.nn.silu(jnp.dot(normed.astype(jnp.float32), mesh_up.astype(jnp.float32))).astype(jnp.bfloat16)
    mesh_out = (mesh_in + jnp.dot(mesh_hidden.astype(jnp.float32), mesh_down.astype(jnp.float32))).astype(jnp.bfloat16)
    tile_value = mesh_out.reshape(TILES, TILE_M, D)[tile_list.astype(jnp.int32)].astype(jnp.float32) * maskf[:, :, None, None]
    back = jnp.einsum('bkmr,bkmd->brd', weights, tile_value)
    grid_out = (latent.astype(jnp.float32) + back).reshape(GRID, D).astype(jnp.bfloat16)
    return (grid_out, mesh_out)
```

```python
import functools

import jax
import jax.numpy as jnp
from jax import lax
from jax.experimental import pallas as pl
from jax.experimental.pallas import tpu as pltpu
from jax.sharding import PartitionSpec as P

F32 = jnp.float32
BF16 = jnp.bfloat16
VMEM_LIMIT = 48 * 1024 * 1024


def silu(values):
    half = 0.5 * values
    return half * (1.0 + jnp.tanh(half))


def layer_norm(values, gain):
    centred = values - jnp.mean(values, axis=-1, keepdims=True)
    spread = jnp.mean(centred * centred, axis=-1, keepdims=True)
    return centred * lax.rsqrt(spread + 1e-05) * gain


def embed_kernel(
    first, per_step, info_ref, x_ref, w1_ref, w2_ref, gain_ref, interp_ref, *rest
):
    latent_ref, *outs, placed = rest[1:] if first else rest
    step = pl.program_id(0)
    list_len, tile_rows, block_rows = interp_ref.shape[1:]
    hidden = silu(jnp.dot(x_ref[...], w1_ref[...], preferred_element_type=F32)).astype(BF16)
    before = jnp.dot(hidden, w2_ref[...], preferred_element_type=F32)
    latent = layer_norm(before, gain_ref[...]).astype(BF16)
    latent_ref[...] = latent
    for b in range(per_step):
        weights = interp_ref[b].reshape(list_len * tile_rows, block_rows)
        part = jnp.dot(
            weights, latent[b * block_rows : (b + 1) * block_rows], preferred_element_type=F32
        )
        for k in range(list_len):
            entry = first + (step * per_step + b) * list_len + k
            masked = part[k * tile_rows : (k + 1) * tile_rows] * info_ref[1, entry].astype(F32)
            placed[info_ref[0, entry]] = masked.astype(BF16)

    @pl.when(step == pl.num_programs(0) - 1)
    def _():
        count = outs[0].shape[0]
        for number, out in enumerate(outs):
            out[...] = placed[number * count : (number + 1) * count]


def combine_kernel(slots, ways, core, tile_ref, *refs):
    parts, (send_ref, own_ref, total) = refs[: slots * ways], refs[slots * ways :]
    away = pl.program_id(0)
    total[...] = jnp.zeros_like(total)
    for way in range(ways):
        for slot in range(slots):
            for other in range(core):
                tile = tile_ref[way, slot, away * core + other]
                total[other, tile] += parts[way * slots + slot][other].astype(F32)
    own_ref[0] = total[0]
    send_ref[0] = total[1].astype(BF16)


def add_kernel(own_ref, other_ref, here_ref, *there):
    here_ref[...] = own_ref[0] + other_ref[0].astype(F32)
    for away, out in enumerate(there, 1):
        out[...] = (own_ref[away] + other_ref[away].astype(F32)).astype(BF16)


def mesh_kernel(latent_ref, up_ref, down_ref, gain_ref, here_ref, *rest):
    others, out_ref = rest[:-1], rest[-1]
    mesh_in = latent_ref[...].astype(F32) + here_ref[...]
    for other in others:
        mesh_in = mesh_in + other[...].astype(F32)
    normed = layer_norm(mesh_in, gain_ref[...]).astype(BF16)
    hidden = silu(jnp.dot(normed, up_ref[...], preferred_element_type=F32)).astype(BF16)
    out_ref[...] = (
        mesh_in + jnp.dot(hidden, down_ref[...], preferred_element_type=F32)
    ).astype(BF16)


def back_kernel(count, per_step, info_ref, latent_ref, interp_ref, *rest):
    pieces, (out_ref, held, picked, sems) = rest[:count], rest[count:]
    step = pl.program_id(0)
    list_len, tile_rows, block_rows = interp_ref.shape[1:]

    @pl.when(step == 0)
    def _():
        copies = [
            pltpu.make_async_copy(pieces[i], held.at[i], sems.at[i]) for i in range(count)
        ]
        for copy in copies:
            copy.start()
        for copy in copies:
            copy.wait()

    for b in range(per_step):
        for k in range(list_len):
            entry = (step * per_step + b) * list_len + k
            rows = pl.ds(pl.multiple_of(info_ref[2, entry] * tile_rows, tile_rows), tile_rows)
            value = held[info_ref[3, entry], rows].astype(F32) * info_ref[1, entry].astype(F32)
            picked[b, k * tile_rows : (k + 1) * tile_rows] = value.astype(BF16)
        weights = interp_ref[b].reshape(list_len * tile_rows, block_rows)
        back = lax.dot_general(
            weights, picked[b], (((0,), (0,)), ((), ())), preferred_element_type=F32
        )
        rows = slice(b * block_rows, (b + 1) * block_rows)
        out_ref[rows] = (latent_ref[rows].astype(F32) + back).astype(BF16)


def whole(array):
    zeros = (0,) * array.ndim
    return pl.BlockSpec(array.shape, lambda *_: zeros)


def params():
    return pltpu.CompilerParams(vmem_limit_bytes=VMEM_LIMIT)


def cost(flops, *arrays):
    size = sum(a.size * a.dtype.itemsize for a in arrays)
    return pl.CostEstimate(flops=int(flops), bytes_accessed=int(size), transcendentals=0)


def shape(dims, kind=BF16):
    return jax.ShapeDtypeStruct(dims, kind)


def on_device(
    n_y,
    grid_features,
    mesh_latent,
    embed_in,
    embed_out,
    embed_gain,
    interp,
    block_mask,
    tile_list,
    mesh_up,
    mesh_down,
    mesh_gain,
):
    n_band = lax.axis_size("band")
    n_core = 2
    n_z = n_band // (n_y * n_core)
    me = lax.axis_index("band")
    blk_count, list_len, tile_rows, block_rows = interp.shape
    channels, width = embed_in.shape
    tiles_here = mesh_latent.shape[0] // tile_rows
    node_rows = mesh_latent.shape[0]
    entries = blk_count * list_len
    slots = entries // n_band
    group_blocks = n_band // list_len
    ahead = n_z * n_core

    def index_of(z, y, c):
        return (z % n_z * n_y + y) * n_core + c

    def place_of(i):
        return i // (n_y * n_core), i // n_core % n_y, i % n_core

    def move(value, where):
        pairs = [(i, index_of(*where(*place_of(i)))) for i in range(n_band)]
        return lax.ppermute(value, "band", pairs)

    def over_core(value):
        return move(value, lambda z, y, c: (z, y, 1 - c))

    def over_y(value):
        return move(value, lambda z, y, c: (z, 1 - y, c))

    def over_z(value, by):
        return move(value, lambda z, y, c: (z + by, y, c))

    all_tiles = tile_list.reshape(n_band, entries)
    all_mask = block_mask.reshape(n_band, entries)

    def relative(index):
        tiles = lax.dynamic_index_in_dim(all_tiles, index, 0, keepdims=False)
        owner = tiles // tiles_here
        z, y, c = place_of(owner)
        my_z, my_y, my_c = place_of(index)
        rel = ((y - my_y) % n_y * n_z + (z - my_z) % n_z) * n_core + (c - my_c) % n_core
        return rel, tiles % tiles_here

    my_mask = lax.dynamic_index_in_dim(all_mask, me, 0, keepdims=False)
    my_rel, my_local = relative(me)
    my_z, my_y, my_c = place_of(me)
    z_of, rest_of = my_rel // n_core % n_z, my_rel % n_core + my_rel // ahead * ahead
    piece_of = rest_of + (n_z - z_of) % n_z * n_core
    info = jnp.stack([my_rel, my_mask, my_local, piece_of])

    def by_place(rel, local):
        rel, local = rel.reshape(slots, n_band, 1), local.reshape(slots, n_band, 1)
        return jnp.sum(jnp.where(rel == jnp.arange(n_band), local, 0), axis=1)

    tables = [by_place(my_rel, my_local)[:, :ahead]]
    if n_y > 1:
        tables.append(by_place(*relative(index_of(my_z, 1 - my_y, my_c)))[:, ahead:])
    tables = jnp.stack(tables)

    gain = embed_gain.reshape(1, width)
    per_step = min(2, group_blocks)
    rows = per_step * block_rows
    latent, kept, sent = [], [], []
    for slot in range(slots):
        begin = slot * group_blocks // per_step
        outs = pl.pallas_call(
            functools.partial(embed_kernel, slot * n_band, per_step),
            out_shape=[shape((blk_count * block_rows, width))]
            + [shape((ahead, tile_rows, width))] * n_y,
            grid_spec=pltpu.PrefetchScalarGridSpec(
                num_scalar_prefetch=1,
                grid=(group_blocks // per_step,),
                in_specs=[
                    pl.BlockSpec((rows, channels), lambda i, _, begin=begin: (begin + i, 0)),
                    whole(embed_in),
                    whole(embed_out),
                    whole(gain),
                    pl.BlockSpec(
                        (per_step,) + interp.shape[1:],
                        lambda i, _, begin=begin: (begin + i, 0, 0, 0),
                    ),
                ]
                + [pl.BlockSpec(memory_space=pl.ANY)] * len(latent),
                out_specs=[pl.BlockSpec((rows, width), lambda i, _, begin=begin: (begin + i, 0))]
                + [pl.BlockSpec((ahead, tile_rows, width), lambda i, _: (0, 0, 0))] * n_y,
                scratch_shapes=[pltpu.VMEM((n_band, tile_rows, width), BF16)],
            ),
            input_output_aliases={6: 0} if latent else {},
            compiler_params=params(),
            cost_estimate=cost(
                2 * group_blocks * block_rows * width * (channels + width + list_len * tile_rows),
                grid_features,
                interp,
            ),
            name=f"embed_{slot}",
        )(info, grid_features, embed_in, embed_out, gain, interp, *latent)
        latent = [outs[0]]
        kept.append(outs[1])
        if n_y > 1:
            sent.append(over_y(outs[2]))

    parts = kept + sent
    dense = (n_z, tiles_here, tile_rows, width)
    one = (1,) + dense[1:]
    to_core, own = pl.pallas_call(
        functools.partial(combine_kernel, slots, n_y, n_core),
        out_shape=[shape(dense), shape(dense, F32)],
        grid_spec=pltpu.PrefetchScalarGridSpec(
            num_scalar_prefetch=1,
            grid=(n_z,),
            in_specs=[pl.BlockSpec((n_core, tile_rows, width), lambda i, _: (i, 0, 0))]
            * len(parts),
            out_specs=[pl.BlockSpec(one, lambda i, _: (i, 0, 0, 0))] * 2,
            scratch_shapes=[pltpu.VMEM((n_core,) + dense[1:], F32)],
        ),
        compiler_params=params(),
        cost_estimate=cost(0, *parts),
        name="combine",
    )(tables, *parts)
    from_core = over_core(to_core)
    flat = (n_z, node_rows, width)
    chunks = pl.pallas_call(
        add_kernel,
        out_shape=[shape(flat[1:], F32)] + [shape(flat[1:])] * (n_z - 1),
        compiler_params=params(),
        cost_estimate=cost(0, own, from_core),
        name="add_cores",
    )(own.reshape(flat), from_core.reshape(flat))
    arrived = [over_z(chunk, by) for by, chunk in enumerate(chunks[1:], 1)]
    mesh_out = pl.pallas_call(
        mesh_kernel,
        out_shape=shape((node_rows, width)),
        compiler_params=params(),
        cost_estimate=cost(4 * node_rows * width * width, mesh_up, mesh_down),
        name="mesh_step",
    )(mesh_latent, mesh_up, mesh_down, mesh_gain.reshape(1, width), chunks[0], *arrived)

    line = [mesh_out] + [over_z(mesh_out, by) for by in range(1, n_z)]
    if n_y > 1:
        line = line + [over_y(piece) for piece in line]
    pieces = []
    for piece in line:
        pieces += [piece, over_core(piece)]

    latent = latent[0]
    per_step = 2
    rows = per_step * block_rows
    steps = blk_count // per_step
    grid_out = pl.pallas_call(
        functools.partial(back_kernel, len(pieces), per_step),
        out_shape=shape((blk_count * block_rows, width)),
        grid_spec=pltpu.PrefetchScalarGridSpec(
            num_scalar_prefetch=1,
            grid=(steps,),
            in_specs=[
                pl.BlockSpec((rows, width), lambda i, _: (i, 0)),
                pl.BlockSpec((per_step,) + interp.shape[1:], lambda i, _: (i, 0, 0, 0)),
            ]
            + [pl.BlockSpec(memory_space=pl.ANY)] * len(pieces),
            out_specs=pl.BlockSpec((rows, width), lambda i, _: (i, 0)),
            scratch_shapes=[
                pltpu.VMEM((len(pieces), node_rows, width), BF16),
                pltpu.VMEM((per_step, list_len * tile_rows, width), BF16),
                pltpu.SemaphoreType.DMA((len(pieces),)),
            ],
        ),
        compiler_params=params(),
        cost_estimate=cost(
            2 * blk_count * block_rows * width * list_len * tile_rows, latent, latent, interp
        ),
        name="back",
    )(info, latent, interp, *pieces)
    return (grid_out, mesh_out)


def solution(mesh):
    placed = (
        P(("groups", "band"), None),
        P(("groups", "band"), None),
        P(),
        P(),
        P(),
        P("band", None, None, None),
        P(),
        P(),
        P(),
        P(),
        P(),
    )
    n_y = max(1, 4 // mesh.shape["groups"])
    return jax.shard_map(
        functools.partial(on_device, n_y),
        mesh=mesh,
        in_specs=placed,
        out_specs=(P(("groups", "band"), None), P(("groups", "band"), None)),
        check_vma=False,
    )
```

```python
import functools

import jax
import jax.numpy as jnp
from jax import lax
from jax.experimental import pallas as pl
from jax.experimental.pallas import tpu as pltpu
from jax.sharding import PartitionSpec as P

F32 = jnp.float32
BF16 = jnp.bfloat16
VMEM_LIMIT = 56 * 1024 * 1024


def silu(values):
    half = 0.5 * values
    return half * (1.0 + jnp.tanh(half))


def layer_norm(values, gain):
    centred = values - jnp.mean(values, axis=-1, keepdims=True)
    spread = jnp.mean(centred * centred, axis=-1, keepdims=True)
    return centred * lax.rsqrt(spread + 1e-05) * gain


def embed_kernel(
    per_step, info_ref, x_ref, w1_ref, w2_ref, gain_ref, interp_ref, latent_ref, *rest
):
    outs, placed = rest[:-1], rest[-1]
    step = pl.program_id(0)
    list_len, tile_rows, block_rows = interp_ref.shape[1:]
    first = lax.dot_general(
        x_ref[...], w1_ref[...], (((0,), (0,)), ((), ())), preferred_element_type=F32
    )
    before = jnp.dot(silu(first).astype(BF16), w2_ref[...], preferred_element_type=F32)
    latent = layer_norm(before, gain_ref[...]).astype(BF16)
    latent_ref[...] = latent
    for b in range(per_step):
        weights = interp_ref[b].reshape(list_len * tile_rows, block_rows)
        part = jnp.dot(
            weights, latent[b * block_rows : (b + 1) * block_rows], preferred_element_type=F32
        )
        for k in range(list_len):
            entry = (step * per_step + b) * list_len + k
            masked = part[k * tile_rows : (k + 1) * tile_rows] * info_ref[1, entry].astype(F32)
            placed[info_ref[0, entry]] = masked.astype(BF16)

    @pl.when(step == pl.num_programs(0) - 1)
    def _():
        count = outs[0].shape[0]
        for number, out in enumerate(outs):
            out[...] = placed[number * count : (number + 1) * count]


def add_entries(total, table_ref, base, parts):
    for way, part in enumerate(parts):
        for slot in range(part.shape[0]):
            total[table_ref[way, base + slot]] += part[slot].astype(F32)


def chunk_kernel(slots, distance, chips, table_ref, *refs):
    kept, other, came = refs[0:2], refs[2:4], refs[4:-3]
    outs, total = refs[-3:-1], refs[-1]
    tiles = total.shape[0]
    half = tiles // 2
    for side in range(2):
        lower = slice(0, half) if side == 0 else slice(half, tiles)
        if not came:
            total[...] = jnp.zeros_like(total)
        elif came[side].shape[0] == tiles:
            total[...] = came[side][...].astype(F32)
        else:
            total[...] = jnp.zeros_like(total)
            total[lower] = came[side][...].astype(F32)
        owner = distance if side == 0 else chips - distance
        add_entries(total, table_ref, owner * slots, [kept[side], other[side]])
        out = outs[side]
        out[...] = (total[...] if out.shape[0] == tiles else total[lower]).astype(BF16)


def mesh_kernel(table_ref, latent_ref, up_ref, down_ref, gain_ref, kept, other, *rest):
    came, out_ref, total = rest[:-2], rest[-2], rest[-1]
    tiles, tile_rows, width = total.shape
    half = tiles // 2
    total[...] = latent_ref[...].astype(F32).reshape(total.shape)
    for side, value in enumerate(came):
        if value.shape[0] == tiles:
            total[...] += value[...].astype(F32)
        else:
            part = slice(0, half) if side == 0 else slice(half, tiles)
            total[part] += value[...].astype(F32)
    add_entries(total, table_ref, 0, [kept, other])
    mesh_in = total[...].reshape(tiles * tile_rows, width)
    normed = layer_norm(mesh_in, gain_ref[...]).astype(BF16)
    hidden = silu(jnp.dot(normed, up_ref[...], preferred_element_type=F32)).astype(BF16)
    out_ref[...] = (
        mesh_in + jnp.dot(hidden, down_ref[...], preferred_element_type=F32)
    ).astype(BF16)


def back_kernel(places, per_step, info_ref, latent_ref, interp_ref, *rest):
    count = len(places)
    pieces, (out_ref, held, picked, sems) = rest[:count], rest[count:]
    step = pl.program_id(0)
    list_len, tile_rows, block_rows = interp_ref.shape[1:]

    @pl.when(step == 0)
    def _():
        copies = []
        for i, (place, row) in enumerate(places):
            into = held.at[place, pl.ds(row, pieces[i].shape[0])]
            copies.append(pltpu.make_async_copy(pieces[i], into, sems.at[i]))
        for copy in copies:
            copy.start()
        for copy in copies:
            copy.wait()

    for b in range(per_step):
        for k in range(list_len):
            entry = (step * per_step + b) * list_len + k
            rows = pl.ds(pl.multiple_of(info_ref[2, entry] * tile_rows, tile_rows), tile_rows)
            value = held[info_ref[3, entry], rows].astype(F32) * info_ref[1, entry].astype(F32)
            picked[b, k * tile_rows : (k + 1) * tile_rows] = value.astype(BF16)
        weights = interp_ref[b].reshape(list_len * tile_rows, block_rows)
        back = lax.dot_general(
            weights, picked[b], (((0,), (0,)), ((), ())), preferred_element_type=F32
        )
        rows = slice(b * block_rows, (b + 1) * block_rows)
        out_ref[rows] = (latent_ref[rows].astype(F32) + back).astype(BF16)


def whole(array):
    zeros = (0,) * array.ndim
    return pl.BlockSpec(array.shape, lambda *_: zeros)


def params():
    return pltpu.CompilerParams(vmem_limit_bytes=VMEM_LIMIT)


def cost(flops, *arrays):
    size = sum(a.size * a.dtype.itemsize for a in arrays)
    return pl.CostEstimate(flops=int(flops), bytes_accessed=int(size), transcendentals=0)


def shape(dims, kind=BF16):
    return jax.ShapeDtypeStruct(dims, kind)


def on_device(
    n_y,
    grid_features,
    mesh_latent,
    embed_in,
    embed_out,
    embed_gain,
    interp,
    block_mask,
    tile_list,
    mesh_up,
    mesh_down,
    mesh_gain,
):
    n_band = lax.axis_size("band")
    n_core = 2
    chips = n_band // n_core
    n_z = chips // n_y
    me = lax.axis_index("band")
    blk_count, list_len, tile_rows, block_rows = interp.shape
    channels, width = embed_in.shape
    node_rows = mesh_latent.shape[0]
    tiles_here = node_rows // tile_rows
    entries = blk_count * list_len
    slots = entries // n_band
    far = chips // 2

    def ring_of(index):
        z, y = index // (n_y * n_core), index // n_core % n_y
        return z + y * (chips - 1 - 2 * z)

    def index_at(ring, core):
        ring = ring % chips
        z, y = (ring, 0) if ring < n_z else (chips - 1 - ring, 1)
        return (z * n_y + y) * n_core + core

    def over_core(value):
        return lax.ppermute(value, "band", [(i, i ^ 1) for i in range(n_band)])

    def over_ring(value, by):
        pairs = [(i, index_at(ring_of(i) + by, i % n_core)) for i in range(n_band)]
        return lax.ppermute(value, "band", pairs)

    def mine(table, index):
        rows = lax.dynamic_slice_in_dim(table.T, index * blk_count, blk_count, 1)
        return rows.T.reshape(entries)

    def relative(index):
        tiles = mine(tile_list, index)
        owner = tiles // tiles_here
        return (ring_of(owner) - ring_of(index)) % chips, (owner - index) % n_core, tiles % tiles_here

    slot_of = jnp.arange(entries, dtype=jnp.int32) // n_band
    ahead, across, local = relative(me)
    info = jnp.stack(
        [(across * chips + ahead) * slots + slot_of, mine(block_mask, me), local, ahead * n_core + across]
    )

    def by_place(ahead, across, local, which):
        place = jnp.where(across == which, ahead * slots + slot_of, -1)
        spots = jnp.arange(chips * slots, dtype=jnp.int32)
        return jnp.sum(jnp.where(place[:, None] == spots, local[:, None], 0), axis=0)

    tables = jnp.stack(
        [by_place(ahead, across, local, 0), by_place(*relative(me + 1 - me % 2 * 2), 1)]
    )

    gain = embed_gain.reshape(1, width)
    per_step = 2
    rows = per_step * block_rows
    held_shape = (chips * slots, tile_rows, width)
    latent, kept, sent = pl.pallas_call(
        functools.partial(embed_kernel, per_step),
        out_shape=[shape((blk_count * block_rows, width))] + [shape(held_shape)] * n_core,
        grid_spec=pltpu.PrefetchScalarGridSpec(
            num_scalar_prefetch=1,
            grid=(blk_count // per_step,),
            in_specs=[
                pl.BlockSpec((channels, rows), lambda i, _: (0, i)),
                whole(embed_in),
                whole(embed_out),
                whole(gain),
                pl.BlockSpec((per_step,) + interp.shape[1:], lambda i, _: (i, 0, 0, 0)),
            ],
            out_specs=[pl.BlockSpec((rows, width), lambda i, _: (i, 0))]
            + [pl.BlockSpec(held_shape, lambda i, _: (0, 0, 0))] * n_core,
            scratch_shapes=[pltpu.VMEM((entries, tile_rows, width), BF16)],
        ),
        compiler_params=params(),
        cost_estimate=cost(
            2 * blk_count * block_rows * width * (channels + width + list_len * tile_rows),
            grid_features,
            interp,
        ),
        name="embed",
    )(info, grid_features.T, embed_in, embed_out, gain, interp)
    other = over_core(sent)

    def entries_of(owner):
        return pl.BlockSpec((slots, tile_rows, width), lambda i, _: (owner, 0, 0))

    dense = (tiles_here, tile_rows, width)
    came = []
    for distance in range(far, 0, -1):
        out = (tiles_here // 2,) + dense[1:] if distance == far else dense
        sides = [entries_of(distance), entries_of(chips - distance)]
        chunks = pl.pallas_call(
            functools.partial(chunk_kernel, slots, distance, chips),
            out_shape=[shape(out)] * 2,
            grid_spec=pltpu.PrefetchScalarGridSpec(
                num_scalar_prefetch=1,
                grid=(1,),
                in_specs=sides + sides + [whole(c) for c in came],
                out_specs=[pl.BlockSpec(out, lambda i, _: (0, 0, 0))] * 2,
                scratch_shapes=[pltpu.VMEM(dense, F32)],
            ),
            compiler_params=params(),
            cost_estimate=cost(0, *came, *came),
            name=f"chunk_{distance}",
        )(tables, kept, kept, other, other, *came)
        came = [over_ring(chunks[0], 1), over_ring(chunks[1], -1)]

    mesh_gain = mesh_gain.reshape(1, width)
    mesh_out = pl.pallas_call(
        mesh_kernel,
        out_shape=shape((node_rows, width)),
        grid_spec=pltpu.PrefetchScalarGridSpec(
            num_scalar_prefetch=1,
            grid=(1,),
            in_specs=[whole(a) for a in (mesh_latent, mesh_up, mesh_down, mesh_gain)]
            + [entries_of(0)] * 2
            + [whole(c) for c in came],
            out_specs=pl.BlockSpec((node_rows, width), lambda i, _: (0, 0)),
            scratch_shapes=[pltpu.VMEM(dense, F32)],
        ),
        compiler_params=params(),
        cost_estimate=cost(4 * node_rows * width * width, mesh_up, mesh_down),
        name="mesh_step",
    )(tables, mesh_latent, mesh_up, mesh_down, mesh_gain, kept, other, *came)

    pieces, places = [], []

    def keep(piece, owner, row=0):
        for across, value in enumerate((piece, over_core(piece))):
            pieces.append(value)
            places.append((owner % chips * n_core + across, row))

    right = left = mesh_out
    for distance in range(1, far):
        right, left = over_ring(right, 1), over_ring(left, -1)
        if distance == 1:
            keep(mesh_out, 0)
        keep(right, -distance)
        keep(left, distance)
    half = node_rows // 2
    right, left = over_ring(right[:half], 1), over_ring(left[half:], -1)
    keep(right, far)
    keep(left, far, half)

    per_step = 2
    rows = per_step * block_rows
    grid_out = pl.pallas_call(
        functools.partial(back_kernel, places, per_step),
        out_shape=shape((blk_count * block_rows, width)),
        grid_spec=pltpu.PrefetchScalarGridSpec(
            num_scalar_prefetch=1,
            grid=(blk_count // per_step,),
            in_specs=[
                pl.BlockSpec((rows, width), lambda i, _: (i, 0)),
                pl.BlockSpec((per_step,) + interp.shape[1:], lambda i, _: (i, 0, 0, 0)),
            ]
            + [pl.BlockSpec(memory_space=pl.ANY)] * len(pieces),
            out_specs=pl.BlockSpec((rows, width), lambda i, _: (i, 0)),
            scratch_shapes=[
                pltpu.VMEM((n_band, node_rows, width), BF16),
                pltpu.VMEM((per_step, list_len * tile_rows, width), BF16),
                pltpu.SemaphoreType.DMA((len(pieces),)),
            ],
        ),
        compiler_params=params(),
        cost_estimate=cost(
            2 * blk_count * block_rows * width * list_len * tile_rows, latent, latent, interp
        ),
        name="back",
    )(info, latent, interp, *pieces)
    return (grid_out, mesh_out)


def solution(mesh):
    placed = (
        P(("groups", "band"), None),
        P(("groups", "band"), None),
        P(),
        P(),
        P(),
        P("band", None, None, None),
        P(),
        P(),
        P(),
        P(),
        P(),
    )
    n_y = max(1, 4 // mesh.shape["groups"])
    return jax.shard_map(
        functools.partial(on_device, n_y),
        mesh=mesh,
        in_specs=placed,
        out_specs=(P(("groups", "band"), None), P(("groups", "band"), None)),
        check_vma=False,
    )
```

```python
import functools

import jax
import jax.numpy as jnp
from jax import lax
from jax.experimental import pallas as pl
from jax.experimental.pallas import tpu as pltpu
from jax.sharding import PartitionSpec as P

F32 = jnp.float32
BF16 = jnp.bfloat16
N_CORE = 2


def silu(values):
    half = 0.5 * values
    return half * (1.0 + jnp.tanh(half))


def layer_norm(values, gain):
    centred = values - jnp.mean(values, axis=-1, keepdims=True)
    spread = jnp.mean(centred * centred, axis=-1, keepdims=True)
    return centred * lax.rsqrt(spread + 1e-05) * gain


def split(value, size):
    if size & (size - 1) == 0:
        return lax.shift_right_logical(value, size.bit_length() - 1), value & (size - 1)
    return lax.div(value, size), lax.rem(value, size)


class Ring:
    def __init__(self, n_band, n_y, tiles):
        self.n_band, self.n_y, self.tiles = n_band, n_y, tiles
        self.chips = n_band // N_CORE
        self.far = self.chips // 2

    def place(self, index):
        chip, core = split(index, N_CORE)
        z, y = split(chip, self.n_y)
        return z + y * (self.chips - 1 - 2 * z), core

    def index(self, ring, core):
        ring = ring % self.chips
        n_z = self.chips // self.n_y
        z, y = (ring, 0) if ring < n_z else (self.chips - 1 - ring, 1)
        return (z * self.n_y + y) * N_CORE + core

    def over_core(self, value):
        return lax.ppermute(value, "band", [(i, i ^ 1) for i in range(self.n_band)])

    def over(self, value, by):
        pairs = []
        for i in range(self.n_band):
            chip, core = divmod(i, N_CORE)
            z, y = divmod(chip, self.n_y)
            ring = z if y == 0 else self.chips - 1 - z
            pairs.append((i, self.index(ring + by, core)))
        return lax.ppermute(value, "band", pairs)

    def entry(self, lists_ref, me, block, k):
        owner, tile = split(lists_ref[k, block], self.tiles)
        ring, core = self.place(owner)
        my_ring, my_core = self.place(me)
        ahead = split(ring - my_ring + self.chips, self.chips)[1]
        return ahead, core ^ my_core, tile


def embed_kernel(
    ring, per_step, slots, me_ref, lists_ref, mask_ref,
    x_ref, w1_ref, w2_ref, gain_ref, interp_ref,
    latent_ref, kept_ref, sent_ref, table_ref, placed,
):
    step = pl.program_id(0)
    me = me_ref[0]
    list_len, tile_rows, block_rows = interp_ref.shape[1:]
    blk_count = pl.num_programs(0) * per_step

    def spot(index, b, k):
        block = step * per_step + b
        ahead, across, tile = ring.entry(lists_ref, index, index * blk_count + block, k)
        slot = split(block * list_len + k, ring.n_band)[0]
        return (across * ring.chips + ahead) * slots + slot, tile

    first = lax.dot_general(
        x_ref[...], w1_ref[...], (((0,), (0,)), ((), ())), preferred_element_type=F32
    )
    before = jnp.dot(silu(first).astype(BF16), w2_ref[...], preferred_element_type=F32)
    latent = layer_norm(before, gain_ref[...]).astype(BF16)
    latent_ref[...] = latent
    for b in range(per_step):
        weights = interp_ref[b].reshape(list_len * tile_rows, block_rows)
        part = jnp.dot(
            weights, latent[b * block_rows : (b + 1) * block_rows], preferred_element_type=F32
        )
        for k in range(list_len):
            place, tile = spot(me, b, k)
            table_ref[0, place] = tile
            there, its_tile = spot(me ^ 1, b, k)
            table_ref[1, there] = its_tile
            mask = mask_ref[k, me * blk_count + step * per_step + b].astype(F32)
            masked = part[k * tile_rows : (k + 1) * tile_rows] * mask
            placed[place] = masked.astype(BF16)

    @pl.when(step == pl.num_programs(0) - 1)
    def _():
        count = kept_ref.shape[0]
        kept_ref[...] = placed[:count]
        sent_ref[...] = placed[count:]


def add_entries(total, table_ref, owner, kept, other, chips):
    slots = kept.shape[0]
    for slot in range(slots):
        total[table_ref[0, owner * slots + slot]] += kept[slot].astype(F32)
        total[table_ref[1, (chips + owner) * slots + slot]] += other[slot].astype(F32)


def far_kernel(ring, table_ref, *refs):
    kept, other = refs[0:3], refs[3:6]
    far_right, far_left, next_right, next_left, total = refs[6:]
    half = total.shape[0] // 2
    owners = (ring.far, ring.far - 1, ring.chips - ring.far + 1)
    for number, owner in enumerate(owners):
        total[...] = jnp.zeros_like(total)
        add_entries(total, table_ref, owner, kept[number], other[number], ring.chips)
        if number == 0:
            far_right[...] = total[:half].astype(BF16)
            far_left[...] = total[half:].astype(BF16)
        elif number == 1:
            next_right[...] = total[half:].astype(BF16)
        else:
            next_left[...] = total[:half].astype(BF16)


def own_kernel(ring, table_ref, kept, other, own):
    number = pl.program_id(0)
    owner = number + (number >= ring.far).astype(jnp.int32)
    own[...] = jnp.zeros_like(own)
    add_entries(own.at[0], table_ref, owner, kept, other, ring.chips)


def mesh_kernel(
    latent_ref, up_ref, down_ref, gain_ref, own, right_a, left_b, right_b, left_a,
    out_ref, out_a, out_b,
):
    tiles, tile_rows, width = own.shape[1:]
    half = tiles // 2
    lower = own[0, :half] + right_a[...].astype(F32) + left_a[...].astype(F32)
    upper = own[0, half:] + right_b[...].astype(F32) + left_b[...].astype(F32)
    came = jnp.concatenate([lower, upper], axis=0).reshape(tiles * tile_rows, width)
    mesh_in = latent_ref[...].astype(F32) + came
    normed = layer_norm(mesh_in, gain_ref[...]).astype(BF16)
    hidden = silu(jnp.dot(normed, up_ref[...], preferred_element_type=F32)).astype(BF16)
    out = (mesh_in + jnp.dot(hidden, down_ref[...], preferred_element_type=F32)).astype(BF16)
    out_ref[...] = out
    out_a[...] = out[: half * tile_rows]
    out_b[...] = out[half * tile_rows :]


def back_kernel(
    ring, places, per_step, me_ref, lists_ref, mask_ref, latent_ref, interp_ref, *rest
):
    count = len(places)
    pieces, (out_ref, held, picked, sems) = rest[:count], rest[count:]
    step = pl.program_id(0)
    me = me_ref[0]
    list_len, tile_rows, block_rows = interp_ref.shape[1:]

    @pl.when(step == 0)
    def _():
        copies = []
        for i, (place, row) in enumerate(places):
            into = held.at[place, pl.ds(row, pieces[i].shape[0])]
            copies.append(pltpu.make_async_copy(pieces[i], into, sems.at[i]))
        for copy in copies:
            copy.start()
        for copy in copies:
            copy.wait()

    for b in range(per_step):
        block = (me * pl.num_programs(0) + step) * per_step + b
        for k in range(list_len):
            ahead, across, tile = ring.entry(lists_ref, me, block, k)
            rows = pl.ds(pl.multiple_of(tile * tile_rows, tile_rows), tile_rows)
            mask = mask_ref[k, block].astype(F32)
            value = held[ahead * N_CORE + across, rows].astype(F32) * mask
            picked[b, k * tile_rows : (k + 1) * tile_rows] = value.astype(BF16)
        weights = interp_ref[b].reshape(list_len * tile_rows, block_rows)
        back = lax.dot_general(
            weights, picked[b], (((0,), (0,)), ((), ())), preferred_element_type=F32
        )
        rows = slice(b * block_rows, (b + 1) * block_rows)
        out_ref[rows] = (latent_ref[rows].astype(F32) + back).astype(BF16)


def whole(array):
    zeros = (0,) * array.ndim
    return pl.BlockSpec(array.shape, lambda *_: zeros)


def params(mib):
    return pltpu.CompilerParams(vmem_limit_bytes=mib * 1024 * 1024)


def cost(flops, *arrays):
    size = sum(a.size * a.dtype.itemsize for a in arrays)
    return pl.CostEstimate(flops=int(flops), bytes_accessed=int(size), transcendentals=0)


def shape(dims, kind=BF16):
    return jax.ShapeDtypeStruct(dims, kind)


def on_device(
    n_y,
    grid_features,
    mesh_latent,
    embed_in,
    embed_out,
    embed_gain,
    interp,
    block_mask,
    tile_list,
    mesh_up,
    mesh_down,
    mesh_gain,
):
    n_band = lax.axis_size("band")
    blk_count, list_len, tile_rows, block_rows = interp.shape
    channels, width = embed_in.shape
    node_rows = mesh_latent.shape[0]
    tiles = node_rows // tile_rows
    half_tiles, half_rows = tiles // 2, node_rows // 2
    entries = blk_count * list_len
    slots = entries // n_band
    ring = Ring(n_band, n_y, tiles)
    chips, far = ring.chips, ring.far
    lists = (lax.axis_index("band").reshape(1), tile_list.T, block_mask.T)

    gain = embed_gain.reshape(1, width)
    per_step = 2
    rows = per_step * block_rows
    held_shape = (chips * slots, tile_rows, width)
    latent, kept, sent, table = pl.pallas_call(
        functools.partial(embed_kernel, ring, per_step, slots),
        out_shape=[shape((blk_count * block_rows, width))]
        + [shape(held_shape)] * N_CORE
        + [shape((2, entries), jnp.int32)],
        grid_spec=pltpu.PrefetchScalarGridSpec(
            num_scalar_prefetch=3,
            grid=(blk_count // per_step,),
            in_specs=[
                pl.BlockSpec((channels, rows), lambda i, *_: (0, i)),
                whole(embed_in),
                whole(embed_out),
                whole(gain),
                pl.BlockSpec((per_step,) + interp.shape[1:], lambda i, *_: (i, 0, 0, 0)),
            ],
            out_specs=[pl.BlockSpec((rows, width), lambda i, *_: (i, 0))]
            + [pl.BlockSpec(held_shape, lambda i, *_: (0, 0, 0))] * N_CORE
            + [pl.BlockSpec(memory_space=pltpu.SMEM)],
            scratch_shapes=[pltpu.VMEM((entries, tile_rows, width), BF16)],
        ),
        compiler_params=params(24),
        cost_estimate=cost(
            2 * blk_count * block_rows * width * (channels + width + list_len * tile_rows),
            grid_features,
            interp,
        ),
        name="embed",
    )(*lists, grid_features.T, embed_in, embed_out, gain, interp)
    other = ring.over_core(sent)

    dense = (tiles, tile_rows, width)
    half_dense = (half_tiles, tile_rows, width)

    def entries_of(owner):
        return pl.BlockSpec((slots, tile_rows, width), lambda i, _: (owner, 0, 0))

    near = [entries_of(owner) for owner in (far, far - 1, chips - far + 1)]
    far_right, far_left, next_right, next_left = pl.pallas_call(
        functools.partial(far_kernel, ring),
        out_shape=[shape(half_dense)] * 4,
        grid_spec=pltpu.PrefetchScalarGridSpec(
            num_scalar_prefetch=1,
            grid=(1,),
            in_specs=near + near,
            out_specs=[pl.BlockSpec(half_dense, lambda i, _: (0, 0, 0))] * 4,
            scratch_shapes=[pltpu.VMEM(dense, F32)],
        ),
        compiler_params=params(8),
        cost_estimate=cost(0, kept),
        name="far_chunks",
    )(table, *[kept] * 3, *[other] * 3)

    def skip_far(i):
        return i + (i >= far).astype(jnp.int32)

    per_owner = pl.BlockSpec((slots, tile_rows, width), lambda i, _: (skip_far(i), 0, 0))
    own = pl.pallas_call(
        functools.partial(own_kernel, ring),
        out_shape=shape((chips,) + dense, F32),
        grid_spec=pltpu.PrefetchScalarGridSpec(
            num_scalar_prefetch=1,
            grid=(chips - 1,),
            in_specs=[per_owner] * 2,
            out_specs=pl.BlockSpec((1,) + dense, lambda i, _: (skip_far(i), 0, 0, 0)),
        ),
        compiler_params=params(8),
        cost_estimate=cost(0, kept, kept, kept, kept),
        name="own_chunks",
    )(table, kept, other)

    def add_own(distance, part, value):
        mine = own[distance % chips, part]
        return (mine + value.astype(F32)).astype(BF16)

    lower, upper = slice(0, half_tiles), slice(half_tiles, tiles)
    right_a, left_b = ring.over(far_right, 1), ring.over(far_left, -1)
    right_b, left_a = ring.over(next_right, 1), ring.over(next_left, -1)
    for distance in range(far - 1, 0, -1):
        right_a = ring.over(add_own(distance, lower, right_a), 1)
        left_b = ring.over(add_own(-distance, upper, left_b), -1)
        if distance > 1:
            right_b = ring.over(add_own(distance - 1, upper, right_b), 1)
            left_a = ring.over(add_own(1 - distance, lower, left_a), -1)

    mesh_gain = mesh_gain.reshape(1, width)
    came = (right_a, left_b, right_b, left_a)
    mesh_out, out_a, out_b = pl.pallas_call(
        mesh_kernel,
        out_shape=[shape((node_rows, width))] + [shape((half_rows, width))] * 2,
        grid=(1,),
        in_specs=[whole(a) for a in (mesh_latent, mesh_up, mesh_down, mesh_gain)]
        + [pl.BlockSpec((1,) + dense, lambda i: (0, 0, 0, 0))]
        + [whole(c) for c in came],
        out_specs=[pl.BlockSpec((node_rows, width), lambda i: (0, 0))]
        + [pl.BlockSpec((half_rows, width), lambda i: (0, 0))] * 2,
        compiler_params=params(16),
        cost_estimate=cost(4 * node_rows * width * width, mesh_up, mesh_down),
        name="mesh_step",
    )(mesh_latent, mesh_up, mesh_down, mesh_gain, own, *came)

    pieces, places = [], []

    def keep(piece, owner, row):
        for across, value in enumerate((piece, ring.over_core(piece))):
            pieces.append(value)
            places.append((owner % chips * N_CORE + across, row))

    right_a, left_b, right_b, left_a = out_a, out_b, out_b, out_a
    keep(mesh_out, 0, 0)
    for distance in range(1, far + 1):
        right_a, left_b = ring.over(right_a, 1), ring.over(left_b, -1)
        keep(right_a, -distance, 0)
        keep(left_b, distance, half_rows)
        if distance < far:
            right_b, left_a = ring.over(right_b, 1), ring.over(left_a, -1)
            keep(right_b, -distance, half_rows)
            keep(left_a, distance, 0)

    per_step = 2
    rows = per_step * block_rows
    grid_out = pl.pallas_call(
        functools.partial(back_kernel, ring, places, per_step),
        out_shape=shape((blk_count * block_rows, width)),
        grid_spec=pltpu.PrefetchScalarGridSpec(
            num_scalar_prefetch=3,
            grid=(blk_count // per_step,),
            in_specs=[
                pl.BlockSpec((rows, width), lambda i, *_: (i, 0)),
                pl.BlockSpec((per_step,) + interp.shape[1:], lambda i, *_: (i, 0, 0, 0)),
            ]
            + [pl.BlockSpec(memory_space=pl.ANY)] * len(pieces),
            out_specs=pl.BlockSpec((rows, width), lambda i, *_: (i, 0)),
            scratch_shapes=[
                pltpu.VMEM((n_band, node_rows, width), BF16),
                pltpu.VMEM((per_step, list_len * tile_rows, width), BF16),
                pltpu.SemaphoreType.DMA((len(pieces),)),
            ],
        ),
        compiler_params=params(16 if n_band <= 16 else 32),
        cost_estimate=cost(
            2 * blk_count * block_rows * width * list_len * tile_rows, latent, latent, interp
        ),
        name="back",
    )(*lists, latent, interp, *pieces)
    return (grid_out, mesh_out)


def solution(mesh):
    placed = (
        P(("groups", "band"), None),
        P(("groups", "band"), None),
        P(),
        P(),
        P(),
        P("band", None, None, None),
        P(),
        P(),
        P(),
        P(),
        P(),
    )
    n_y = max(1, 4 // mesh.shape["groups"])
    return jax.shard_map(
        functools.partial(on_device, n_y),
        mesh=mesh,
        in_specs=placed,
        out_specs=(P(("groups", "band"), None), P(("groups", "band"), None)),
        check_vma=False,
    )
```

```python
import functools

import jax
import jax.numpy as jnp
from jax import lax
from jax.experimental import pallas as pl
from jax.experimental.pallas import tpu as pltpu
from jax.sharding import PartitionSpec as P

F32 = jnp.float32
BF16 = jnp.bfloat16
N_CORE = 2


def silu(values):
    half = 0.5 * values
    return half * (1.0 + jnp.tanh(half))


def layer_norm(values, gain):
    centred = values - jnp.mean(values, axis=-1, keepdims=True)
    spread = jnp.mean(centred * centred, axis=-1, keepdims=True)
    return centred * lax.rsqrt(spread + 1e-05) * gain


def split(value, size):
    if size & (size - 1) == 0:
        return lax.shift_right_logical(value, size.bit_length() - 1), value & (size - 1)
    return lax.div(value, size), lax.rem(value, size)


class Ring:
    def __init__(self, n_band, n_y, tiles):
        self.n_band, self.n_y, self.tiles = n_band, n_y, tiles
        self.chips = n_band // N_CORE
        self.far = self.chips // 2

    def place(self, index):
        chip, core = split(index, N_CORE)
        z, y = split(chip, self.n_y)
        return z + y * (self.chips - 1 - 2 * z), core

    def index(self, ring, core):
        ring = ring % self.chips
        n_z = self.chips // self.n_y
        z, y = (ring, 0) if ring < n_z else (self.chips - 1 - ring, 1)
        return (z * self.n_y + y) * N_CORE + core

    def over_core(self, value):
        return lax.ppermute(value, "band", [(i, i ^ 1) for i in range(self.n_band)])

    def over(self, value, by):
        pairs = []
        for i in range(self.n_band):
            chip, core = divmod(i, N_CORE)
            z, y = divmod(chip, self.n_y)
            ring = z if y == 0 else self.chips - 1 - z
            pairs.append((i, self.index(ring + by, core)))
        return lax.ppermute(value, "band", pairs)

    def entry(self, lists_ref, me, block, k):
        owner, tile = split(lists_ref[k, block], self.tiles)
        ring, core = self.place(owner)
        my_ring, my_core = self.place(me)
        ahead = split(ring - my_ring + self.chips, self.chips)[1]
        return ahead, core ^ my_core, tile


def embed_kernel(
    ring, per_step, slots, me_ref, lists_ref, mask_ref,
    x_ref, w1_ref, w2_ref, gain_ref, interp_ref,
    latent_ref, kept_ref, sent_ref, table_ref, placed,
):
    step = pl.program_id(0)
    me = me_ref[0]
    list_len, tile_rows, block_rows = interp_ref.shape[1:]
    blk_count = pl.num_programs(0) * per_step

    def spot(index, b, k):
        block = step * per_step + b
        ahead, across, tile = ring.entry(lists_ref, index, index * blk_count + block, k)
        slot = split(block * list_len + k, ring.n_band)[0]
        return (across * ring.chips + ahead) * slots + slot, tile

    first = lax.dot_general(
        x_ref[...], w1_ref[...], (((0,), (0,)), ((), ())), preferred_element_type=F32
    )
    before = jnp.dot(silu(first).astype(BF16), w2_ref[...], preferred_element_type=F32)
    latent = layer_norm(before, gain_ref[...]).astype(BF16)
    latent_ref[...] = latent
    for b in range(per_step):
        weights = interp_ref[b].reshape(list_len * tile_rows, block_rows)
        part = jnp.dot(
            weights, latent[b * block_rows : (b + 1) * block_rows], preferred_element_type=F32
        )
        for k in range(list_len):
            place, tile = spot(me, b, k)
            there, its_tile = spot(me ^ 1, b, k)
            block = step * per_step + b
            mask = mask_ref[k, me * blk_count + block]
            table_ref[0, place] = tile
            table_ref[1, there] = its_tile
            table_ref[2, place] = mask
            table_ref[3, there] = mask_ref[k, (me ^ 1) * blk_count + block]
            masked = part[k * tile_rows : (k + 1) * tile_rows] * mask.astype(F32)
            placed[place] = masked.astype(BF16)

    @pl.when(step == pl.num_programs(0) - 1)
    def _():
        count = kept_ref.shape[0]
        kept_ref[...] = placed[:count]
        sent_ref[...] = placed[count:]


def add_entries(total, table_ref, owner, kept, other, chips):
    slots = kept.shape[0]
    for slot in range(slots):
        total[table_ref[0, owner * slots + slot]] += kept[slot].astype(F32)
        total[table_ref[1, (chips + owner) * slots + slot]] += other[slot].astype(F32)


def far_kernel(ring, table_ref, *refs):
    kept, other = refs[0:3], refs[3:6]
    far_right, far_left, next_right, next_left, total = refs[6:]
    half = total.shape[0] // 2
    owners = (ring.far, ring.far - 1, ring.chips - ring.far + 1)
    for number, owner in enumerate(owners):
        total[...] = jnp.zeros_like(total)
        add_entries(total, table_ref, owner, kept[number], other[number], ring.chips)
        if number == 0:
            far_right[...] = total[:half].astype(BF16)
            far_left[...] = total[half:].astype(BF16)
        elif number == 1:
            next_right[...] = total[half:].astype(BF16)
        else:
            next_left[...] = total[:half].astype(BF16)


def own_kernel(ring, table_ref, kept, other, own):
    number = pl.program_id(0)
    owner = number + (number >= ring.far).astype(jnp.int32)
    own[...] = jnp.zeros_like(own)
    add_entries(own.at[0], table_ref, owner, kept, other, ring.chips)


def mesh_kernel(
    latent_ref, up_ref, down_ref, gain_ref, own, right_a, left_b, right_b, left_a,
    out_ref, out_a, out_b,
):
    tiles, tile_rows, width = own.shape[1:]
    half = tiles // 2
    lower = own[0, :half] + right_a[...].astype(F32) + left_a[...].astype(F32)
    upper = own[0, half:] + right_b[...].astype(F32) + left_b[...].astype(F32)
    came = jnp.concatenate([lower, upper], axis=0).reshape(tiles * tile_rows, width)
    mesh_in = latent_ref[...].astype(F32) + came
    normed = layer_norm(mesh_in, gain_ref[...]).astype(BF16)
    hidden = silu(jnp.dot(normed, up_ref[...], preferred_element_type=F32)).astype(BF16)
    out = (mesh_in + jnp.dot(hidden, down_ref[...], preferred_element_type=F32)).astype(BF16)
    out_ref[...] = out
    out_a[...] = out[: half * tile_rows]
    out_b[...] = out[half * tile_rows :]


def add_kernel(own_right, own_left, right, left, token, out_right, out_left):
    del token
    out_right[...] = (own_right[0] + right[...].astype(F32)).astype(BF16)
    out_left[...] = (own_left[0] + left[...].astype(F32)).astype(BF16)


def order_kernel(*refs):
    del refs


def pick_kernel(owners, slots, chips, table_ref, *refs):
    halves, (mine, theirs) = refs[:-2], refs[-2:]
    tile_rows = mine.shape[1]
    count = halves[0].shape[0] // tile_rows
    for number, owner in enumerate(owners):
        lower, upper = halves[2 * number : 2 * number + 2]
        for slot in range(slots):
            for way, out in enumerate((mine, theirs)):
                place = (way * chips + owner) * slots + slot
                tile, mask = table_ref[way, place], table_ref[2 + way, place]
                above = tile >= count
                within = jnp.where(above, tile - count, tile)
                rows = pl.ds(pl.multiple_of(within * tile_rows, tile_rows), tile_rows)
                value = jnp.where(above, upper[rows], lower[rows]).astype(F32)
                out[number * slots + slot] = (value * mask.astype(F32)).astype(BF16)


def back_kernel(ring, places, slots, per_step, me_ref, lists_ref, latent_ref, weights_ref, *rest):
    count = len(places)
    pieces, (out_ref, held, sems) = rest[:count], rest[count:]
    step = pl.program_id(0)
    me = me_ref[0]
    block_rows, listed = weights_ref.shape[1:]
    list_len = lists_ref.shape[0]
    tile_rows, width = held.shape[1:]

    @pl.when(step == 0)
    def _():
        copies = []
        for i, (piece, place) in enumerate(zip(pieces, places)):
            for number, start in enumerate(place):
                copies.append(
                    pltpu.make_async_copy(
                        piece.at[pl.ds(number * slots, slots)],
                        held.at[pl.ds(start * slots, slots)],
                        sems.at[len(copies)],
                    )
                )
        for copy in copies:
            copy.start()
        for copy in copies:
            copy.wait()

    for b in range(per_step):
        number = step * per_step + b
        values = []
        for k in range(list_len):
            ahead, across, _ = ring.entry(
                lists_ref, me, me * pl.num_programs(0) * per_step + number, k
            )
            slot = split(number * list_len + k, ring.n_band)[0]
            values.append(held[(across * ring.chips + ahead) * slots + slot])
        value = jnp.concatenate(values, axis=0)
        back = jnp.dot(weights_ref[b], value, preferred_element_type=F32)
        rows = slice(b * block_rows, (b + 1) * block_rows)
        out_ref[rows] = (latent_ref[rows].astype(F32) + back).astype(BF16)


def whole(array):
    zeros = (0,) * array.ndim
    return pl.BlockSpec(array.shape, lambda *_: zeros)


def params(mib):
    return pltpu.CompilerParams(vmem_limit_bytes=mib * 1024 * 1024)


def cost(flops, *arrays):
    size = sum(a.size * a.dtype.itemsize for a in arrays)
    return pl.CostEstimate(flops=int(flops), bytes_accessed=int(size), transcendentals=0)


def shape(dims, kind=BF16):
    return jax.ShapeDtypeStruct(dims, kind)


def on_device(
    n_y,
    grid_features,
    mesh_latent,
    embed_in,
    embed_out,
    embed_gain,
    interp,
    block_mask,
    tile_list,
    mesh_up,
    mesh_down,
    mesh_gain,
):
    n_band = lax.axis_size("band")
    blk_count, list_len, tile_rows, block_rows = interp.shape
    channels, width = embed_in.shape
    node_rows = mesh_latent.shape[0]
    tiles = node_rows // tile_rows
    half_tiles, half_rows = tiles // 2, node_rows // 2
    entries = blk_count * list_len
    slots = entries // n_band
    ring = Ring(n_band, n_y, tiles)
    chips, far = ring.chips, ring.far
    lists = (lax.axis_index("band").reshape(1), tile_list.T, block_mask.T)

    def in_hbm(array):
        return pltpu.with_memory_space_constraint(array, pltpu.HBM)

    gain = embed_gain.reshape(1, width)
    per_step = 2
    rows = per_step * block_rows
    held_shape = (chips * slots, tile_rows, width)
    latent, kept, sent, table = pl.pallas_call(
        functools.partial(embed_kernel, ring, per_step, slots),
        out_shape=[shape((blk_count * block_rows, width))]
        + [shape(held_shape)] * N_CORE
        + [shape((4, entries), jnp.int32)],
        grid_spec=pltpu.PrefetchScalarGridSpec(
            num_scalar_prefetch=3,
            grid=(blk_count // per_step,),
            in_specs=[
                pl.BlockSpec((channels, rows), lambda i, *_: (0, i)),
                whole(embed_in),
                whole(embed_out),
                whole(gain),
                pl.BlockSpec((per_step,) + interp.shape[1:], lambda i, *_: (i, 0, 0, 0)),
            ],
            out_specs=[pl.BlockSpec((rows, width), lambda i, *_: (i, 0))]
            + [pl.BlockSpec(held_shape, lambda i, *_: (0, 0, 0))] * N_CORE
            + [pl.BlockSpec(memory_space=pltpu.SMEM)],
            scratch_shapes=[pltpu.VMEM((entries, tile_rows, width), BF16)],
        ),
        compiler_params=params(24),
        cost_estimate=cost(
            2 * blk_count * block_rows * width * (channels + width + list_len * tile_rows),
            grid_features,
            interp,
        ),
        name="embed",
    )(*lists, *map(in_hbm, (grid_features.T, embed_in, embed_out, gain, interp)))
    other = ring.over_core(sent)

    dense = (tiles, tile_rows, width)
    half_dense = (half_tiles, tile_rows, width)

    def entries_of(owner):
        return pl.BlockSpec((slots, tile_rows, width), lambda i, _: (owner, 0, 0))

    near = [entries_of(owner) for owner in (far, far - 1, chips - far + 1)]
    far_right, far_left, next_right, next_left = pl.pallas_call(
        functools.partial(far_kernel, ring),
        out_shape=[shape(half_dense)] * 4,
        grid_spec=pltpu.PrefetchScalarGridSpec(
            num_scalar_prefetch=1,
            grid=(1,),
            in_specs=near + near,
            out_specs=[pl.BlockSpec(half_dense, lambda i, _: (0, 0, 0))] * 4,
            scratch_shapes=[pltpu.VMEM(dense, F32)],
        ),
        compiler_params=params(8),
        cost_estimate=cost(0, kept),
        name="far_chunks",
    )(table, *[kept] * 3, *[other] * 3)

    def skip_far(i):
        return i + (i >= far).astype(jnp.int32)

    per_owner = pl.BlockSpec((slots, tile_rows, width), lambda i, _: (skip_far(i), 0, 0))
    own = pl.pallas_call(
        functools.partial(own_kernel, ring),
        out_shape=shape((chips,) + dense, F32),
        grid_spec=pltpu.PrefetchScalarGridSpec(
            num_scalar_prefetch=1,
            grid=(chips - 1,),
            in_specs=[per_owner] * 2,
            out_specs=pl.BlockSpec((1,) + dense, lambda i, _: (skip_far(i), 0, 0, 0)),
        ),
        compiler_params=params(8),
        cost_estimate=cost(0, kept, kept, kept, kept),
        name="own_chunks",
    )(table, kept, other)

    lower, upper = 0, 1

    def half_of(owner, part):
        return pl.BlockSpec((1,) + half_dense, lambda i: (owner % chips, part, 0, 0))

    def add_own(distance, parts, values, token):
        sums = pl.pallas_call(
            add_kernel,
            out_shape=[shape(half_dense)] * 2,
            grid=(1,),
            in_specs=[half_of(distance, parts[0]), half_of(-distance, parts[1])]
            + [whole(v) for v in values]
            + [pl.BlockSpec(memory_space=pl.ANY)],
            out_specs=[pl.BlockSpec(half_dense, lambda i: (0, 0, 0))] * 2,
            compiler_params=params(8),
            cost_estimate=cost(0, *values, *values),
            name=f"add_{distance}{'ab'[parts[0]]}",
        )(own, own, *values, token)
        return sums, sums[0]

    def both(values):
        return [ring.over(values[0], 1), ring.over(values[1], -1)]

    first, second = both((far_right, far_left)), both((next_right, next_left))
    token = own
    for distance in range(far - 1, 0, -1):
        sums, token = add_own(distance, (lower, upper), first, token)
        first = both(sums)
        if distance > 1:
            sums, token = add_own(distance - 1, (upper, lower), second, token)
            second = both(sums)

    mesh_gain = mesh_gain.reshape(1, width)
    came = (*first, *second)
    mesh_out, out_a, out_b = pl.pallas_call(
        mesh_kernel,
        out_shape=[shape((node_rows, width))] + [shape((half_rows, width))] * 2,
        grid=(1,),
        in_specs=[whole(a) for a in (mesh_latent, mesh_up, mesh_down, mesh_gain)]
        + [pl.BlockSpec((1,) + dense, lambda i: (0, 0, 0, 0))]
        + [whole(c) for c in came],
        out_specs=[pl.BlockSpec((node_rows, width), lambda i: (0, 0))]
        + [pl.BlockSpec((half_rows, width), lambda i: (0, 0))] * 2,
        compiler_params=params(16),
        cost_estimate=cost(4 * node_rows * width * width, mesh_up, mesh_down),
        name="mesh_step",
    )(mesh_latent, mesh_up, mesh_down, mesh_gain, own, *came)

    def in_order(values, token):
        return pl.pallas_call(
            order_kernel,
            out_shape=[shape(v.shape) for v in values],
            in_specs=[pl.BlockSpec(memory_space=pl.ANY)] * (len(values) + 1),
            out_specs=[pl.BlockSpec(memory_space=pl.ANY)] * len(values),
            input_output_aliases={i: i for i in range(len(values))},
            cost_estimate=cost(0),
            name="in_order",
        )(*values, token)

    pieces, places = [], []

    def pick(owners, halves):
        owners = [owner % chips for owner in owners]
        out = shape((len(owners) * slots, tile_rows, width))
        mine, theirs = pl.pallas_call(
            functools.partial(pick_kernel, owners, slots, chips),
            out_shape=[out] * 2,
            grid_spec=pltpu.PrefetchScalarGridSpec(
                num_scalar_prefetch=1,
                grid=(1,),
                in_specs=[whole(h) for h in halves],
                out_specs=[whole(out)] * 2,
            ),
            compiler_params=params(8),
            cost_estimate=cost(0, *halves),
            name=f"pick_{owners[0]}",
        )(table, *halves)
        for across, value in enumerate((mine, ring.over_core(theirs))):
            pieces.append(value)
            places.append([across * chips + owner for owner in owners])
        return mine

    first, second = both((out_a, out_b)), both((out_b, out_a))
    token = pick([0], (out_a, out_b))
    for distance in range(1, far):
        first = in_order(first, token)
        onward = both(first)
        second = in_order(second, first[0])
        if distance < far - 1:
            after = both(second)
        token = pick([-distance, distance], (first[0], second[0], second[1], first[1]))
        first, second = onward, after
    pick([far], first)

    weights = jnp.swapaxes(interp.reshape(blk_count, list_len * tile_rows, block_rows), 1, 2)
    per_step = 4
    rows = per_step * block_rows
    grid_out = pl.pallas_call(
        functools.partial(back_kernel, ring, places, slots, per_step),
        out_shape=shape((blk_count * block_rows, width)),
        grid_spec=pltpu.PrefetchScalarGridSpec(
            num_scalar_prefetch=2,
            grid=(blk_count // per_step,),
            in_specs=[
                pl.BlockSpec((rows, width), lambda i, *_: (i, 0)),
                pl.BlockSpec((per_step,) + weights.shape[1:], lambda i, *_: (i, 0, 0)),
            ]
            + [pl.BlockSpec(memory_space=pl.ANY)] * len(pieces),
            out_specs=pl.BlockSpec((rows, width), lambda i, *_: (i, 0)),
            scratch_shapes=[
                pltpu.VMEM((entries, tile_rows, width), BF16),
                pltpu.SemaphoreType.DMA((n_band,)),
            ],
        ),
        compiler_params=params(20),
        cost_estimate=cost(
            2 * blk_count * block_rows * width * list_len * tile_rows, latent, latent, interp
        ),
        name="back",
    )(*lists[:2], latent, weights, *pieces)
    return (grid_out, mesh_out)


def solution(mesh):
    placed = (
        P(("groups", "band"), None),
        P(("groups", "band"), None),
        P(),
        P(),
        P(),
        P("band", None, None, None),
        P(),
        P(),
        P(),
        P(),
        P(),
    )
    n_y = max(1, 4 // mesh.shape["groups"])
    return jax.shard_map(
        functools.partial(on_device, n_y),
        mesh=mesh,
        in_specs=placed,
        out_specs=(P(("groups", "band"), None), P(("groups", "band"), None)),
        check_vma=False,
    )
```

```python
import functools

import jax
import jax.numpy as jnp
from jax import lax
from jax.experimental import pallas as pl
from jax.experimental.pallas import tpu as pltpu
from jax.sharding import PartitionSpec as P

F32 = jnp.float32
BF16 = jnp.bfloat16
N_CORE = 2


def silu(values):
    half = 0.5 * values
    return half * (1.0 + jnp.tanh(half))


def layer_norm(values, gain):
    centred = values - jnp.mean(values, axis=-1, keepdims=True)
    spread = jnp.mean(centred * centred, axis=-1, keepdims=True)
    return centred * lax.rsqrt(spread + 1e-05) * gain


def split(value, size):
    if size & (size - 1) == 0:
        return lax.shift_right_logical(value, size.bit_length() - 1), value & (size - 1)
    return lax.div(value, size), lax.rem(value, size)


class Ring:
    def __init__(self, n_band, n_y, tiles):
        self.n_band, self.n_y, self.tiles = n_band, n_y, tiles
        self.chips = n_band // N_CORE
        self.far = self.chips // 2

    def place(self, index):
        chip, core = split(index, N_CORE)
        z, y = split(chip, self.n_y)
        return z + y * (self.chips - 1 - 2 * z), core

    def index(self, ring, core):
        ring = ring % self.chips
        n_z = self.chips // self.n_y
        z, y = (ring, 0) if ring < n_z else (self.chips - 1 - ring, 1)
        return (z * self.n_y + y) * N_CORE + core

    def over_core(self, value):
        return lax.ppermute(value, "band", [(i, i ^ 1) for i in range(self.n_band)])

    def over(self, value, by):
        pairs = []
        for i in range(self.n_band):
            chip, core = divmod(i, N_CORE)
            z, y = divmod(chip, self.n_y)
            ring = z if y == 0 else self.chips - 1 - z
            pairs.append((i, self.index(ring + by, core)))
        return lax.ppermute(value, "band", pairs)

    def entry(self, lists_ref, me, block, k):
        owner, tile = split(lists_ref[k, block], self.tiles)
        ring, core = self.place(owner)
        my_ring, my_core = self.place(me)
        ahead = split(ring - my_ring + self.chips, self.chips)[1]
        return ahead, core ^ my_core, tile


def embed_kernel(
    ring, per_step, slots, me_ref, lists_ref, mask_ref,
    x_ref, w1_ref, w2_ref, gain_ref, interp_ref,
    latent_ref, kept_ref, sent_ref, table_ref,
):
    step = pl.program_id(0)
    me = me_ref[0]
    list_len, tile_rows, block_rows = interp_ref.shape[1:]
    blk_count = pl.num_programs(0) * per_step

    def spot(index, b, k):
        block = step * per_step + b
        ahead, across, tile = ring.entry(lists_ref, index, index * blk_count + block, k)
        slot = split(block * list_len + k, ring.n_band)[0]
        return (across * ring.chips + ahead) * slots + slot, tile

    spare = kept_ref.shape[0] - 1
    for b in range(per_step):
        block = step * per_step + b
        rows = slice(b * block_rows, (b + 1) * block_rows)
        first = lax.dot_general(
            x_ref[:, rows], w1_ref[...], (((0,), (0,)), ((), ())), preferred_element_type=F32
        )
        before = jnp.dot(silu(first).astype(BF16), w2_ref[...], preferred_element_type=F32)
        latent = layer_norm(before, gain_ref[...]).astype(BF16)
        start = pl.multiple_of(block * block_rows, block_rows)
        latent_ref[pl.ds(start, block_rows)] = latent
        weights = interp_ref[b].reshape(list_len * tile_rows, block_rows)
        part = jnp.dot(weights, latent, preferred_element_type=F32)
        for k in range(list_len):
            place, tile = spot(me, b, k)
            there, its_tile = spot(me ^ 1, b, k)
            mask = mask_ref[k, me * blk_count + block]
            table_ref[0, place] = tile
            table_ref[1, there] = its_tile
            table_ref[2, place] = mask
            table_ref[3, there] = mask_ref[k, (me ^ 1) * blk_count + block]
            masked = part[k * tile_rows : (k + 1) * tile_rows] * mask.astype(F32)
            masked = masked.astype(BF16)
            kept_ref[jnp.minimum(place, spare)] = masked
            sent_ref[jnp.where(place >= spare, place - spare, spare)] = masked


def add_entries(total, table_ref, owner, kept, other, chips):
    slots = kept.shape[0]
    for slot in range(slots):
        total[table_ref[0, owner * slots + slot]] += kept[slot].astype(F32)
        total[table_ref[1, (chips + owner) * slots + slot]] += other[slot].astype(F32)


def far_kernel(ring, table_ref, *refs):
    kept, other = refs[0:3], refs[3:6]
    far_right, far_left, next_right, next_left, total = refs[6:]
    half = total.shape[0] // 2
    owners = (ring.far, ring.far - 1, ring.chips - ring.far + 1)
    for number, owner in enumerate(owners):
        total[...] = jnp.zeros_like(total)
        add_entries(total, table_ref, owner, kept[number], other[number], ring.chips)
        if number == 0:
            far_right[...] = total[:half].astype(BF16)
            far_left[...] = total[half:].astype(BF16)
        elif number == 1:
            next_right[...] = total[half:].astype(BF16)
        else:
            next_left[...] = total[:half].astype(BF16)


def own_kernel(ring, table_ref, kept, other, own):
    number = pl.program_id(0)
    owner = number + (number >= ring.far).astype(jnp.int32)
    own[...] = jnp.zeros_like(own)
    add_entries(own.at[0], table_ref, owner, kept, other, ring.chips)


def mesh_kernel(
    latent_ref, up_ref, down_ref, gain_ref, own, right_a, left_b, right_b, left_a,
    out_ref, out_a, out_b,
):
    tiles, tile_rows, width = own.shape[1:]
    half = tiles // 2
    lower = own[0, :half] + right_a[...].astype(F32) + left_a[...].astype(F32)
    upper = own[0, half:] + right_b[...].astype(F32) + left_b[...].astype(F32)
    came = jnp.concatenate([lower, upper], axis=0).reshape(tiles * tile_rows, width)
    mesh_in = latent_ref[...].astype(F32) + came
    normed = layer_norm(mesh_in, gain_ref[...]).astype(BF16)
    hidden = silu(jnp.dot(normed, up_ref[...], preferred_element_type=F32)).astype(BF16)
    out = (mesh_in + jnp.dot(hidden, down_ref[...], preferred_element_type=F32)).astype(BF16)
    out_ref[...] = out
    out_a[...] = out[: half * tile_rows]
    out_b[...] = out[half * tile_rows :]


def add_kernel(own_right, own_left, right, left, token, out_right, out_left):
    del token
    out_right[...] = (own_right[0] + right[...].astype(F32)).astype(BF16)
    out_left[...] = (own_left[0] + left[...].astype(F32)).astype(BF16)


def order_kernel(*refs):
    del refs


def pick_kernel(owners, slots, chips, table_ref, *refs):
    halves, (mine, theirs) = refs[:-2], refs[-2:]
    tile_rows = mine.shape[1]
    count = halves[0].shape[0] // tile_rows
    for number, owner in enumerate(owners):
        lower, upper = halves[2 * number : 2 * number + 2]
        for slot in range(slots):
            for way, out in enumerate((mine, theirs)):
                place = (way * chips + owner) * slots + slot
                tile, mask = table_ref[way, place], table_ref[2 + way, place]
                above = tile >= count
                within = jnp.where(above, tile - count, tile)
                rows = pl.ds(pl.multiple_of(within * tile_rows, tile_rows), tile_rows)
                value = jnp.where(above, upper[rows], lower[rows]).astype(F32)
                out[number * slots + slot] = (value * mask.astype(F32)).astype(BF16)


def back_kernel(ring, places, slots, per_step, me_ref, lists_ref, latent_ref, weights_ref, *rest):
    count = len(places)
    pieces, (out_ref, held, sems) = rest[:count], rest[count:]
    step = pl.program_id(0)
    me = me_ref[0]
    block_rows = weights_ref.shape[1]
    list_len = lists_ref.shape[0]
    tile_rows, width = held.shape[1:]

    @pl.when(step == 0)
    def _():
        copies = []
        for i, (piece, place) in enumerate(zip(pieces, places)):
            for number, start in enumerate(place):
                copies.append(
                    pltpu.make_async_copy(
                        piece.at[pl.ds(number * slots, slots)],
                        held.at[pl.ds(start * slots, slots)],
                        sems.at[len(copies)],
                    )
                )
        for copy in copies:
            copy.start()
        for copy in copies:
            copy.wait()

    for b in range(per_step):
        number = step * per_step + b
        values = []
        for k in range(list_len):
            ahead, across, _ = ring.entry(
                lists_ref, me, me * pl.num_programs(0) * per_step + number, k
            )
            slot = split(number * list_len + k, ring.n_band)[0]
            values.append(held[(across * ring.chips + ahead) * slots + slot])
        value = jnp.concatenate(values, axis=0)
        back = jnp.dot(weights_ref[number], value, preferred_element_type=F32)
        start = pl.multiple_of(number * block_rows, block_rows)
        total = latent_ref[pl.ds(start, block_rows)].astype(F32) + back
        out_ref[b * block_rows : (b + 1) * block_rows] = total.astype(BF16)


def whole(array):
    zeros = (0,) * array.ndim
    return pl.BlockSpec(array.shape, lambda *_: zeros)


def params(mib):
    return pltpu.CompilerParams(vmem_limit_bytes=mib * 1024 * 1024)


def cost(flops, *arrays):
    size = sum(a.size * a.dtype.itemsize for a in arrays)
    return pl.CostEstimate(flops=int(flops), bytes_accessed=int(size), transcendentals=0)


def shape(dims, kind=BF16):
    return jax.ShapeDtypeStruct(dims, kind)


def on_device(
    n_y,
    grid_features,
    mesh_latent,
    embed_in,
    embed_out,
    embed_gain,
    interp,
    block_mask,
    tile_list,
    mesh_up,
    mesh_down,
    mesh_gain,
):
    n_band = lax.axis_size("band")
    blk_count, list_len, tile_rows, block_rows = interp.shape
    channels, width = embed_in.shape
    node_rows = mesh_latent.shape[0]
    tiles = node_rows // tile_rows
    half_tiles, half_rows = tiles // 2, node_rows // 2
    entries = blk_count * list_len
    slots = entries // n_band
    ring = Ring(n_band, n_y, tiles)
    chips, far = ring.chips, ring.far
    lists = (lax.axis_index("band").reshape(1), tile_list.T, block_mask.T)

    def in_hbm(array):
        return pltpu.with_memory_space_constraint(array, pltpu.HBM)

    gain = embed_gain.reshape(1, width)
    per_step = 4
    rows = per_step * block_rows
    held_shape = (chips * slots + 1, tile_rows, width)
    latent, kept, sent, table = pl.pallas_call(
        functools.partial(embed_kernel, ring, per_step, slots),
        out_shape=[shape((blk_count * block_rows, width))]
        + [shape(held_shape)] * N_CORE
        + [shape((4, entries), jnp.int32)],
        grid_spec=pltpu.PrefetchScalarGridSpec(
            num_scalar_prefetch=3,
            grid=(blk_count // per_step,),
            in_specs=[
                pl.BlockSpec((channels, rows), lambda i, *_: (0, i)),
                whole(embed_in),
                whole(embed_out),
                whole(gain),
                pl.BlockSpec((per_step,) + interp.shape[1:], lambda i, *_: (i, 0, 0, 0)),
            ],
            out_specs=[pl.BlockSpec(memory_space=pltpu.VMEM)] * (1 + N_CORE)
            + [pl.BlockSpec(memory_space=pltpu.SMEM)],
        ),
        compiler_params=params(24),
        cost_estimate=cost(
            2 * blk_count * block_rows * width * (channels + width + list_len * tile_rows),
            grid_features,
            interp,
        ),
        name="embed",
    )(*lists, *map(in_hbm, (grid_features.T, embed_in, embed_out, gain, interp)))
    other = ring.over_core(sent)

    dense = (tiles, tile_rows, width)
    half_dense = (half_tiles, tile_rows, width)

    def entries_of(owner):
        return pl.BlockSpec((slots, tile_rows, width), lambda i, _: (owner, 0, 0))

    near = [entries_of(owner) for owner in (far, far - 1, chips - far + 1)]
    far_right, far_left, next_right, next_left = pl.pallas_call(
        functools.partial(far_kernel, ring),
        out_shape=[shape(half_dense)] * 4,
        grid_spec=pltpu.PrefetchScalarGridSpec(
            num_scalar_prefetch=1,
            grid=(1,),
            in_specs=near + near,
            out_specs=[pl.BlockSpec(half_dense, lambda i, _: (0, 0, 0))] * 4,
            scratch_shapes=[pltpu.VMEM(dense, F32)],
        ),
        compiler_params=params(8),
        cost_estimate=cost(0, kept),
        name="far_chunks",
    )(table, *[kept] * 3, *[other] * 3)

    def skip_far(i):
        return i + (i >= far).astype(jnp.int32)

    per_owner = pl.BlockSpec((slots, tile_rows, width), lambda i, _: (skip_far(i), 0, 0))
    own = pl.pallas_call(
        functools.partial(own_kernel, ring),
        out_shape=shape((chips,) + dense, F32),
        grid_spec=pltpu.PrefetchScalarGridSpec(
            num_scalar_prefetch=1,
            grid=(chips - 1,),
            in_specs=[per_owner] * 2,
            out_specs=pl.BlockSpec((1,) + dense, lambda i, _: (skip_far(i), 0, 0, 0)),
        ),
        compiler_params=params(8),
        cost_estimate=cost(0, kept, kept, kept, kept),
        name="own_chunks",
    )(table, kept, other)

    lower, upper = 0, 1

    def half_of(owner, part):
        return pl.BlockSpec((1,) + half_dense, lambda i: (owner % chips, part, 0, 0))

    def add_own(distance, parts, values, token):
        sums = pl.pallas_call(
            add_kernel,
            out_shape=[shape(half_dense)] * 2,
            grid=(1,),
            in_specs=[half_of(distance, parts[0]), half_of(-distance, parts[1])]
            + [whole(v) for v in values]
            + [pl.BlockSpec(memory_space=pl.ANY)],
            out_specs=[pl.BlockSpec(half_dense, lambda i: (0, 0, 0))] * 2,
            compiler_params=params(8),
            cost_estimate=cost(0, *values, *values),
            name=f"add_{distance}{'ab'[parts[0]]}",
        )(own, own, *values, token)
        return sums, sums[0]

    def both(values):
        return [ring.over(values[0], 1), ring.over(values[1], -1)]

    first, second = both((far_right, far_left)), both((next_right, next_left))
    token = own
    for distance in range(far - 1, 0, -1):
        sums, token = add_own(distance, (lower, upper), first, token)
        first = both(sums)
        if distance > 1:
            sums, token = add_own(distance - 1, (upper, lower), second, token)
            second = both(sums)

    mesh_gain = mesh_gain.reshape(1, width)
    came = (*first, *second)
    mesh_out, out_a, out_b = pl.pallas_call(
        mesh_kernel,
        out_shape=[shape((node_rows, width))] + [shape((half_rows, width))] * 2,
        grid=(1,),
        in_specs=[whole(a) for a in (mesh_latent, mesh_up, mesh_down, mesh_gain)]
        + [pl.BlockSpec((1,) + dense, lambda i: (0, 0, 0, 0))]
        + [whole(c) for c in came],
        out_specs=[pl.BlockSpec((node_rows, width), lambda i: (0, 0))]
        + [pl.BlockSpec((half_rows, width), lambda i: (0, 0))] * 2,
        compiler_params=params(16),
        cost_estimate=cost(4 * node_rows * width * width, mesh_up, mesh_down),
        name="mesh_step",
    )(mesh_latent, mesh_up, mesh_down, mesh_gain, own, *came)

    def in_order(values, token):
        return pl.pallas_call(
            order_kernel,
            out_shape=[shape(v.shape) for v in values],
            in_specs=[pl.BlockSpec(memory_space=pl.ANY)] * (len(values) + 1),
            out_specs=[pl.BlockSpec(memory_space=pl.ANY)] * len(values),
            input_output_aliases={i: i for i in range(len(values))},
            compiler_params=params(1),
            cost_estimate=cost(0),
            name="in_order",
        )(*values, token)

    pieces, places = [], []

    def pick(owners, halves):
        owners = [owner % chips for owner in owners]
        out = shape((len(owners) * slots, tile_rows, width))
        mine, theirs = pl.pallas_call(
            functools.partial(pick_kernel, owners, slots, chips),
            out_shape=[out] * 2,
            grid_spec=pltpu.PrefetchScalarGridSpec(
                num_scalar_prefetch=1,
                grid=(1,),
                in_specs=[whole(h) for h in halves],
                out_specs=[whole(out)] * 2,
            ),
            compiler_params=params(8),
            cost_estimate=cost(0, *halves),
            name=f"pick_{owners[0]}",
        )(table, *halves)
        for across, value in enumerate((mine, ring.over_core(theirs))):
            pieces.append(value)
            places.append([across * chips + owner for owner in owners])
        return mine

    first, second = both((out_a, out_b)), both((out_b, out_a))
    token = pick([0], (out_a, out_b))
    for distance in range(1, far):
        first = in_order(first, token)
        onward = both(first)
        second = in_order(second, first[0])
        if distance < far - 1:
            after = both(second)
        token = pick([-distance, distance], (first[0], second[0], second[1], first[1]))
        first, second = onward, after
    pick([far], first)

    weights = jnp.swapaxes(interp.reshape(blk_count, list_len * tile_rows, block_rows), 1, 2)
    per_step = 4
    rows = per_step * block_rows
    grid_out = pl.pallas_call(
        functools.partial(back_kernel, ring, places, slots, per_step),
        out_shape=shape((blk_count * block_rows, width)),
        grid_spec=pltpu.PrefetchScalarGridSpec(
            num_scalar_prefetch=2,
            grid=(blk_count // per_step,),
            in_specs=[pl.BlockSpec(memory_space=pltpu.VMEM)] * 2
            + [pl.BlockSpec(memory_space=pl.ANY)] * len(pieces),
            out_specs=pl.BlockSpec((rows, width), lambda i, *_: (i, 0)),
            scratch_shapes=[
                pltpu.VMEM((entries, tile_rows, width), BF16),
                pltpu.SemaphoreType.DMA((n_band,)),
            ],
        ),
        compiler_params=params(20),
        cost_estimate=cost(
            2 * blk_count * block_rows * width * list_len * tile_rows, latent, latent, interp
        ),
        name="back",
    )(*lists[:2], latent, weights, *pieces)
    return (grid_out, mesh_out)


def solution(mesh):
    placed = (
        P(("groups", "band"), None),
        P(("groups", "band"), None),
        P(),
        P(),
        P(),
        P("band", None, None, None),
        P(),
        P(),
        P(),
        P(),
        P(),
    )
    n_y = max(1, 4 // mesh.shape["groups"])
    return jax.shard_map(
        functools.partial(on_device, n_y),
        mesh=mesh,
        in_specs=placed,
        out_specs=(P(("groups", "band"), None), P(("groups", "band"), None)),
        check_vma=False,
    )
```

```python
import functools

import jax
import jax.numpy as jnp
from jax import lax
from jax.experimental import pallas as pl
from jax.experimental.pallas import tpu as pltpu
from jax.sharding import PartitionSpec as P

F32 = jnp.float32
BF16 = jnp.bfloat16
N_CORE = 2


def silu(values):
    half = 0.5 * values
    return half * (1.0 + jnp.tanh(half))


def layer_norm(values, gain):
    centred = values - jnp.mean(values, axis=-1, keepdims=True)
    spread = jnp.mean(centred * centred, axis=-1, keepdims=True)
    return centred * lax.rsqrt(spread + 1e-05) * gain


def split(value, size):
    if size & (size - 1) == 0:
        return lax.shift_right_logical(value, size.bit_length() - 1), value & (size - 1)
    return lax.div(value, size), lax.rem(value, size)


class Ring:
    def __init__(self, n_band, n_y, tiles):
        self.n_band, self.n_y, self.tiles = n_band, n_y, tiles
        self.chips = n_band // N_CORE
        self.far = self.chips // 2

    def place(self, index):
        chip, core = split(index, N_CORE)
        z, y = split(chip, self.n_y)
        return z + y * (self.chips - 1 - 2 * z), core

    def index(self, ring, core):
        ring = ring % self.chips
        n_z = self.chips // self.n_y
        z, y = (ring, 0) if ring < n_z else (self.chips - 1 - ring, 1)
        return (z * self.n_y + y) * N_CORE + core

    def over_core(self, value):
        return lax.ppermute(value, "band", [(i, i ^ 1) for i in range(self.n_band)])

    def over(self, value, by):
        pairs = []
        for i in range(self.n_band):
            chip, core = divmod(i, N_CORE)
            z, y = divmod(chip, self.n_y)
            ring = z if y == 0 else self.chips - 1 - z
            pairs.append((i, self.index(ring + by, core)))
        return lax.ppermute(value, "band", pairs)

    def entry(self, lists_ref, me, block, k):
        owner, tile = split(lists_ref[k, block], self.tiles)
        ring, core = self.place(owner)
        my_ring, my_core = self.place(me)
        ahead = split(ring - my_ring + self.chips, self.chips)[1]
        return ahead, core ^ my_core, tile


def embed_kernel(
    ring, per_step, slots, me_ref, lists_ref, mask_ref,
    x_ref, w1_ref, w2_ref, gain_ref, interp_ref,
    latent_ref, kept_ref, sent_ref, table_ref,
):
    step = pl.program_id(0)
    me = me_ref[0]
    list_len, tile_rows, block_rows = interp_ref.shape[1:]
    blk_count = pl.num_programs(0) * per_step

    def spot(index, b, k):
        block = step * per_step + b
        ahead, across, tile = ring.entry(lists_ref, index, index * blk_count + block, k)
        slot = split(block * list_len + k, ring.n_band)[0]
        return (across * ring.chips + ahead) * slots + slot, tile

    def embedded(rows):
        first = lax.dot_general(
            x_ref[:, rows], w1_ref[...], (((0,), (0,)), ((), ())), preferred_element_type=F32
        )
        return jnp.dot(silu(first).astype(BF16), w2_ref[...], preferred_element_type=F32)

    spare = kept_ref.shape[0] - 1
    parts = 2
    part_rows = latent_ref.shape[0] // parts
    spans = [slice(i * part_rows, (i + 1) * part_rows) for i in range(parts)]
    befores = [embedded(rows) for rows in spans]
    for number, rows in enumerate(spans):
        latent = layer_norm(befores[number], gain_ref[...]).astype(BF16)
        latent_ref[rows] = latent
        for i in range(per_step // parts):
            b = number * (per_step // parts) + i
            block = step * per_step + b
            weights = interp_ref[b].reshape(list_len * tile_rows, block_rows)
            part = jnp.dot(
                weights, latent[i * block_rows : (i + 1) * block_rows], preferred_element_type=F32
            )
            for k in range(list_len):
                place, tile = spot(me, b, k)
                there, its_tile = spot(me ^ 1, b, k)
                mask = mask_ref[k, me * blk_count + block]
                table_ref[0, place] = tile
                table_ref[1, there] = its_tile
                table_ref[2, place] = mask
                table_ref[3, there] = mask_ref[k, (me ^ 1) * blk_count + block]
                table_ref[4, block * list_len + k] = place
                masked = part[k * tile_rows : (k + 1) * tile_rows] * mask.astype(F32)
                masked = masked.astype(BF16)
                kept_ref[jnp.minimum(place, spare)] = masked
                sent_ref[jnp.where(place >= spare, place - spare, spare)] = masked


def add_entries(total, table_ref, owner, slots, kept, other, chips):
    for slot in range(slots):
        place = owner * slots + slot
        total[table_ref[0, place]] += kept[place].astype(F32)
        total[table_ref[1, chips * slots + place]] += other[place].astype(F32)


def far_kernel(
    ring, slots, table_ref, kept, other, far_right, far_left, next_right, next_left, total
):
    half = total.shape[0] // 2
    for number, owner in enumerate((ring.far, ring.far - 1, ring.chips - ring.far + 1)):
        total[...] = jnp.zeros_like(total)
        add_entries(total, table_ref, owner, slots, kept, other, ring.chips)
        if number == 0:
            far_right[...] = total[:half].astype(BF16)
            far_left[...] = total[half:].astype(BF16)
        elif number == 1:
            next_right[...] = total[half:].astype(BF16)
        else:
            next_left[...] = total[:half].astype(BF16)


def own_kernel(ring, slots, table_ref, kept, other, own):
    number = pl.program_id(0)
    owner = number + (number >= ring.far).astype(jnp.int32)
    total = own.at[owner]
    total[...] = jnp.zeros_like(total)
    add_entries(total, table_ref, owner, slots, kept, other, ring.chips)


def mesh_kernel(
    latent_ref, up_ref, down_ref, gain_ref, own, right_a, left_b, right_b, left_a,
    out_ref, out_a, out_b,
):
    tiles, tile_rows, width = own.shape[1:]
    half = tiles // 2
    lower = own[0, :half] + right_a[...].astype(F32) + left_a[...].astype(F32)
    upper = own[0, half:] + right_b[...].astype(F32) + left_b[...].astype(F32)
    came = jnp.concatenate([lower, upper], axis=0).reshape(tiles * tile_rows, width)
    mesh_in = latent_ref[...].astype(F32) + came
    normed = layer_norm(mesh_in, gain_ref[...]).astype(BF16)
    hidden = silu(jnp.dot(normed, up_ref[...], preferred_element_type=F32)).astype(BF16)
    out = (mesh_in + jnp.dot(hidden, down_ref[...], preferred_element_type=F32)).astype(BF16)
    out_ref[...] = out
    out_a[...] = out[: half * tile_rows]
    out_b[...] = out[half * tile_rows :]


def add_kernel(owner, part, own, came, token, out):
    del token
    count = out.shape[0]
    mine = own[owner, part * count : (part + 1) * count]
    out[...] = (mine + came[...].astype(F32)).astype(BF16)


def order_kernel(*refs):
    del refs


def pick_kernel(owners, slots, chips, table_ref, *refs):
    halves, (mine, theirs) = refs[:-2], refs[-2:]
    tile_rows = mine.shape[1]
    count = halves[0].shape[0] // tile_rows
    for number, owner in enumerate(owners):
        lower, upper = halves[2 * number : 2 * number + 2]
        for slot in range(slots):
            for way, out in enumerate((mine, theirs)):
                place = (way * chips + owner) * slots + slot
                tile, mask = table_ref[way, place], table_ref[2 + way, place]
                above = tile >= count
                within = jnp.where(above, tile - count, tile)
                rows = pl.ds(pl.multiple_of(within * tile_rows, tile_rows), tile_rows)
                value = jnp.where(above, upper[rows], lower[rows])
                out[number * slots + slot] = jnp.where(mask == 1, value, jnp.zeros_like(value))


def back_kernel(places, slots, list_len, per_step, table_ref, latent_ref, weights_ref, *rest):
    count = len(places)
    pieces, (out_ref, held, sems) = rest[:count], rest[count:]
    step = pl.program_id(0)
    block_rows = weights_ref.shape[1]

    @pl.when(step == 0)
    def _():
        copies = []
        for i, (piece, place) in enumerate(zip(pieces, places)):
            for number, start in enumerate(place):
                copies.append(
                    pltpu.make_async_copy(
                        piece.at[pl.ds(number * slots, slots)],
                        held.at[pl.ds(start * slots, slots)],
                        sems.at[len(copies)],
                    )
                )
        for copy in copies:
            copy.start()
        for copy in copies:
            copy.wait()

    for b in range(per_step):
        first = (step * per_step + b) * list_len
        value = jnp.concatenate([held[table_ref[4, first + k]] for k in range(list_len)], axis=0)
        back = jnp.dot(weights_ref[b], value, preferred_element_type=F32)
        rows = slice(b * block_rows, (b + 1) * block_rows)
        out_ref[rows] = (latent_ref[rows].astype(F32) + back).astype(BF16)


def whole(array):
    zeros = (0,) * array.ndim
    return pl.BlockSpec(array.shape, lambda *_: zeros)


def params(mib):
    return pltpu.CompilerParams(vmem_limit_bytes=mib * 1024 * 1024)


def cost(flops, *arrays):
    size = sum(a.size * a.dtype.itemsize for a in arrays)
    return pl.CostEstimate(flops=int(flops), bytes_accessed=int(size), transcendentals=0)


def shape(dims, kind=BF16):
    return jax.ShapeDtypeStruct(dims, kind)


def on_device(
    n_y,
    grid_features,
    mesh_latent,
    embed_in,
    embed_out,
    embed_gain,
    interp,
    block_mask,
    tile_list,
    mesh_up,
    mesh_down,
    mesh_gain,
):
    n_band = lax.axis_size("band")
    blk_count, list_len, tile_rows, block_rows = interp.shape
    channels, width = embed_in.shape
    node_rows = mesh_latent.shape[0]
    tiles = node_rows // tile_rows
    half_tiles, half_rows = tiles // 2, node_rows // 2
    entries = blk_count * list_len
    slots = entries // n_band
    ring = Ring(n_band, n_y, tiles)
    chips, far = ring.chips, ring.far
    lists = (lax.axis_index("band").reshape(1), tile_list.T, block_mask.T)

    def in_hbm(array):
        return pltpu.with_memory_space_constraint(array, pltpu.HBM)

    gain = embed_gain.reshape(1, width)
    per_step = 4
    rows = per_step * block_rows
    held_shape = (chips * slots + 1, tile_rows, width)
    latent, kept, sent, table = pl.pallas_call(
        functools.partial(embed_kernel, ring, per_step, slots),
        out_shape=[shape((blk_count * block_rows, width))]
        + [shape(held_shape)] * N_CORE
        + [shape((5, entries), jnp.int32)],
        grid_spec=pltpu.PrefetchScalarGridSpec(
            num_scalar_prefetch=3,
            grid=(blk_count // per_step,),
            in_specs=[
                pl.BlockSpec((channels, rows), lambda i, *_: (0, i)),
                whole(embed_in),
                whole(embed_out),
                whole(gain),
                pl.BlockSpec((per_step,) + interp.shape[1:], lambda i, *_: (i, 0, 0, 0)),
            ],
            out_specs=[pl.BlockSpec((rows, width), lambda i, *_: (i, 0))]
            + [pl.BlockSpec(memory_space=pltpu.VMEM)] * N_CORE
            + [pl.BlockSpec(memory_space=pltpu.SMEM)],
        ),
        compiler_params=params(24),
        cost_estimate=cost(
            2 * blk_count * block_rows * width * (channels + width + list_len * tile_rows),
            grid_features,
            interp,
        ),
        name="embed",
    )(lists[0], *map(in_hbm, lists[1:] + (grid_features.T, embed_in, embed_out, gain, interp)))
    other = ring.over_core(sent)

    dense = (tiles, tile_rows, width)
    half_dense = (half_tiles, tile_rows, width)

    in_vmem = pl.BlockSpec(memory_space=pltpu.VMEM)
    far_right, far_left, next_right, next_left = pl.pallas_call(
        functools.partial(far_kernel, ring, slots),
        out_shape=[shape(half_dense)] * 4,
        grid_spec=pltpu.PrefetchScalarGridSpec(
            num_scalar_prefetch=1,
            grid=(1,),
            in_specs=[in_vmem] * 2,
            out_specs=[in_vmem] * 4,
            scratch_shapes=[pltpu.VMEM(dense, F32)],
        ),
        compiler_params=params(8),
        cost_estimate=cost(0, kept),
        name="far_chunks",
    )(table, kept, other)
    own = pl.pallas_call(
        functools.partial(own_kernel, ring, slots),
        out_shape=shape((chips,) + dense, F32),
        grid_spec=pltpu.PrefetchScalarGridSpec(
            num_scalar_prefetch=1,
            grid=(chips - 1,),
            in_specs=[in_vmem] * 2,
            out_specs=in_vmem,
        ),
        compiler_params=params(8 if n_band <= 16 else 24),
        cost_estimate=cost(0, kept, kept, kept, kept),
        name="own_chunks",
    )(table, kept, other)

    lower, upper = 0, 1

    def add_own(distance, part, value, token):
        return pl.pallas_call(
            functools.partial(add_kernel, distance % chips, part),
            out_shape=shape(half_dense),
            in_specs=[in_vmem] * 2 + [pl.BlockSpec(memory_space=pl.ANY)],
            out_specs=in_vmem,
            compiler_params=params(8),
            cost_estimate=cost(0, value, value),
            name=f"add_{'lr'[distance > 0]}{abs(distance)}{'ab'[part]}",
        )(own, value, token)

    def both(values):
        return [ring.over(values[0], 1), ring.over(values[1], -1)]

    def both_with_own(distance, parts, values, token):
        sent = []
        for way, part, value in zip((1, -1), parts, values):
            token = add_own(way * distance, part, value, token)
            sent.append(ring.over(token, way))
        return sent, token

    first, second = both((far_right, far_left)), both((next_right, next_left))
    token = own
    for distance in range(far - 1, 0, -1):
        first, token = both_with_own(distance, (lower, upper), first, token)
        if distance > 1:
            second, token = both_with_own(distance - 1, (upper, lower), second, token)

    mesh_gain = mesh_gain.reshape(1, width)
    came = (*first, *second)
    mesh_out, out_a, out_b = pl.pallas_call(
        mesh_kernel,
        out_shape=[shape((node_rows, width))] + [shape((half_rows, width))] * 2,
        in_specs=[in_vmem] * 9,
        out_specs=[in_vmem] * 3,
        compiler_params=params(16),
        cost_estimate=cost(4 * node_rows * width * width, mesh_up, mesh_down),
        name="mesh_step",
    )(mesh_latent, mesh_up, mesh_down, mesh_gain, own, *came)

    def in_order(values, token):
        return pl.pallas_call(
            order_kernel,
            out_shape=[shape(v.shape) for v in values],
            in_specs=[pl.BlockSpec(memory_space=pl.ANY)] * (len(values) + 1),
            out_specs=[pl.BlockSpec(memory_space=pl.ANY)] * len(values),
            input_output_aliases={i: i for i in range(len(values))},
            compiler_params=params(1),
            cost_estimate=cost(0),
            name="in_order",
        )(*values, token)

    pieces, places = [], []

    def pick(owners, halves):
        owners = [owner % chips for owner in owners]
        out = shape((len(owners) * slots, tile_rows, width))
        mine, theirs = pl.pallas_call(
            functools.partial(pick_kernel, owners, slots, chips),
            out_shape=[out] * 2,
            grid_spec=pltpu.PrefetchScalarGridSpec(
                num_scalar_prefetch=1,
                grid=(1,),
                in_specs=[in_vmem] * len(halves),
                out_specs=[in_vmem] * 2,
            ),
            compiler_params=params(8),
            cost_estimate=cost(0, *halves),
            name=f"pick_{owners[0]}",
        )(table, *halves)
        for across, value in enumerate((mine, ring.over_core(theirs))):
            pieces.append(value)
            places.append([across * chips + owner for owner in owners])
        return mine

    first, second = both((out_a, out_b)), both((out_b, out_a))
    token = pick([0], (out_a, out_b))
    for distance in range(1, far):
        first = in_order(first, token)
        onward = both(first)
        second = in_order(second, first[0])
        if distance < far - 1:
            after = both(second)
        token = pick([-distance, distance], (first[0], second[0], second[1], first[1]))
        first, second = onward, after
    pick([far], first)

    weights = jnp.swapaxes(interp.reshape(blk_count, list_len * tile_rows, block_rows), 1, 2)
    per_step = 4
    rows = per_step * block_rows
    grid_out = pl.pallas_call(
        functools.partial(back_kernel, places, slots, list_len, per_step),
        out_shape=shape((blk_count * block_rows, width)),
        grid_spec=pltpu.PrefetchScalarGridSpec(
            num_scalar_prefetch=1,
            grid=(blk_count // per_step,),
            in_specs=[
                pl.BlockSpec((rows, width), lambda i, *_: (i, 0)),
                pl.BlockSpec((per_step,) + weights.shape[1:], lambda i, *_: (i, 0, 0)),
            ]
            + [pl.BlockSpec(memory_space=pl.ANY)] * len(pieces),
            out_specs=pl.BlockSpec((rows, width), lambda i, *_: (i, 0)),
            scratch_shapes=[
                pltpu.VMEM((entries, tile_rows, width), BF16),
                pltpu.SemaphoreType.DMA((n_band,)),
            ],
        ),
        compiler_params=params(20),
        cost_estimate=cost(
            2 * blk_count * block_rows * width * list_len * tile_rows, latent, latent, interp
        ),
        name="back",
    )(table, latent, weights, *pieces)
    return (grid_out, mesh_out)


def solution(mesh):
    placed = (
        P(("groups", "band"), None),
        P(("groups", "band"), None),
        P(),
        P(),
        P(),
        P("band", None, None, None),
        P(),
        P(),
        P(),
        P(),
        P(),
    )
    n_y = max(1, 4 // mesh.shape["groups"])
    return jax.shard_map(
        functools.partial(on_device, n_y),
        mesh=mesh,
        in_specs=placed,
        out_specs=(P(("groups", "band"), None), P(("groups", "band"), None)),
        check_vma=False,
    )
```

```python
import functools

import jax
import jax.numpy as jnp
from jax import lax
from jax.experimental import pallas as pl
from jax.experimental.pallas import tpu as pltpu
from jax.sharding import PartitionSpec as P

F32 = jnp.float32
BF16 = jnp.bfloat16
N_CORE = 2


def silu(values):
    half = 0.5 * values
    return half * (1.0 + jnp.tanh(half))


def layer_norm(values, gain):
    centred = values - jnp.mean(values, axis=-1, keepdims=True)
    spread = jnp.mean(centred * centred, axis=-1, keepdims=True)
    return centred * lax.rsqrt(spread + 1e-05) * gain


def split(value, size):
    if size & (size - 1) == 0:
        return lax.shift_right_logical(value, size.bit_length() - 1), value & (size - 1)
    return lax.div(value, size), lax.rem(value, size)


class Ring:
    def __init__(self, n_band, n_y, tiles):
        self.n_band, self.n_y, self.tiles = n_band, n_y, tiles
        self.chips = n_band // N_CORE
        self.far = self.chips // 2

    def place(self, index):
        chip, core = split(index, N_CORE)
        z, y = split(chip, self.n_y)
        return z + y * (self.chips - 1 - 2 * z), core

    def index(self, ring, core):
        ring = ring % self.chips
        n_z = self.chips // self.n_y
        z, y = (ring, 0) if ring < n_z else (self.chips - 1 - ring, 1)
        return (z * self.n_y + y) * N_CORE + core

    def over_core(self, value):
        return lax.ppermute(value, "band", [(i, i ^ 1) for i in range(self.n_band)])

    def over(self, value, by):
        pairs = []
        for i in range(self.n_band):
            chip, core = divmod(i, N_CORE)
            z, y = divmod(chip, self.n_y)
            ring = z if y == 0 else self.chips - 1 - z
            pairs.append((i, self.index(ring + (-by if core else by), core)))
        return lax.ppermute(value, "band", pairs)

    def entry(self, lists_ref, me, block, k):
        owner, tile = split(lists_ref[k, block], self.tiles)
        ring, core = self.place(owner)
        my_ring, my_core = self.place(me)
        ahead = split(ring - my_ring + self.chips, self.chips)[1]
        left = (ahead > self.far).astype(jnp.int32)
        shared = (ahead == 0) | (ahead == self.far)
        handler = jnp.where(shared, core, left)
        distance = jnp.where(ahead > self.far, self.chips - ahead, ahead)
        group = jnp.maximum(2 * distance - 1 + (core ^ handler), 0)
        return handler ^ my_core, group, tile


def embed_kernel(
    ring, per_step, slots, me_ref, lists_ref, mask_ref,
    x_ref, w1_ref, w2_ref, gain_ref, interp_ref,
    latent_ref, kept_ref, sent_ref, table_ref,
):
    step = pl.program_id(0)
    me = me_ref[0]
    list_len, tile_rows, block_rows = interp_ref.shape[1:]
    blk_count = pl.num_programs(0) * per_step

    def spot(index, b, k):
        block = step * per_step + b
        across, group, tile = ring.entry(lists_ref, index, index * blk_count + block, k)
        slot = split(block * list_len + k, ring.n_band)[0]
        return (across * ring.chips + group) * slots + slot, tile

    def embedded(rows):
        first = lax.dot_general(
            x_ref[:, rows], w1_ref[...], (((0,), (0,)), ((), ())), preferred_element_type=F32
        )
        return jnp.dot(silu(first).astype(BF16), w2_ref[...], preferred_element_type=F32)

    spare = kept_ref.shape[0] - 1
    parts = 2
    part_rows = latent_ref.shape[0] // parts
    spans = [slice(i * part_rows, (i + 1) * part_rows) for i in range(parts)]
    befores = [embedded(rows) for rows in spans]
    for number, rows in enumerate(spans):
        latent = layer_norm(befores[number], gain_ref[...]).astype(BF16)
        latent_ref[rows] = latent
        for i in range(per_step // parts):
            b = number * (per_step // parts) + i
            block = step * per_step + b
            weights = interp_ref[b].reshape(list_len * tile_rows, block_rows)
            part = jnp.dot(
                weights, latent[i * block_rows : (i + 1) * block_rows], preferred_element_type=F32
            )
            for k in range(list_len):
                place, tile = spot(me, b, k)
                there, its_tile = spot(me ^ 1, b, k)
                mask = mask_ref[k, me * blk_count + block]
                table_ref[0, place] = tile
                table_ref[1, there] = its_tile
                table_ref[2, place] = mask
                table_ref[3, there] = mask_ref[k, (me ^ 1) * blk_count + block]
                table_ref[4, block * list_len + k] = place
                masked = part[k * tile_rows : (k + 1) * tile_rows] * mask.astype(F32)
                masked = masked.astype(BF16)
                kept_ref[jnp.minimum(place, spare)] = masked
                sent_ref[jnp.where(place >= spare, place - spare, spare)] = masked


def add_entries(total, table_ref, group, slots, kept, other, groups):
    for slot in range(slots):
        place = group * slots + slot
        total[table_ref[0, place]] += kept[place].astype(F32)
        total[table_ref[1, groups * slots + place]] += other[place].astype(F32)


def far_kernel(slots, groups, table_ref, kept, other, far, before, total):
    for group, out in ((groups - 1, far), (groups - 2, before)):
        total[...] = jnp.zeros_like(total)
        add_entries(total, table_ref, group, slots, kept, other, groups)
        out[...] = total[...].astype(BF16)


def own_kernel(slots, groups, table_ref, kept, other, own):
    group = pl.program_id(0)
    total = own.at[group]
    total[...] = jnp.zeros_like(total)
    add_entries(total, table_ref, group, slots, kept, other, groups)


def add_kernel(group, own, came, token, out):
    del token
    out[...] = (own[group] + came[...].astype(F32)).astype(BF16)


def mesh_kernel(
    latent_ref, up_ref, down_ref, gain_ref, own, came, neighbour, out_ref, piece_ref
):
    total = own[0] + came[...].astype(F32) + neighbour[...].astype(F32)
    mesh_in = latent_ref[...].astype(F32) + total.reshape(latent_ref.shape)
    normed = layer_norm(mesh_in, gain_ref[...]).astype(BF16)
    hidden = silu(jnp.dot(normed, up_ref[...], preferred_element_type=F32)).astype(BF16)
    out = (mesh_in + jnp.dot(hidden, down_ref[...], preferred_element_type=F32)).astype(BF16)
    out_ref[...] = out
    piece_ref[...] = out


def order_kernel(*refs):
    del refs


def pick_kernel(chosen, slots, groups, table_ref, *refs):
    pieces, (mine, theirs) = refs[:-2], refs[-2:]
    tile_rows = mine.shape[1]
    for number, group in enumerate(chosen):
        for slot in range(slots):
            for way, out in enumerate((mine, theirs)):
                place = (way * groups + group) * slots + slot
                tile = table_ref[way, place]
                rows = pl.ds(pl.multiple_of(tile * tile_rows, tile_rows), tile_rows)
                value = pieces[number][rows]
                listed = table_ref[2 + way, place] == 1
                out[number * slots + slot] = jnp.where(listed, value, jnp.zeros_like(value))


def back_kernel(places, slots, list_len, per_step, table_ref, latent_ref, weights_ref, *rest):
    count = len(places)
    pieces, (out_ref, held, sems) = rest[:count], rest[count:]
    step = pl.program_id(0)
    block_rows = weights_ref.shape[1]

    @pl.when(step == 0)
    def _():
        copies = []
        for i, (piece, place) in enumerate(zip(pieces, places)):
            for number, start in enumerate(place):
                copies.append(
                    pltpu.make_async_copy(
                        piece.at[pl.ds(number * slots, slots)],
                        held.at[pl.ds(start * slots, slots)],
                        sems.at[len(copies)],
                    )
                )
        for copy in copies:
            copy.start()
        for copy in copies:
            copy.wait()

    for b in range(per_step):
        first = (step * per_step + b) * list_len
        value = jnp.concatenate([held[table_ref[4, first + k]] for k in range(list_len)], axis=0)
        back = jnp.dot(weights_ref[b], value, preferred_element_type=F32)
        rows = slice(b * block_rows, (b + 1) * block_rows)
        out_ref[rows] = (latent_ref[rows].astype(F32) + back).astype(BF16)


def whole(array):
    zeros = (0,) * array.ndim
    return pl.BlockSpec(array.shape, lambda *_: zeros)


def params(mib):
    return pltpu.CompilerParams(vmem_limit_bytes=mib * 1024 * 1024)


def cost(flops, *arrays):
    size = sum(a.size * a.dtype.itemsize for a in arrays)
    return pl.CostEstimate(flops=int(flops), bytes_accessed=int(size), transcendentals=0)


def shape(dims, kind=BF16):
    return jax.ShapeDtypeStruct(dims, kind)


def on_device(
    n_y,
    grid_features,
    mesh_latent,
    embed_in,
    embed_out,
    embed_gain,
    interp,
    block_mask,
    tile_list,
    mesh_up,
    mesh_down,
    mesh_gain,
):
    n_band = lax.axis_size("band")
    blk_count, list_len, tile_rows, block_rows = interp.shape
    channels, width = embed_in.shape
    node_rows = mesh_latent.shape[0]
    tiles = node_rows // tile_rows
    entries = blk_count * list_len
    slots = entries // n_band
    ring = Ring(n_band, n_y, tiles)
    chips, far = ring.chips, ring.far
    lists = (lax.axis_index("band").reshape(1), tile_list.T, block_mask.T)

    def in_hbm(array):
        return pltpu.with_memory_space_constraint(array, pltpu.HBM)

    gain = embed_gain.reshape(1, width)
    per_step = 4
    rows = per_step * block_rows
    held_shape = (chips * slots + 1, tile_rows, width)
    latent, kept, sent, table = pl.pallas_call(
        functools.partial(embed_kernel, ring, per_step, slots),
        out_shape=[pltpu.HBM((blk_count * block_rows, width), BF16)]
        + [shape(held_shape)] * N_CORE
        + [shape((5, entries), jnp.int32)],
        grid_spec=pltpu.PrefetchScalarGridSpec(
            num_scalar_prefetch=3,
            grid=(blk_count // per_step,),
            in_specs=[
                pl.BlockSpec((channels, rows), lambda i, *_: (0, i)),
                whole(embed_in),
                whole(embed_out),
                whole(gain),
                pl.BlockSpec((per_step,) + interp.shape[1:], lambda i, *_: (i, 0, 0, 0)),
            ],
            out_specs=[pl.BlockSpec((rows, width), lambda i, *_: (i, 0))]
            + [pl.BlockSpec(memory_space=pltpu.VMEM)] * N_CORE
            + [pl.BlockSpec(memory_space=pltpu.SMEM)],
        ),
        compiler_params=params(24),
        cost_estimate=cost(
            2 * blk_count * block_rows * width * (channels + width + list_len * tile_rows),
            grid_features,
            interp,
        ),
        name="embed",
    )(lists[0], *map(in_hbm, lists[1:] + (grid_features.T, embed_in, embed_out, gain, interp)))
    other = ring.over_core(sent)

    dense = (tiles, tile_rows, width)
    in_vmem = pl.BlockSpec(memory_space=pltpu.VMEM)
    in_any = pl.BlockSpec(memory_space=pl.ANY)
    first, second = pl.pallas_call(
        functools.partial(far_kernel, slots, chips),
        out_shape=[shape(dense)] * 2,
        grid_spec=pltpu.PrefetchScalarGridSpec(
            num_scalar_prefetch=1,
            grid=(1,),
            in_specs=[in_vmem] * 2,
            out_specs=[in_vmem] * 2,
            scratch_shapes=[pltpu.VMEM(dense, F32)],
        ),
        compiler_params=params(8),
        cost_estimate=cost(0, kept),
        name="far_sums",
    )(table, kept, other)
    own = pl.pallas_call(
        functools.partial(own_kernel, slots, chips),
        out_shape=shape((chips - 1,) + dense, F32),
        grid_spec=pltpu.PrefetchScalarGridSpec(
            num_scalar_prefetch=1,
            grid=(chips - 1,),
            in_specs=[in_vmem] * 2,
            out_specs=in_vmem,
        ),
        compiler_params=params(8 if n_band <= 16 else 24),
        cost_estimate=cost(0, kept, kept, kept, kept),
        name="own_sums",
    )(table, kept, other)

    def add_own(group, value, token):
        return pl.pallas_call(
            functools.partial(add_kernel, group),
            out_shape=shape(dense),
            in_specs=[in_vmem] * 2 + [in_any],
            out_specs=in_vmem,
            compiler_params=params(8),
            cost_estimate=cost(0, value, value),
            name=f"add_{group}",
        )(own, value, token)

    first, second = ring.over(first, 1), ring.over(second, 1)
    token = own
    for group in range(chips - 3, 0, -1):
        if group % 2:
            token = add_own(group, first, token)
            first = ring.over(token, 1)
        else:
            token = add_own(group, second, token)
            second = ring.over(token, 1)
    second = ring.over_core(second)

    mesh_gain = mesh_gain.reshape(1, width)
    mesh_out, piece = pl.pallas_call(
        mesh_kernel,
        out_shape=[shape((node_rows, width))] * 2,
        in_specs=[in_vmem] * 7,
        out_specs=[in_vmem] * 2,
        compiler_params=params(16),
        cost_estimate=cost(4 * node_rows * width * width, mesh_up, mesh_down),
        name="mesh_step",
    )(mesh_latent, mesh_up, mesh_down, mesh_gain, own, first, second)

    def in_order(value, token):
        return pl.pallas_call(
            order_kernel,
            out_shape=shape(value.shape),
            in_specs=[in_any] * 2,
            out_specs=in_any,
            input_output_aliases={0: 0},
            compiler_params=params(1),
            cost_estimate=cost(0),
            name="in_order",
        )(value, token)

    pieces, places = [], []

    def pick(chosen, values):
        out = shape((len(chosen) * slots, tile_rows, width))
        mine, theirs = pl.pallas_call(
            functools.partial(pick_kernel, chosen, slots, chips),
            out_shape=[out] * 2,
            grid_spec=pltpu.PrefetchScalarGridSpec(
                num_scalar_prefetch=1,
                grid=(1,),
                in_specs=[in_vmem] * len(values),
                out_specs=[in_vmem] * 2,
            ),
            compiler_params=params(8),
            cost_estimate=cost(0, *values),
            name=f"pick_{chosen[0]}",
        )(table, *values)
        for across, value in enumerate((mine, ring.over_core(theirs))):
            pieces.append(value)
            places.append([across * chips + group for group in chosen])
        return mine

    first = ring.over(piece, -1)
    second = ring.over(ring.over_core(piece), -1)
    token = pick([0], [piece])
    for distance in range(1, far):
        first = in_order(first, token)
        onward = ring.over(first, -1)
        second = in_order(second, first)
        if distance < far - 1:
            after = ring.over(second, -1)
        token = pick([2 * distance - 1, 2 * distance], [first, second])
        first, second = onward, after
    pick([chips - 1], [first])

    weights = jnp.swapaxes(interp.reshape(blk_count, list_len * tile_rows, block_rows), 1, 2)
    per_step = 4
    rows = per_step * block_rows
    grid_out = pl.pallas_call(
        functools.partial(back_kernel, places, slots, list_len, per_step),
        out_shape=shape((blk_count * block_rows, width)),
        grid_spec=pltpu.PrefetchScalarGridSpec(
            num_scalar_prefetch=1,
            grid=(blk_count // per_step,),
            in_specs=[
                pl.BlockSpec((rows, width), lambda i, *_: (i, 0)),
                pl.BlockSpec((per_step,) + weights.shape[1:], lambda i, *_: (i, 0, 0)),
            ]
            + [pl.BlockSpec(memory_space=pl.ANY)] * len(pieces),
            out_specs=pl.BlockSpec((rows, width), lambda i, *_: (i, 0)),
            scratch_shapes=[
                pltpu.VMEM((entries, tile_rows, width), BF16),
                pltpu.SemaphoreType.DMA((n_band,)),
            ],
        ),
        compiler_params=params(20),
        cost_estimate=cost(
            2 * blk_count * block_rows * width * list_len * tile_rows, latent, latent, interp
        ),
        name="back",
    )(table, latent, weights, *pieces)
    return (grid_out, mesh_out)


def solution(mesh):
    placed = (
        P(("groups", "band"), None),
        P(("groups", "band"), None),
        P(),
        P(),
        P(),
        P("band", None, None, None),
        P(),
        P(),
        P(),
        P(),
        P(),
    )
    n_y = max(1, 4 // mesh.shape["groups"])
    return jax.shard_map(
        functools.partial(on_device, n_y),
        mesh=mesh,
        in_specs=placed,
        out_specs=(P(("groups", "band"), None), P(("groups", "band"), None)),
        check_vma=False,
    )
```

```python
import functools

import jax
import jax.numpy as jnp
from jax import lax
from jax.experimental import pallas as pl
from jax.experimental.pallas import tpu as pltpu
from jax.sharding import PartitionSpec as P

F32 = jnp.float32
BF16 = jnp.bfloat16
N_CORE = 2
STRIP = 32
PART = 2


def silu(values):
    half = 0.5 * values
    return half * (1.0 + jnp.tanh(half))


def layer_norm(values, gain):
    centred = values - jnp.mean(values, axis=-1, keepdims=True)
    spread = jnp.mean(centred * centred, axis=-1, keepdims=True)
    return centred * lax.rsqrt(spread + 1e-05) * gain


def split(value, size):
    if size & (size - 1) == 0:
        return lax.shift_right_logical(value, size.bit_length() - 1), value & (size - 1)
    return lax.div(value, size), lax.rem(value, size)


class Ring:
    def __init__(self, n_band, n_y, tiles):
        self.n_band, self.n_y, self.tiles = n_band, n_y, tiles
        self.chips = n_band // N_CORE
        self.far = self.chips // 2

    def place(self, index):
        chip, core = split(index, N_CORE)
        z, y = split(chip, self.n_y)
        return z + y * (self.chips - 1 - 2 * z), core

    def index(self, ring, core):
        ring = ring % self.chips
        n_z = self.chips // self.n_y
        z, y = (ring, 0) if ring < n_z else (self.chips - 1 - ring, 1)
        return (z * self.n_y + y) * N_CORE + core

    def over_core(self, value):
        return lax.ppermute(value, "band", [(i, i ^ 1) for i in range(self.n_band)])

    def over(self, value, by, cross=0):
        pairs = []
        for i in range(self.n_band):
            chip, core = divmod(i, N_CORE)
            z, y = divmod(chip, self.n_y)
            ring = z if y == 0 else self.chips - 1 - z
            pairs.append((i, self.index(ring + (-by if core else by), core ^ cross)))
        return lax.ppermute(value, "band", pairs)

    def entry(self, lists_ref, me, block, k):
        owner, tile = split(lists_ref[k, block], self.tiles)
        ring, core = self.place(owner)
        my_ring, my_core = self.place(me)
        ahead = split(ring - my_ring + self.chips, self.chips)[1]
        left = (ahead > self.far).astype(jnp.int32)
        shared = (ahead == 0) | (ahead == self.far)
        handler = jnp.where(shared, core, left)
        distance = jnp.where(ahead > self.far, self.chips - ahead, ahead)
        group = jnp.maximum(2 * distance - 1 + (core ^ handler), 0)
        return handler ^ my_core, group, tile


def strips(rows):
    return [slice(r, r + STRIP) for r in range(rows.start, rows.stop, STRIP)]


def embed_kernel(
    ring, per_step, slots, me_ref, lists_ref, mask_ref,
    x_ref, w1_ref, w2_ref, gain_ref, interp_ref,
    latent_ref, kept_ref, sent_ref, table_ref, wide, hidden,
):
    step = pl.program_id(0)
    me = me_ref[0]
    list_len, tile_rows, block_rows = interp_ref.shape[1:]
    blk_count = pl.num_programs(0) * per_step
    groups = ring.chips

    def spot(index, block, k):
        across, group, tile = ring.entry(lists_ref, index, index * blk_count + block, k)
        slot = split(block * list_len + k, ring.n_band)[0]
        return across, group, tile, slot

    part_rows = PART * block_rows
    spans = [slice(i * part_rows, (i + 1) * part_rows) for i in range(per_step // PART)]
    for rows in spans:
        wide[rows] = lax.dot_general(
            x_ref[:, rows], w1_ref[...], (((0,), (0,)), ((), ())), preferred_element_type=F32
        )
    for rows in spans:
        for strip in strips(rows):
            hidden[strip] = silu(wide[strip]).astype(BF16)
        wide[rows] = jnp.dot(hidden[rows], w2_ref[...], preferred_element_type=F32)
    spare = kept_ref.shape[0] - 1
    for number, rows in enumerate(spans):
        for strip in strips(rows):
            latent_ref[strip] = layer_norm(wide[strip], gain_ref[...]).astype(BF16)
        for b in range(number * PART, (number + 1) * PART):
            block = step * per_step + b
            weights = interp_ref[b].reshape(list_len * tile_rows, block_rows)
            latent = latent_ref[b * block_rows : (b + 1) * block_rows]
            part = jnp.dot(weights, latent, preferred_element_type=F32)
            for k in range(list_len):
                across, group, tile, slot = spot(me, block, k)
                place = (across * groups + group) * slots + slot
                mask = mask_ref[k, me * blk_count + block]
                table_ref[0, place] = tile
                found = group * slots + jnp.where(group == groups - 1, tile, slot)
                table_ref[2, block * list_len + k] = found + across * (
                    (groups - 1) * slots + ring.tiles
                )
                table_ref[3, block * list_len + k] = mask
                across, group, tile, slot = spot(me ^ 1, block, k)
                table_ref[1, (across * groups + group) * slots + slot] = tile
                masked = part[k * tile_rows : (k + 1) * tile_rows] * mask.astype(F32)
                masked = masked.astype(BF16)
                kept_ref[jnp.minimum(place, spare)] = masked
                sent_ref[jnp.where(place >= spare, place - spare, spare)] = masked


def add_entries(total, table_ref, group, slots, kept, other, groups):
    for slot in range(slots):
        place = group * slots + slot
        total[table_ref[0, place]] += kept[place].astype(F32)
        total[table_ref[1, groups * slots + place]] += other[place].astype(F32)


def far_kernel(slots, groups, table_ref, kept, other, far, before, total):
    for group, out in ((groups - 1, far), (groups - 2, before)):
        total[...] = jnp.zeros_like(total)
        add_entries(total, table_ref, group, slots, kept, other, groups)
        out[...] = total[...].astype(BF16)


def own_kernel(slots, groups, table_ref, kept, other, own):
    group = pl.program_id(0)
    total = own.at[group]
    total[...] = jnp.zeros_like(total)
    add_entries(total, table_ref, group, slots, kept, other, groups)


def add_kernel(group, own, came, token, out):
    del token
    out[...] = (own[group] + came[...].astype(F32)).astype(BF16)


def mesh_kernel(
    latent_ref, up_ref, down_ref, gain_ref, own, came, neighbour, out_ref, piece_ref
):
    total = own[0] + came[...].astype(F32) + neighbour[...].astype(F32)
    mesh_in = latent_ref[...].astype(F32) + total.reshape(latent_ref.shape)
    normed = layer_norm(mesh_in, gain_ref[...]).astype(BF16)
    hidden = silu(jnp.dot(normed, up_ref[...], preferred_element_type=F32)).astype(BF16)
    out = (mesh_in + jnp.dot(hidden, down_ref[...], preferred_element_type=F32)).astype(BF16)
    out_ref[...] = out
    piece_ref[...] = out


def order_kernel(*refs):
    del refs


def pick_kernel(chosen, slots, groups, tile_rows, table_ref, *refs):
    pieces, outs = refs[:-2], refs[-2:]
    for number, group in enumerate(chosen):
        for slot in range(slots):
            for way, out in enumerate(outs):
                tile = table_ref[way, (way * groups + group) * slots + slot]
                rows = pl.ds(pl.multiple_of(tile * tile_rows, tile_rows), tile_rows)
                into = (number * slots + slot) * tile_rows
                out[into : into + tile_rows] = pieces[number][rows]


def turn_kernel(interp_ref, token, out_ref):
    del token
    for b in range(interp_ref.shape[0]):
        out_ref[b] = interp_ref[b].reshape(out_ref.shape[2], out_ref.shape[1]).T


def back_kernel(starts, list_len, per_step, table_ref, latent_ref, weights_ref, *rest):
    count = len(starts)
    pieces, (out_ref, held, total, sems) = rest[:count], rest[count:]
    step = pl.program_id(0)
    block_rows = weights_ref.shape[1]
    tile_rows = weights_ref.shape[2] // list_len

    @pl.when(step == 0)
    def _():
        copies = []
        for i, (piece, start) in enumerate(zip(pieces, starts)):
            into = held.at[pl.ds(start, piece.shape[0])]
            copies.append(pltpu.make_async_copy(piece, into, sems.at[i]))
        for copy in copies:
            copy.start()
        for copy in copies:
            copy.wait()

    for b in range(per_step):
        values = []
        for k in range(list_len):
            entry = (step * per_step + b) * list_len + k
            rows = pl.ds(pl.multiple_of(table_ref[2, entry] * tile_rows, tile_rows), tile_rows)
            value = held[rows]
            values.append(jnp.where(table_ref[3, entry] == 1, value, jnp.zeros_like(value)))
        value = jnp.concatenate(values, axis=0)
        rows = slice(b * block_rows, (b + 1) * block_rows)
        total[rows] = jnp.dot(weights_ref[b], value, preferred_element_type=F32)
        for strip in strips(rows):
            out_ref[strip] = (latent_ref[strip].astype(F32) + total[strip]).astype(BF16)


def whole(array):
    zeros = (0,) * array.ndim
    return pl.BlockSpec(array.shape, lambda *_: zeros)


def params(mib):
    return pltpu.CompilerParams(vmem_limit_bytes=mib * 1024 * 1024)


def cost(flops, *arrays):
    size = sum(a.size * a.dtype.itemsize for a in arrays)
    return pl.CostEstimate(flops=int(flops), bytes_accessed=int(size), transcendentals=0)


def shape(dims, kind=BF16):
    return jax.ShapeDtypeStruct(dims, kind)


def on_device(
    n_y,
    grid_features,
    mesh_latent,
    embed_in,
    embed_out,
    embed_gain,
    interp,
    block_mask,
    tile_list,
    mesh_up,
    mesh_down,
    mesh_gain,
):
    n_band = lax.axis_size("band")
    blk_count, list_len, tile_rows, block_rows = interp.shape
    channels, width = embed_in.shape
    node_rows = mesh_latent.shape[0]
    tiles = node_rows // tile_rows
    entries = blk_count * list_len
    slots = entries // n_band
    ring = Ring(n_band, n_y, tiles)
    chips, far = ring.chips, ring.far
    lists = (lax.axis_index("band").reshape(1), tile_list.T, block_mask.T)

    def in_hbm(array):
        return pltpu.with_memory_space_constraint(array, pltpu.HBM)

    gain = embed_gain.reshape(1, width)
    per_step = 4
    rows = per_step * block_rows
    held_shape = (chips * slots + 1, tile_rows, width)
    latent, kept, sent, table = pl.pallas_call(
        functools.partial(embed_kernel, ring, per_step, slots),
        out_shape=[pltpu.HBM((blk_count * block_rows, width), BF16)]
        + [shape(held_shape)] * N_CORE
        + [shape((4, entries), jnp.int32)],
        grid_spec=pltpu.PrefetchScalarGridSpec(
            num_scalar_prefetch=3,
            grid=(blk_count // per_step,),
            in_specs=[
                pl.BlockSpec((channels, rows), lambda i, *_: (0, i)),
                whole(embed_in),
                whole(embed_out),
                whole(gain),
                pl.BlockSpec((per_step,) + interp.shape[1:], lambda i, *_: (i, 0, 0, 0)),
            ],
            out_specs=[pl.BlockSpec((rows, width), lambda i, *_: (i, 0))]
            + [pl.BlockSpec(memory_space=pltpu.VMEM)] * N_CORE
            + [pl.BlockSpec(memory_space=pltpu.SMEM)],
            scratch_shapes=[pltpu.VMEM((rows, width), F32), pltpu.VMEM((rows, width), BF16)],
        ),
        compiler_params=params(24),
        cost_estimate=cost(
            2 * blk_count * block_rows * width * (channels + width + list_len * tile_rows),
            grid_features,
            interp,
        ),
        name="embed",
    )(lists[0], *map(in_hbm, lists[1:] + (grid_features.T, embed_in, embed_out, gain, interp)))
    other = ring.over_core(sent)

    dense = (tiles, tile_rows, width)
    in_vmem = pl.BlockSpec(memory_space=pltpu.VMEM)
    in_any = pl.BlockSpec(memory_space=pl.ANY)
    first, second = pl.pallas_call(
        functools.partial(far_kernel, slots, chips),
        out_shape=[shape(dense)] * 2,
        grid_spec=pltpu.PrefetchScalarGridSpec(
            num_scalar_prefetch=1,
            grid=(1,),
            in_specs=[in_vmem] * 2,
            out_specs=[in_vmem] * 2,
            scratch_shapes=[pltpu.VMEM(dense, F32)],
        ),
        compiler_params=params(8),
        cost_estimate=cost(0, kept),
        name="far_sums",
    )(table, kept, other)
    own = pl.pallas_call(
        functools.partial(own_kernel, slots, chips),
        out_shape=shape((chips - 1,) + dense, F32),
        grid_spec=pltpu.PrefetchScalarGridSpec(
            num_scalar_prefetch=1,
            grid=(chips - 1,),
            in_specs=[in_vmem] * 2,
            out_specs=in_vmem,
        ),
        compiler_params=params(8 if n_band <= 16 else 24),
        cost_estimate=cost(0, kept, kept, kept, kept),
        name="own_sums",
    )(table, kept, other)

    def in_order(value, token):
        return pl.pallas_call(
            order_kernel,
            out_shape=shape(value.shape),
            in_specs=[in_any] * 2,
            out_specs=in_any,
            input_output_aliases={0: 0},
            compiler_params=params(1),
            cost_estimate=cost(0),
            name="in_order",
        )(value, token)

    def add_own(group, value, token):
        return pl.pallas_call(
            functools.partial(add_kernel, group),
            out_shape=shape(dense),
            in_specs=[in_vmem] * 2 + [in_any],
            out_specs=in_vmem,
            compiler_params=params(8),
            cost_estimate=cost(0),
            name=f"add_{group}",
        )(own, value, token)

    first, second = ring.over(first, 1), ring.over(second, 1)
    turned = (blk_count, block_rows, list_len * tile_rows)
    per_step = 4
    token = weights = pl.pallas_call(
        turn_kernel,
        out_shape=shape(turned),
        grid=(blk_count // per_step,),
        in_specs=[pl.BlockSpec((per_step,) + interp.shape[1:], lambda i: (i, 0, 0, 0)), in_any],
        out_specs=pl.BlockSpec((per_step,) + turned[1:], lambda i: (i, 0, 0)),
        compiler_params=params(8),
        cost_estimate=cost(0, interp, interp),
        name="turn",
    )(interp, own)
    for group in range(chips - 3, 0, -1):
        if group % 2:
            token = add_own(group, first, token)
            first = ring.over(token, 1)
        else:
            token = add_own(group, second, token)
            second = ring.over(token, 1, int(group == 2))

    mesh_gain = mesh_gain.reshape(1, width)
    mesh_out, piece = pl.pallas_call(
        mesh_kernel,
        out_shape=[shape((node_rows, width))] * 2,
        in_specs=[in_vmem] * 7,
        out_specs=[in_vmem] * 2,
        compiler_params=params(16),
        cost_estimate=cost(4 * node_rows * width * width, mesh_up, mesh_down),
        name="mesh_step",
    )(mesh_latent, mesh_up, mesh_down, mesh_gain, own, first, second)

    pieces, starts = [], []

    def share(index, mine, theirs):
        for across, value in enumerate((mine, ring.over_core(theirs))):
            pieces.append(value)
            starts.append((across * ((chips - 1) * slots + tiles) + index) * tile_rows)

    def pick(chosen, values):
        out = shape((len(chosen) * slots * tile_rows, width))
        mine, theirs = pl.pallas_call(
            functools.partial(pick_kernel, chosen, slots, chips, tile_rows),
            out_shape=[out] * 2,
            grid_spec=pltpu.PrefetchScalarGridSpec(
                num_scalar_prefetch=1,
                grid=(1,),
                in_specs=[in_vmem] * len(values),
                out_specs=[in_vmem] * 2,
            ),
            compiler_params=params(8),
            cost_estimate=cost(0, *values),
            name=f"pick_{chosen[0]}",
        )(table, *values)
        share(chosen[0] * slots, mine, theirs)
        return mine

    first = ring.over(piece, -1)
    second = ring.over(piece, 1, 1)
    token = pick([0], [piece])
    for distance in range(1, far):
        first = in_order(first, token)
        onward = ring.over(first, -1)
        second = in_order(second, first)
        if distance < far - 1:
            after = ring.over(second, -1)
        token = pick([2 * distance - 1, 2 * distance], [first, second])
        first, second = onward, after
    share((chips - 1) * slots, first, first)

    per_step = 4
    rows = per_step * block_rows
    grid_out = pl.pallas_call(
        functools.partial(back_kernel, starts, list_len, per_step),
        out_shape=shape((blk_count * block_rows, width)),
        grid_spec=pltpu.PrefetchScalarGridSpec(
            num_scalar_prefetch=1,
            grid=(blk_count // per_step,),
            in_specs=[
                pl.BlockSpec((rows, width), lambda i, *_: (i, 0)),
                pl.BlockSpec((per_step,) + weights.shape[1:], lambda i, *_: (i, 0, 0)),
            ]
            + [pl.BlockSpec(memory_space=pl.ANY)] * len(pieces),
            out_specs=pl.BlockSpec((rows, width), lambda i, *_: (i, 0)),
            scratch_shapes=[
                pltpu.VMEM((N_CORE * ((chips - 1) * slots + tiles) * tile_rows, width), BF16),
                pltpu.VMEM((rows, width), F32),
                pltpu.SemaphoreType.DMA((len(pieces),)),
            ],
        ),
        compiler_params=params(20),
        cost_estimate=cost(
            2 * blk_count * block_rows * width * list_len * tile_rows, latent, latent, interp
        ),
        name="back",
    )(table, in_hbm(latent), weights, *pieces)
    return (grid_out, mesh_out)


def solution(mesh):
    placed = (
        P(("groups", "band"), None),
        P(("groups", "band"), None),
        P(),
        P(),
        P(),
        P("band", None, None, None),
        P(),
        P(),
        P(),
        P(),
        P(),
    )
    n_y = max(1, 4 // mesh.shape["groups"])
    return jax.shard_map(
        functools.partial(on_device, n_y),
        mesh=mesh,
        in_specs=placed,
        out_specs=(P(("groups", "band"), None), P(("groups", "band"), None)),
        check_vma=False,
    )
```

```python
import functools

import jax
import jax.numpy as jnp
from jax import lax
from jax.experimental import pallas as pl
from jax.experimental.pallas import tpu as pltpu
from jax.sharding import PartitionSpec as P

F32 = jnp.float32
BF16 = jnp.bfloat16
N_CORE = 2
STRIP = 32
PART = 4


def silu(values):
    half = 0.5 * values
    return half * (1.0 + jnp.tanh(half))


def layer_norm(values, gain):
    centred = values - jnp.mean(values, axis=-1, keepdims=True)
    spread = jnp.mean(centred * centred, axis=-1, keepdims=True)
    return centred * lax.rsqrt(spread + 1e-05) * gain


def split(value, size):
    if size & (size - 1) == 0:
        return lax.shift_right_logical(value, size.bit_length() - 1), value & (size - 1)
    return lax.div(value, size), lax.rem(value, size)


class Ring:
    def __init__(self, n_band, n_y, tiles):
        self.n_band, self.n_y, self.tiles = n_band, n_y, tiles
        self.chips = n_band // N_CORE
        self.far = self.chips // 2

    def place(self, index):
        chip, core = split(index, N_CORE)
        z, y = split(chip, self.n_y)
        return z + y * (self.chips - 1 - 2 * z), core

    def index(self, ring, core):
        ring = ring % self.chips
        n_z = self.chips // self.n_y
        z, y = (ring, 0) if ring < n_z else (self.chips - 1 - ring, 1)
        return (z * self.n_y + y) * N_CORE + core

    def over_core(self, value):
        return lax.ppermute(value, "band", [(i, i ^ 1) for i in range(self.n_band)])

    def over(self, value, by, cross=0):
        pairs = []
        for i in range(self.n_band):
            chip, core = divmod(i, N_CORE)
            z, y = divmod(chip, self.n_y)
            ring = z if y == 0 else self.chips - 1 - z
            pairs.append((i, self.index(ring + (-by if core else by), core ^ cross)))
        return lax.ppermute(value, "band", pairs)

    def entry(self, lists_ref, me, block, k):
        owner, tile = split(lists_ref[k, block], self.tiles)
        ring, core = self.place(owner)
        my_ring, my_core = self.place(me)
        ahead = split(ring - my_ring + self.chips, self.chips)[1]
        left = (ahead > self.far).astype(jnp.int32)
        shared = (ahead == 0) | (ahead == self.far)
        handler = jnp.where(shared, core, left)
        distance = jnp.where(ahead > self.far, self.chips - ahead, ahead)
        group = jnp.maximum(2 * distance - 1 + (core ^ handler), 0)
        return handler ^ my_core, group, tile


def strips(rows):
    return [slice(r, r + STRIP) for r in range(rows.start, rows.stop, STRIP)]


def embed_kernel(
    ring, per_step, slots, me_ref, lists_ref, mask_ref,
    x_ref, w1_ref, w2_ref, gain_ref, interp_ref,
    latent_ref, kept_ref, far_ref, rest_ref, table_ref, wide, hidden,
):
    step = pl.program_id(0)
    me = me_ref[0]
    list_len, tile_rows, block_rows = interp_ref.shape[1:]
    blk_count = pl.num_programs(0) * per_step
    groups = ring.chips

    def spot(index, block, k):
        across, group, tile = ring.entry(lists_ref, index, index * blk_count + block, k)
        slot = split(block * list_len + k, ring.n_band)[0]
        return across, group, tile, slot

    part_rows = PART * block_rows
    spans = [slice(i * part_rows, (i + 1) * part_rows) for i in range(per_step // PART)]
    for rows in spans:
        wide[rows] = lax.dot_general(
            x_ref[:, rows], w1_ref[...], (((0,), (0,)), ((), ())), preferred_element_type=F32
        )
    for rows in spans:
        for strip in strips(rows):
            hidden[strip] = silu(wide[strip]).astype(BF16)
        wide[rows] = jnp.dot(hidden[rows], w2_ref[...], preferred_element_type=F32)
    kept_spare, far_spare, rest_spare = (ref.shape[0] - 1 for ref in (kept_ref, far_ref, rest_ref))
    for number, rows in enumerate(spans):
        for strip in strips(rows):
            latent_ref[strip] = layer_norm(wide[strip], gain_ref[...]).astype(BF16)
        for b in range(number * PART, (number + 1) * PART):
            block = step * per_step + b
            weights = interp_ref[b].reshape(list_len * tile_rows, block_rows)
            latent = latent_ref[b * block_rows : (b + 1) * block_rows]
            part = jnp.dot(weights, latent, preferred_element_type=F32)
            for k in range(list_len):
                across, group, tile, slot = spot(me, block, k)
                place = (across * groups + group) * slots + slot
                mask = mask_ref[k, me * blk_count + block]
                table_ref[0, place] = tile
                found = group * slots + jnp.where(group == groups - 1, tile, slot)
                table_ref[2, block * list_len + k] = found + across * (
                    (groups - 1) * slots + ring.tiles
                )
                table_ref[3, block * list_len + k] = mask
                across, group, tile, slot = spot(me ^ 1, block, k)
                table_ref[1, (across * groups + group) * slots + slot] = tile
                masked = part[k * tile_rows : (k + 1) * tile_rows] * mask.astype(F32)
                masked = masked.astype(BF16)
                kept_ref[jnp.minimum(place, kept_spare)] = masked
                there = place - kept_spare
                rest_ref[jnp.where(there < 0, rest_spare, jnp.minimum(there, rest_spare))] = masked
                beyond = there - rest_spare
                far_ref[jnp.where(beyond < 0, far_spare, beyond)] = masked


def add_entries(total, table_ref, group, slots, kept, other, groups, first=0):
    for slot in range(slots):
        place = group * slots + slot
        total[table_ref[0, place]] += kept[place].astype(F32)
        total[table_ref[1, groups * slots + place]] += other[place - first * slots].astype(F32)


def far_kernel(slots, groups, table_ref, kept, other, far, before, total):
    for group, out in ((groups - 1, far), (groups - 2, before)):
        total[...] = jnp.zeros_like(total)
        add_entries(total, table_ref, group, slots, kept, other, groups, groups - 2)
        out[...] = total[...].astype(BF16)


def own_kernel(slots, groups, table_ref, kept, other, own):
    group = pl.program_id(0)
    total = own.at[group]
    total[...] = jnp.zeros_like(total)
    add_entries(total, table_ref, group, slots, kept, other, groups)


def add_kernel(group, own, came, token, out):
    del token
    out[...] = (own[group] + came[...].astype(F32)).astype(BF16)


def mesh_kernel(
    latent_ref, up_ref, down_ref, gain_ref, own, came, neighbour, out_ref, piece_ref
):
    total = own[0] + came[...].astype(F32) + neighbour[...].astype(F32)
    mesh_in = latent_ref[...].astype(F32) + total.reshape(latent_ref.shape)
    normed = layer_norm(mesh_in, gain_ref[...]).astype(BF16)
    hidden = silu(jnp.dot(normed, up_ref[...], preferred_element_type=F32)).astype(BF16)
    out = (mesh_in + jnp.dot(hidden, down_ref[...], preferred_element_type=F32)).astype(BF16)
    out_ref[...] = out
    piece_ref[...] = out


def order_kernel(*refs):
    del refs


def pick_kernel(chosen, slots, groups, tile_rows, table_ref, *refs):
    pieces, outs = refs[:-2], refs[-2:]
    for number, group in enumerate(chosen):
        for slot in range(slots):
            for way, out in enumerate(outs):
                tile = table_ref[way, (way * groups + group) * slots + slot]
                rows = pl.ds(pl.multiple_of(tile * tile_rows, tile_rows), tile_rows)
                into = (number * slots + slot) * tile_rows
                out[into : into + tile_rows] = pieces[number][rows]


def turn_kernel(interp_ref, token, out_ref):
    del token
    for b in range(interp_ref.shape[0]):
        out_ref[b] = interp_ref[b].reshape(out_ref.shape[2], out_ref.shape[1]).T


def back_kernel(starts, list_len, per_step, table_ref, latent_ref, weights_ref, *rest):
    count = len(starts)
    pieces, (out_ref, held, total, sems) = rest[:count], rest[count:]
    step = pl.program_id(0)
    block_rows = weights_ref.shape[1]
    tile_rows = weights_ref.shape[2] // list_len

    @pl.when(step == 0)
    def _():
        copies = []
        for i, (piece, start) in enumerate(zip(pieces, starts)):
            into = held.at[pl.ds(start, piece.shape[0])]
            copies.append(pltpu.make_async_copy(piece, into, sems.at[i]))
        for copy in copies:
            copy.start()
        for copy in copies:
            copy.wait()

    for b in range(per_step):
        values = []
        for k in range(list_len):
            entry = (step * per_step + b) * list_len + k
            rows = pl.ds(pl.multiple_of(table_ref[2, entry] * tile_rows, tile_rows), tile_rows)
            value = held[rows]
            values.append(jnp.where(table_ref[3, entry] == 1, value, jnp.zeros_like(value)))
        value = jnp.concatenate(values, axis=0)
        rows = slice(b * block_rows, (b + 1) * block_rows)
        total[rows] = jnp.dot(weights_ref[b], value, preferred_element_type=F32)
        for strip in strips(rows):
            out_ref[strip] = (latent_ref[strip].astype(F32) + total[strip]).astype(BF16)


def whole(array):
    zeros = (0,) * array.ndim
    return pl.BlockSpec(array.shape, lambda *_: zeros)


def params(mib):
    return pltpu.CompilerParams(vmem_limit_bytes=mib * 1024 * 1024)


def cost(flops, *arrays):
    size = sum(a.size * a.dtype.itemsize for a in arrays)
    return pl.CostEstimate(flops=int(flops), bytes_accessed=int(size), transcendentals=0)


def shape(dims, kind=BF16):
    return jax.ShapeDtypeStruct(dims, kind)


def on_device(
    n_y,
    grid_features,
    mesh_latent,
    embed_in,
    embed_out,
    embed_gain,
    interp,
    block_mask,
    tile_list,
    mesh_up,
    mesh_down,
    mesh_gain,
):
    n_band = lax.axis_size("band")
    blk_count, list_len, tile_rows, block_rows = interp.shape
    channels, width = embed_in.shape
    node_rows = mesh_latent.shape[0]
    tiles = node_rows // tile_rows
    entries = blk_count * list_len
    slots = entries // n_band
    ring = Ring(n_band, n_y, tiles)
    chips, far = ring.chips, ring.far
    lists = (lax.axis_index("band").reshape(1), tile_list.T, block_mask.T)

    def in_hbm(array):
        return pltpu.with_memory_space_constraint(array, pltpu.HBM)

    gain = embed_gain.reshape(1, width)
    per_step = 8
    rows = per_step * block_rows
    counts = (chips * slots, 2 * slots, (chips - 2) * slots)
    latent, kept, sent_far, sent_rest, table = pl.pallas_call(
        functools.partial(embed_kernel, ring, per_step, slots),
        out_shape=[pltpu.HBM((blk_count * block_rows, width), BF16)]
        + [shape((count + 1, tile_rows, width)) for count in counts]
        + [shape((4, entries), jnp.int32)],
        grid_spec=pltpu.PrefetchScalarGridSpec(
            num_scalar_prefetch=3,
            grid=(blk_count // per_step,),
            in_specs=[
                pl.BlockSpec((channels, rows), lambda i, *_: (0, i)),
                whole(embed_in),
                whole(embed_out),
                whole(gain),
                pl.BlockSpec((per_step,) + interp.shape[1:], lambda i, *_: (i, 0, 0, 0)),
            ],
            out_specs=[pl.BlockSpec((rows, width), lambda i, *_: (i, 0))]
            + [pl.BlockSpec(memory_space=pltpu.VMEM)] * len(counts)
            + [pl.BlockSpec(memory_space=pltpu.SMEM)],
            scratch_shapes=[pltpu.VMEM((rows, width), F32), pltpu.VMEM((rows, width), BF16)],
        ),
        compiler_params=params(32),
        cost_estimate=cost(
            2 * blk_count * block_rows * width * (channels + width + list_len * tile_rows),
            grid_features,
            interp,
        ),
        name="embed",
    )(lists[0], *map(in_hbm, lists[1:] + (grid_features.T, embed_in, embed_out, gain, interp)))
    other_far = ring.over_core(sent_far)

    dense = (tiles, tile_rows, width)
    in_vmem = pl.BlockSpec(memory_space=pltpu.VMEM)
    in_any = pl.BlockSpec(memory_space=pl.ANY)
    def in_order(value, token):
        return pl.pallas_call(
            order_kernel,
            out_shape=shape(value.shape),
            in_specs=[in_any] * 2,
            out_specs=in_any,
            input_output_aliases={0: 0},
            compiler_params=params(1),
            cost_estimate=cost(0),
            name="in_order",
        )(value, token)

    first, second = pl.pallas_call(
        functools.partial(far_kernel, slots, chips),
        out_shape=[shape(dense)] * 2,
        grid_spec=pltpu.PrefetchScalarGridSpec(
            num_scalar_prefetch=1,
            grid=(1,),
            in_specs=[in_vmem] * 2,
            out_specs=[in_vmem] * 2,
            scratch_shapes=[pltpu.VMEM(dense, F32)],
        ),
        compiler_params=params(8),
        cost_estimate=cost(0, kept),
        name="far_sums",
    )(table, kept, other_far)
    other_rest = ring.over_core(in_order(sent_rest, first))
    own = pl.pallas_call(
        functools.partial(own_kernel, slots, chips),
        out_shape=shape((chips - 2,) + dense, F32),
        grid_spec=pltpu.PrefetchScalarGridSpec(
            num_scalar_prefetch=1,
            grid=(chips - 2,),
            in_specs=[in_vmem] * 2,
            out_specs=in_vmem,
        ),
        compiler_params=params(8 if n_band <= 16 else 24),
        cost_estimate=cost(0, kept, kept, kept, kept),
        name="own_sums",
    )(table, kept, other_rest)

    def add_own(group, value, token):
        return pl.pallas_call(
            functools.partial(add_kernel, group),
            out_shape=shape(dense),
            in_specs=[in_vmem] * 2 + [in_any],
            out_specs=in_vmem,
            compiler_params=params(8),
            cost_estimate=cost(0),
            name=f"add_{group}",
        )(own, value, token)

    first, second = ring.over(first, 1), ring.over(second, 1)
    turned = (blk_count, block_rows, list_len * tile_rows)
    per_step = 4
    token = weights = pl.pallas_call(
        turn_kernel,
        out_shape=shape(turned),
        grid=(blk_count // per_step,),
        in_specs=[pl.BlockSpec((per_step,) + interp.shape[1:], lambda i: (i, 0, 0, 0)), in_any],
        out_specs=pl.BlockSpec((per_step,) + turned[1:], lambda i: (i, 0, 0)),
        compiler_params=params(8),
        cost_estimate=cost(0, interp, interp),
        name="turn",
    )(interp, own)
    for group in range(chips - 3, 0, -1):
        if group % 2:
            token = add_own(group, first, token)
            first = ring.over(token, 1)
        else:
            token = add_own(group, second, token)
            second = ring.over(token, 1, int(group == 2))

    mesh_gain = mesh_gain.reshape(1, width)
    mesh_out, piece = pl.pallas_call(
        mesh_kernel,
        out_shape=[shape((node_rows, width))] * 2,
        in_specs=[in_vmem] * 7,
        out_specs=[in_vmem] * 2,
        compiler_params=params(16),
        cost_estimate=cost(4 * node_rows * width * width, mesh_up, mesh_down),
        name="mesh_step",
    )(mesh_latent, mesh_up, mesh_down, mesh_gain, own, first, second)

    pieces, starts = [], []

    def share(index, mine, theirs):
        for across, value in enumerate((mine, ring.over_core(theirs))):
            pieces.append(value)
            starts.append((across * ((chips - 1) * slots + tiles) + index) * tile_rows)

    def pick(chosen, values):
        out = shape((len(chosen) * slots * tile_rows, width))
        mine, theirs = pl.pallas_call(
            functools.partial(pick_kernel, chosen, slots, chips, tile_rows),
            out_shape=[out] * 2,
            grid_spec=pltpu.PrefetchScalarGridSpec(
                num_scalar_prefetch=1,
                grid=(1,),
                in_specs=[in_vmem] * len(values),
                out_specs=[in_vmem] * 2,
            ),
            compiler_params=params(8),
            cost_estimate=cost(0, *values),
            name=f"pick_{chosen[0]}",
        )(table, *values)
        share(chosen[0] * slots, mine, theirs)
        return mine

    first = ring.over(piece, -1)
    second = ring.over(piece, 1, 1)
    token = piece
    for distance in range(1, far):
        first = in_order(first, token)
        onward = ring.over(first, -1)
        second = in_order(second, first)
        if distance < far - 1:
            after = ring.over(second, -1)
        chosen, values = [2 * distance - 1, 2 * distance], [first, second]
        if distance == 1:
            chosen, values = [0] + chosen, [piece] + values
        token = pick(chosen, values)
        first, second = onward, after
    share((chips - 1) * slots, first, first)

    per_step = 4
    rows = per_step * block_rows
    grid_out = pl.pallas_call(
        functools.partial(back_kernel, starts, list_len, per_step),
        out_shape=shape((blk_count * block_rows, width)),
        grid_spec=pltpu.PrefetchScalarGridSpec(
            num_scalar_prefetch=1,
            grid=(blk_count // per_step,),
            in_specs=[
                pl.BlockSpec((rows, width), lambda i, *_: (i, 0)),
                pl.BlockSpec((per_step,) + weights.shape[1:], lambda i, *_: (i, 0, 0)),
            ]
            + [pl.BlockSpec(memory_space=pl.ANY)] * len(pieces),
            out_specs=pl.BlockSpec((rows, width), lambda i, *_: (i, 0)),
            scratch_shapes=[
                pltpu.VMEM((N_CORE * ((chips - 1) * slots + tiles) * tile_rows, width), BF16),
                pltpu.VMEM((rows, width), F32),
                pltpu.SemaphoreType.DMA((len(pieces),)),
            ],
        ),
        compiler_params=params(20),
        cost_estimate=cost(
            2 * blk_count * block_rows * width * list_len * tile_rows, latent, latent, interp
        ),
        name="back",
    )(table, in_hbm(latent), weights, *pieces)
    return (grid_out, mesh_out)


def solution(mesh):
    placed = (
        P(("groups", "band"), None),
        P(("groups", "band"), None),
        P(),
        P(),
        P(),
        P("band", None, None, None),
        P(),
        P(),
        P(),
        P(),
        P(),
    )
    n_y = max(1, 4 // mesh.shape["groups"])
    return jax.shard_map(
        functools.partial(on_device, n_y),
        mesh=mesh,
        in_specs=placed,
        out_specs=(P(("groups", "band"), None), P(("groups", "band"), None)),
        check_vma=False,
    )
```

```python
import functools

import jax
import jax.numpy as jnp
from jax import lax
from jax.experimental import pallas as pl
from jax.experimental.pallas import tpu as pltpu
from jax.sharding import PartitionSpec as P

F32 = jnp.float32
BF16 = jnp.bfloat16
N_CORE = 2
STRIP = 32
PART = 4


def silu(values):
    half = 0.5 * values
    return half * (1.0 + jnp.tanh(half))


def layer_norm(values, gain):
    centred = values - jnp.mean(values, axis=-1, keepdims=True)
    spread = jnp.mean(centred * centred, axis=-1, keepdims=True)
    return centred * lax.rsqrt(spread + 1e-05) * gain


def split(value, size):
    if size & (size - 1) == 0:
        return lax.shift_right_logical(value, size.bit_length() - 1), value & (size - 1)
    return lax.div(value, size), lax.rem(value, size)


class Ring:
    def __init__(self, n_band, n_y, tiles):
        self.n_band, self.n_y, self.tiles = n_band, n_y, tiles
        self.chips = n_band // N_CORE
        self.far = self.chips // 2

    def place(self, index):
        chip, core = split(index, N_CORE)
        z, y = split(chip, self.n_y)
        return z + y * (self.chips - 1 - 2 * z), core

    def index(self, ring, core):
        ring = ring % self.chips
        n_z = self.chips // self.n_y
        z, y = (ring, 0) if ring < n_z else (self.chips - 1 - ring, 1)
        return (z * self.n_y + y) * N_CORE + core

    def over_core(self, value):
        return lax.ppermute(value, "band", [(i, i ^ 1) for i in range(self.n_band)])

    def over(self, value, by, cross=0):
        pairs = []
        for i in range(self.n_band):
            chip, core = divmod(i, N_CORE)
            z, y = divmod(chip, self.n_y)
            ring = z if y == 0 else self.chips - 1 - z
            pairs.append((i, self.index(ring + (-by if core else by), core ^ cross)))
        return lax.ppermute(value, "band", pairs)

    def entry(self, lists_ref, me, block, k):
        owner, tile = split(lists_ref[k, block], self.tiles)
        ring, core = self.place(owner)
        my_ring, my_core = self.place(me)
        ahead = split(ring - my_ring + self.chips, self.chips)[1]
        left = (ahead > self.far).astype(jnp.int32)
        shared = (ahead == 0) | (ahead == self.far)
        handler = jnp.where(shared, core, left)
        distance = jnp.where(ahead > self.far, self.chips - ahead, ahead)
        group = jnp.maximum(2 * distance - 1 + (core ^ handler), 0)
        return handler ^ my_core, group, tile


def strips(rows):
    return [slice(r, r + STRIP) for r in range(rows.start, rows.stop, STRIP)]


def embed_kernel(
    ring, slots, me_ref, lists_ref, mask_ref, x_any, w1_any, w2_any, gain_ref, interp_any,
    latent_any, kept_ref, far_ref, rest_ref, table_ref,
    x_ref, w1_ref, w2_ref, interp_ref, wide, hidden, latent_ref, sems,
):
    me = me_ref[0]
    blk_count, list_len, tile_rows, block_rows = interp_ref.shape
    groups = ring.chips
    parts = x_ref.shape[0]
    part_rows = x_ref.shape[2]
    part_blocks = part_rows // block_rows
    spans = [slice(i * part_rows, (i + 1) * part_rows) for i in range(parts)]

    copies = []

    def copy(source, target):
        copies.append(pltpu.make_async_copy(source, target, sems.at[len(copies)]))
        return copies[-1]

    w1_in, w2_in = copy(w1_any, w1_ref), copy(w2_any, w2_ref)
    x_in = [copy(x_any.at[:, pl.ds(s.start, part_rows)], x_ref.at[i]) for i, s in enumerate(spans)]
    interp_in = []
    for i in range(parts):
        blocks = pl.ds(i * part_blocks, part_blocks)
        interp_in.append(copy(interp_any.at[blocks], interp_ref.at[blocks]))
    latent_out = []
    for s in spans:
        rows = pl.ds(s.start, part_rows)
        latent_out.append(copy(latent_ref.at[rows], latent_any.at[rows]))
    for started in (w1_in, x_in[0], w2_in, interp_in[0]):
        started.start()
    for i in range(1, parts):
        x_in[i].start()
        interp_in[i].start()

    def spot(index, block, k):
        across, group, tile = ring.entry(lists_ref, index, index * blk_count + block, k)
        return across, group, tile, (block * list_len + k) // ring.n_band

    kept_spare, far_spare, rest_spare = (ref.shape[0] - 1 for ref in (kept_ref, far_ref, rest_ref))

    def first_layer(i):
        x_in[i].wait()
        wide[spans[i]] = lax.dot_general(
            x_ref[i], w1_ref[...], (((0,), (0,)), ((), ())), preferred_element_type=F32
        )

    def second_layer(i):
        for strip in strips(spans[i]):
            hidden[strip] = silu(wide[strip]).astype(BF16)
        wide[spans[i]] = jnp.dot(hidden[spans[i]], w2_ref[...], preferred_element_type=F32)

    def listed_sums(i):
        for strip in strips(spans[i]):
            latent_ref[strip] = layer_norm(wide[strip], gain_ref[...]).astype(BF16)
        latent_out[i].start()
        interp_in[i].wait()
        for block in range(i * part_blocks, (i + 1) * part_blocks):
            weights = interp_ref[block].reshape(list_len * tile_rows, block_rows)
            latent = latent_ref[block * block_rows : (block + 1) * block_rows]
            part = jnp.dot(weights, latent, preferred_element_type=F32)
            for k in range(list_len):
                entry = block * list_len + k
                across, group, tile, slot = spot(me, block, k)
                place = (across * groups + group) * slots + slot
                mask = mask_ref[k, me * blk_count + block]
                table_ref[0, place] = tile
                found = group * slots + jnp.where(group == groups - 1, tile, slot)
                table_ref[2, entry] = found + across * ((groups - 1) * slots + ring.tiles)
                table_ref[3, entry] = mask
                across, group, tile, slot = spot(me ^ 1, block, k)
                table_ref[1, (across * groups + group) * slots + slot] = tile
                masked = part[k * tile_rows : (k + 1) * tile_rows] * mask.astype(F32)
                masked = masked.astype(BF16)
                kept_ref[jnp.minimum(place, kept_spare)] = masked
                there = place - kept_spare
                rest_ref[jnp.where(there < 0, rest_spare, jnp.minimum(there, rest_spare))] = masked
                beyond = there - rest_spare
                far_ref[jnp.where(beyond < 0, far_spare, beyond)] = masked

    w1_in.wait()
    first_layer(0)
    w2_in.wait()
    for i in range(parts):
        if i + 1 < parts:
            first_layer(i + 1)
        second_layer(i)
        if i:
            listed_sums(i - 1)
    listed_sums(parts - 1)
    for started in latent_out:
        started.wait()


def add_entries(total, table_ref, group, slots, kept, other, groups, first=0):
    for slot in range(slots):
        place = group * slots + slot
        total[table_ref[0, place]] += kept[place].astype(F32)
        total[table_ref[1, groups * slots + place]] += other[place - first * slots].astype(F32)


def far_kernel(slots, groups, table_ref, kept, other, far, before, total):
    for group, out in ((groups - 1, far), (groups - 2, before)):
        total[...] = jnp.zeros_like(total)
        add_entries(total, table_ref, group, slots, kept, other, groups, groups - 2)
        out[...] = total[...].astype(BF16)


def own_kernel(slots, groups, table_ref, kept, other, own):
    group = pl.program_id(0)
    total = own.at[group]
    total[...] = jnp.zeros_like(total)
    add_entries(total, table_ref, group, slots, kept, other, groups)


def add_kernel(group, own, came, token, out):
    del token
    out[...] = (own[group] + came[...].astype(F32)).astype(BF16)


def mesh_kernel(
    latent_ref, up_ref, down_ref, gain_ref, own, came, neighbour, out_ref, piece_ref
):
    total = own[0] + came[...].astype(F32) + neighbour[...].astype(F32)
    mesh_in = latent_ref[...].astype(F32) + total.reshape(latent_ref.shape)
    normed = layer_norm(mesh_in, gain_ref[...]).astype(BF16)
    hidden = silu(jnp.dot(normed, up_ref[...], preferred_element_type=F32)).astype(BF16)
    out = (mesh_in + jnp.dot(hidden, down_ref[...], preferred_element_type=F32)).astype(BF16)
    out_ref[...] = out
    piece_ref[...] = out


def order_kernel(*refs):
    del refs


def pick_kernel(chosen, slots, groups, tile_rows, table_ref, *refs):
    pieces, outs = refs[:-2], refs[-2:]
    for number, group in enumerate(chosen):
        for slot in range(slots):
            for way, out in enumerate(outs):
                tile = table_ref[way, (way * groups + group) * slots + slot]
                rows = pl.ds(pl.multiple_of(tile * tile_rows, tile_rows), tile_rows)
                into = (number * slots + slot) * tile_rows
                out[into : into + tile_rows] = pieces[number][rows]


def turn_kernel(interp_ref, token, out_ref):
    del token
    for b in range(interp_ref.shape[0]):
        out_ref[b] = interp_ref[b].reshape(out_ref.shape[2], out_ref.shape[1]).T


def back_kernel(starts, list_len, table_ref, weights_ref, latent_any, *rest):
    count = len(starts)
    pieces, (out_any, held, latent_ref, total, out_ref, sems) = rest[:count], rest[count:]
    blk_count, block_rows, listed = weights_ref.shape
    tile_rows = listed // list_len
    copies = []

    def copy(source, target):
        copies.append(pltpu.make_async_copy(source, target, sems.at[len(copies)]))
        return copies[-1]

    pieces_in = []
    for piece, start in zip(pieces, starts):
        pieces_in.append(copy(piece, held.at[pl.ds(start, piece.shape[0])]))
    part_rows = PART * block_rows
    parts = [pl.ds(i * part_rows, part_rows) for i in range(blk_count // PART)]
    latent_in = [copy(latent_any.at[rows], latent_ref.at[rows]) for rows in parts]
    outs = [copy(out_ref.at[rows], out_any.at[rows]) for rows in parts]
    for started in pieces_in + latent_in:
        started.start()
    for started in pieces_in:
        started.wait()

    for block in range(blk_count):
        values = []
        for k in range(list_len):
            entry = block * list_len + k
            rows = pl.ds(pl.multiple_of(table_ref[2, entry] * tile_rows, tile_rows), tile_rows)
            value = held[rows]
            values.append(jnp.where(table_ref[3, entry] == 1, value, jnp.zeros_like(value)))
        value = jnp.concatenate(values, axis=0)
        rows = slice(block * block_rows, (block + 1) * block_rows)
        total[rows] = jnp.dot(weights_ref[block], value, preferred_element_type=F32)
        if block % PART == 0:
            latent_in[block // PART].wait()
        for strip in strips(rows):
            out_ref[strip] = (latent_ref[strip].astype(F32) + total[strip]).astype(BF16)
        if block % PART == PART - 1:
            outs[block // PART].start()
    for started in outs:
        started.wait()


def whole(array):
    zeros = (0,) * array.ndim
    return pl.BlockSpec(array.shape, lambda *_: zeros)


def params(mib):
    return pltpu.CompilerParams(vmem_limit_bytes=mib * 1024 * 1024)


def cost(flops, *arrays):
    size = sum(a.size * a.dtype.itemsize for a in arrays)
    return pl.CostEstimate(flops=int(flops), bytes_accessed=int(size), transcendentals=0)


def shape(dims, kind=BF16):
    return jax.ShapeDtypeStruct(dims, kind)


def on_device(
    n_y,
    grid_features,
    mesh_latent,
    embed_in,
    embed_out,
    embed_gain,
    interp,
    block_mask,
    tile_list,
    mesh_up,
    mesh_down,
    mesh_gain,
):
    n_band = lax.axis_size("band")
    blk_count, list_len, tile_rows, block_rows = interp.shape
    channels, width = embed_in.shape
    node_rows = mesh_latent.shape[0]
    tiles = node_rows // tile_rows
    entries = blk_count * list_len
    slots = entries // n_band
    ring = Ring(n_band, n_y, tiles)
    chips, far = ring.chips, ring.far
    lists = (lax.axis_index("band").reshape(1), tile_list.T, block_mask.T)

    def in_hbm(array):
        return pltpu.with_memory_space_constraint(array, pltpu.HBM)

    gain = embed_gain.reshape(1, width)
    in_vmem = pl.BlockSpec(memory_space=pltpu.VMEM)
    in_any = pl.BlockSpec(memory_space=pl.ANY)
    grid_rows = blk_count * block_rows
    parts, part_rows = blk_count // PART, PART * block_rows
    counts = (chips * slots, 2 * slots, (chips - 2) * slots)
    latent, kept, sent_far, sent_rest, table = pl.pallas_call(
        functools.partial(embed_kernel, ring, slots),
        out_shape=[pltpu.HBM((grid_rows, width), BF16)]
        + [shape((count + 1, tile_rows, width)) for count in counts]
        + [shape((4, entries), jnp.int32)],
        grid_spec=pltpu.PrefetchScalarGridSpec(
            num_scalar_prefetch=3,
            grid=(1,),
            in_specs=[in_any] * 3 + [whole(gain), in_any],
            out_specs=[in_any]
            + [in_vmem] * len(counts)
            + [pl.BlockSpec(memory_space=pltpu.SMEM)],
            scratch_shapes=[
                pltpu.VMEM((parts, channels, part_rows), BF16),
                pltpu.VMEM(embed_in.shape, BF16),
                pltpu.VMEM(embed_out.shape, BF16),
                pltpu.VMEM(interp.shape, BF16),
                pltpu.VMEM((grid_rows, width), F32),
                pltpu.VMEM((grid_rows, width), BF16),
                pltpu.VMEM((grid_rows, width), BF16),
                pltpu.SemaphoreType.DMA((2 + 3 * parts,)),
            ],
        ),
        compiler_params=params(40),
        cost_estimate=cost(
            2 * grid_rows * width * (channels + width + list_len * tile_rows),
            grid_features,
            interp,
        ),
        name="embed",
    )(lists[0], *map(in_hbm, lists[1:] + (grid_features.T, embed_in, embed_out, gain, interp)))
    other_far = ring.over_core(sent_far)

    dense = (tiles, tile_rows, width)

    def in_order(value, token):
        return pl.pallas_call(
            order_kernel,
            out_shape=shape(value.shape),
            in_specs=[in_any] * 2,
            out_specs=in_any,
            input_output_aliases={0: 0},
            compiler_params=params(1),
            cost_estimate=cost(0),
            name="in_order",
        )(value, token)

    first, second = pl.pallas_call(
        functools.partial(far_kernel, slots, chips),
        out_shape=[shape(dense)] * 2,
        grid_spec=pltpu.PrefetchScalarGridSpec(
            num_scalar_prefetch=1,
            grid=(1,),
            in_specs=[in_vmem] * 2,
            out_specs=[in_vmem] * 2,
            scratch_shapes=[pltpu.VMEM(dense, F32)],
        ),
        compiler_params=params(8),
        cost_estimate=cost(0, kept),
        name="far_sums",
    )(table, kept, other_far)
    other_rest = ring.over_core(in_order(sent_rest, first))
    own = pl.pallas_call(
        functools.partial(own_kernel, slots, chips),
        out_shape=shape((chips - 2,) + dense, F32),
        grid_spec=pltpu.PrefetchScalarGridSpec(
            num_scalar_prefetch=1,
            grid=(chips - 2,),
            in_specs=[in_vmem] * 2,
            out_specs=in_vmem,
        ),
        compiler_params=params(8 if n_band <= 16 else 24),
        cost_estimate=cost(0, kept, kept, kept, kept),
        name="own_sums",
    )(table, kept, other_rest)

    def add_own(group, value, token):
        return pl.pallas_call(
            functools.partial(add_kernel, group),
            out_shape=shape(dense),
            in_specs=[in_vmem] * 2 + [in_any],
            out_specs=in_vmem,
            compiler_params=params(8),
            cost_estimate=cost(0),
            name=f"add_{group}",
        )(own, value, token)

    first, second = ring.over(first, 1), ring.over(second, 1)
    turned = (blk_count, block_rows, list_len * tile_rows)
    per_step = 4
    token = weights = pl.pallas_call(
        turn_kernel,
        out_shape=shape(turned),
        grid=(blk_count // per_step,),
        in_specs=[pl.BlockSpec((per_step,) + interp.shape[1:], lambda i: (i, 0, 0, 0)), in_any],
        out_specs=pl.BlockSpec((per_step,) + turned[1:], lambda i: (i, 0, 0)),
        compiler_params=params(8),
        cost_estimate=cost(0, interp, interp),
        name="turn",
    )(interp, own)
    for group in range(chips - 3, 0, -1):
        if group % 2:
            token = add_own(group, first, token)
            first = ring.over(token, 1)
        else:
            token = add_own(group, second, token)
            second = ring.over(token, 1, int(group == 2))

    mesh_gain = mesh_gain.reshape(1, width)
    mesh_out, piece = pl.pallas_call(
        mesh_kernel,
        out_shape=[shape((node_rows, width))] * 2,
        in_specs=[in_vmem] * 7,
        out_specs=[in_vmem] * 2,
        compiler_params=params(16),
        cost_estimate=cost(4 * node_rows * width * width, mesh_up, mesh_down),
        name="mesh_step",
    )(mesh_latent, mesh_up, mesh_down, mesh_gain, own, first, second)

    pieces, starts = [], []

    def share(index, mine, theirs):
        for across, value in enumerate((mine, ring.over_core(theirs))):
            pieces.append(value)
            starts.append((across * ((chips - 1) * slots + tiles) + index) * tile_rows)

    def pick(chosen, values):
        out = shape((len(chosen) * slots * tile_rows, width))
        mine, theirs = pl.pallas_call(
            functools.partial(pick_kernel, chosen, slots, chips, tile_rows),
            out_shape=[out] * 2,
            grid_spec=pltpu.PrefetchScalarGridSpec(
                num_scalar_prefetch=1,
                grid=(1,),
                in_specs=[in_vmem] * len(values),
                out_specs=[in_vmem] * 2,
            ),
            compiler_params=params(8),
            cost_estimate=cost(0, *values),
            name=f"pick_{chosen[0]}",
        )(table, *values)
        share(chosen[0] * slots, mine, theirs)
        return mine

    first = ring.over(piece, -1)
    second = ring.over(piece, 1, 1)
    token = piece
    for distance in range(1, far):
        first = in_order(first, token)
        onward = ring.over(first, -1)
        second = in_order(second, first)
        if distance < far - 1:
            after = ring.over(second, -1)
        chosen, values = [2 * distance - 1, 2 * distance], [first, second]
        if distance == 1:
            chosen, values = [0] + chosen, [piece] + values
        token = pick(chosen, values)
        first, second = onward, after
    share((chips - 1) * slots, first, first)

    grid_out = pl.pallas_call(
        functools.partial(back_kernel, starts, list_len),
        out_shape=shape((grid_rows, width)),
        grid_spec=pltpu.PrefetchScalarGridSpec(
            num_scalar_prefetch=1,
            grid=(1,),
            in_specs=[in_vmem] + [in_any] * (1 + len(pieces)),
            out_specs=in_any,
            scratch_shapes=[
                pltpu.VMEM((N_CORE * ((chips - 1) * slots + tiles) * tile_rows, width), BF16),
                pltpu.VMEM((grid_rows, width), BF16),
                pltpu.VMEM((grid_rows, width), F32),
                pltpu.VMEM((grid_rows, width), BF16),
                pltpu.SemaphoreType.DMA((len(pieces) + 2 * parts,)),
            ],
        ),
        compiler_params=params(32),
        cost_estimate=cost(2 * grid_rows * width * list_len * tile_rows, latent, latent, interp),
        name="back",
    )(table, weights, in_hbm(latent), *pieces)
    return (grid_out, mesh_out)


def solution(mesh):
    placed = (
        P(("groups", "band"), None),
        P(("groups", "band"), None),
        P(),
        P(),
        P(),
        P("band", None, None, None),
        P(),
        P(),
        P(),
        P(),
        P(),
    )
    n_y = max(1, 4 // mesh.shape["groups"])
    return jax.shard_map(
        functools.partial(on_device, n_y),
        mesh=mesh,
        in_specs=placed,
        out_specs=(P(("groups", "band"), None), P(("groups", "band"), None)),
        check_vma=False,
    )
```

```python
import functools

import jax
import jax.numpy as jnp
from jax import lax
from jax.experimental import pallas as pl
from jax.experimental.pallas import tpu as pltpu
from jax.sharding import PartitionSpec as P

F32 = jnp.float32
BF16 = jnp.bfloat16
N_CORE = 2
STRIP = 32
PART = 2
BACK_PART = 4


def silu(values):
    half = 0.5 * values
    return half * (1.0 + jnp.tanh(half))


def layer_norm(values, gain):
    centred = values - jnp.mean(values, axis=-1, keepdims=True)
    spread = jnp.mean(centred * centred, axis=-1, keepdims=True)
    return centred * lax.rsqrt(spread + 1e-05) * gain


def split(value, size):
    if size & (size - 1) == 0:
        return lax.shift_right_logical(value, size.bit_length() - 1), value & (size - 1)
    return lax.div(value, size), lax.rem(value, size)


class Ring:
    def __init__(self, n_band, n_y, tiles):
        self.n_band, self.n_y, self.tiles = n_band, n_y, tiles
        self.chips = n_band // N_CORE
        self.far = self.chips // 2

    def place(self, index):
        chip, core = split(index, N_CORE)
        z, y = split(chip, self.n_y)
        return z + y * (self.chips - 1 - 2 * z), core

    def index(self, ring, core):
        ring = ring % self.chips
        n_z = self.chips // self.n_y
        z, y = (ring, 0) if ring < n_z else (self.chips - 1 - ring, 1)
        return (z * self.n_y + y) * N_CORE + core

    def over_core(self, value):
        return lax.ppermute(value, "band", [(i, i ^ 1) for i in range(self.n_band)])

    def over(self, value, by, cross=0):
        pairs = []
        for i in range(self.n_band):
            chip, core = divmod(i, N_CORE)
            z, y = divmod(chip, self.n_y)
            ring = z if y == 0 else self.chips - 1 - z
            pairs.append((i, self.index(ring + (-by if core else by), core ^ cross)))
        return lax.ppermute(value, "band", pairs)

    def entry(self, lists_ref, me, block, k):
        owner, tile = split(lists_ref[k, block], self.tiles)
        ring, core = self.place(owner)
        my_ring, my_core = self.place(me)
        ahead = split(ring - my_ring + self.chips, self.chips)[1]
        left = (ahead > self.far).astype(jnp.int32)
        shared = (ahead == 0) | (ahead == self.far)
        handler = jnp.where(shared, core, left)
        distance = jnp.where(ahead > self.far, self.chips - ahead, ahead)
        group = jnp.maximum(2 * distance - 1 + (core ^ handler), 0)
        return handler ^ my_core, group, tile


def strips(rows):
    return [slice(r, r + STRIP) for r in range(rows.start, rows.stop, STRIP)]


def embed_kernel(
    ring, slots, me_ref, lists_ref, mask_ref, x_any, w1_any, w2_any, gain_ref, interp_any,
    latent_any, kept_ref, far_ref, rest_ref, table_ref,
    x_ref, w1_ref, w2_ref, interp_ref, wide, hidden, before, latent_ref, sems,
):
    me = me_ref[0]
    blk_count, list_len, tile_rows, block_rows = interp_ref.shape
    groups = ring.chips
    parts, _, part_rows = x_ref.shape
    part_blocks = part_rows // block_rows
    chunk = slice(0, part_rows)

    def rows_of(i):
        return pl.ds(pl.multiple_of(i * part_rows, part_rows), part_rows)

    def blocks_of(i):
        return pl.ds(i * part_blocks, part_blocks)

    w1_in = pltpu.make_async_copy(w1_any, w1_ref, sems.at[0])
    w2_in = pltpu.make_async_copy(w2_any, w2_ref, sems.at[1])

    def x_in(i):
        return pltpu.make_async_copy(x_any.at[:, rows_of(i)], x_ref.at[i], sems.at[2 + i])

    def interp_in(i):
        blocks = blocks_of(i)
        return pltpu.make_async_copy(
            interp_any.at[blocks], interp_ref.at[blocks], sems.at[2 + parts + i]
        )

    def latent_out(i):
        rows = rows_of(i)
        return pltpu.make_async_copy(
            latent_ref.at[rows], latent_any.at[rows], sems.at[2 + 2 * parts + i]
        )

    w1_in.start()
    x_in(0).start()
    w2_in.start()
    interp_in(0).start()
    for i in range(1, parts):
        x_in(i).start()
        interp_in(i).start()
    w1_in.wait()
    w2_in.wait()

    def spot(index, block, k):
        across, group, tile = ring.entry(lists_ref, index, index * blk_count + block, k)
        return across, group, tile, split(block * list_len + k, ring.n_band)[0]

    kept_spare, far_spare, rest_spare = (ref.shape[0] - 1 for ref in (kept_ref, far_ref, rest_ref))

    def one_chunk(i, carry):
        x_in(i).wait()
        wide[...] = lax.dot_general(
            x_ref[i], w1_ref[...], (((0,), (0,)), ((), ())), preferred_element_type=F32
        )
        for strip in strips(chunk):
            hidden[strip] = silu(wide[strip]).astype(BF16)
        before[...] = jnp.dot(hidden[...], w2_ref[...], preferred_element_type=F32)
        for strip in strips(chunk):
            rows = pl.ds(pl.multiple_of(i * part_rows + strip.start, STRIP), STRIP)
            latent_ref[rows] = layer_norm(before[strip], gain_ref[...]).astype(BF16)
        latent_out(i).start()
        interp_in(i).wait()
        for b in range(part_blocks):
            block = i * part_blocks + b
            weights = interp_ref[block].reshape(list_len * tile_rows, block_rows)
            rows = pl.ds(pl.multiple_of(block * block_rows, block_rows), block_rows)
            part = jnp.dot(weights, latent_ref[rows], preferred_element_type=F32)
            for k in range(list_len):
                entry = block * list_len + k
                across, group, tile, slot = spot(me, block, k)
                place = (across * groups + group) * slots + slot
                mask = mask_ref[k, me * blk_count + block]
                table_ref[0, place] = tile
                found = group * slots + jnp.where(group == groups - 1, tile, slot)
                table_ref[2, entry] = found + across * ((groups - 1) * slots + ring.tiles)
                table_ref[3, entry] = mask
                across, group, tile, slot = spot(me ^ 1, block, k)
                table_ref[1, (across * groups + group) * slots + slot] = tile
                masked = part[k * tile_rows : (k + 1) * tile_rows] * mask.astype(F32)
                masked = masked.astype(BF16)
                kept_ref[jnp.minimum(place, kept_spare)] = masked
                there = place - kept_spare
                rest_ref[jnp.where(there < 0, rest_spare, jnp.minimum(there, rest_spare))] = masked
                beyond = there - rest_spare
                far_ref[jnp.where(beyond < 0, far_spare, beyond)] = masked
        return carry

    lax.fori_loop(0, parts, one_chunk, 0)
    for i in range(parts):
        latent_out(i).wait()


def add_entries(total, table_ref, group, slots, kept, other, groups, first=0):
    for slot in range(slots):
        place = group * slots + slot
        total[table_ref[0, place]] += kept[place].astype(F32)
        total[table_ref[1, groups * slots + place]] += other[place - first * slots].astype(F32)


def far_kernel(slots, groups, table_ref, kept, other, far, before, total):
    for group, out in ((groups - 1, far), (groups - 2, before)):
        total[...] = jnp.zeros_like(total)
        add_entries(total, table_ref, group, slots, kept, other, groups, groups - 2)
        out[...] = total[...].astype(BF16)


def own_kernel(slots, groups, table_ref, kept, other, own):
    group = pl.program_id(0)
    total = own.at[group]
    total[...] = jnp.zeros_like(total)
    add_entries(total, table_ref, group, slots, kept, other, groups)


def add_kernel(group, own, came, token, out):
    del token
    out[...] = (own[group] + came[...].astype(F32)).astype(BF16)


def mesh_kernel(
    latent_ref, up_ref, down_ref, gain_ref, own, came, neighbour, out_ref, piece_ref
):
    total = own[0] + came[...].astype(F32) + neighbour[...].astype(F32)
    mesh_in = latent_ref[...].astype(F32) + total.reshape(latent_ref.shape)
    normed = layer_norm(mesh_in, gain_ref[...]).astype(BF16)
    hidden = silu(jnp.dot(normed, up_ref[...], preferred_element_type=F32)).astype(BF16)
    out = (mesh_in + jnp.dot(hidden, down_ref[...], preferred_element_type=F32)).astype(BF16)
    out_ref[...] = out
    piece_ref[...] = out


def order_kernel(*refs):
    del refs


def pick_kernel(chosen, slots, groups, tile_rows, table_ref, *refs):
    pieces, outs = refs[:-2], refs[-2:]
    for number, group in enumerate(chosen):
        for slot in range(slots):
            for way, out in enumerate(outs):
                tile = table_ref[way, (way * groups + group) * slots + slot]
                rows = pl.ds(pl.multiple_of(tile * tile_rows, tile_rows), tile_rows)
                into = (number * slots + slot) * tile_rows
                out[into : into + tile_rows] = pieces[number][rows]


def turn_kernel(interp_ref, token, out_ref):
    del token
    for b in range(interp_ref.shape[0]):
        out_ref[b] = interp_ref[b].reshape(out_ref.shape[2], out_ref.shape[1]).T


def back_kernel(starts, list_len, table_ref, weights_ref, latent_any, *rest):
    count = len(starts)
    pieces, (out_any, held, latent_ref, total, out_ref, sems) = rest[:count], rest[count:]
    blk_count, block_rows, listed = weights_ref.shape
    tile_rows = listed // list_len
    part_rows = total.shape[0]
    part_blocks = part_rows // block_rows
    parts = blk_count // part_blocks

    def rows_of(i):
        return pl.ds(pl.multiple_of(i * part_rows, part_rows), part_rows)

    def latent_in(i):
        rows = rows_of(i)
        return pltpu.make_async_copy(latent_any.at[rows], latent_ref.at[rows], sems.at[i])

    def out(i):
        rows = rows_of(i)
        return pltpu.make_async_copy(out_ref.at[rows], out_any.at[rows], sems.at[parts + i])

    pieces_in = []
    for i, (piece, start) in enumerate(zip(pieces, starts)):
        into = held.at[pl.ds(start, piece.shape[0])]
        pieces_in.append(pltpu.make_async_copy(piece, into, sems.at[2 * parts + i]))
    for copy in pieces_in:
        copy.start()
    for i in range(parts):
        latent_in(i).start()
    for copy in pieces_in:
        copy.wait()

    def one_chunk(i, carry):
        latent_in(i).wait()
        for b in range(part_blocks):
            block = i * part_blocks + b
            values = []
            for k in range(list_len):
                entry = block * list_len + k
                rows = pl.ds(pl.multiple_of(table_ref[2, entry] * tile_rows, tile_rows), tile_rows)
                value = held[rows]
                values.append(jnp.where(table_ref[3, entry] == 1, value, jnp.zeros_like(value)))
            value = jnp.concatenate(values, axis=0)
            span = slice(b * block_rows, (b + 1) * block_rows)
            total[span] = jnp.dot(weights_ref[block], value, preferred_element_type=F32)
            for strip in strips(span):
                rows = pl.ds(pl.multiple_of(i * part_rows + strip.start, STRIP), STRIP)
                out_ref[rows] = (latent_ref[rows].astype(F32) + total[strip]).astype(BF16)
        out(i).start()
        return carry

    lax.fori_loop(0, parts, one_chunk, 0)
    for i in range(parts):
        out(i).wait()


def whole(array):
    zeros = (0,) * array.ndim
    return pl.BlockSpec(array.shape, lambda *_: zeros)


def params(mib):
    return pltpu.CompilerParams(vmem_limit_bytes=mib * 1024 * 1024)


def cost(flops, *arrays):
    size = sum(a.size * a.dtype.itemsize for a in arrays)
    return pl.CostEstimate(flops=int(flops), bytes_accessed=int(size), transcendentals=0)


def shape(dims, kind=BF16):
    return jax.ShapeDtypeStruct(dims, kind)


def on_device(
    n_y,
    grid_features,
    mesh_latent,
    embed_in,
    embed_out,
    embed_gain,
    interp,
    block_mask,
    tile_list,
    mesh_up,
    mesh_down,
    mesh_gain,
):
    n_band = lax.axis_size("band")
    blk_count, list_len, tile_rows, block_rows = interp.shape
    channels, width = embed_in.shape
    node_rows = mesh_latent.shape[0]
    tiles = node_rows // tile_rows
    entries = blk_count * list_len
    slots = entries // n_band
    ring = Ring(n_band, n_y, tiles)
    chips, far = ring.chips, ring.far
    lists = (lax.axis_index("band").reshape(1), tile_list.T, block_mask.T)

    def in_hbm(array):
        return pltpu.with_memory_space_constraint(array, pltpu.HBM)

    gain = embed_gain.reshape(1, width)
    in_vmem = pl.BlockSpec(memory_space=pltpu.VMEM)
    in_any = pl.BlockSpec(memory_space=pl.ANY)
    grid_rows = blk_count * block_rows
    parts, part_rows = blk_count // PART, PART * block_rows
    counts = (chips * slots, 2 * slots, (chips - 2) * slots)
    latent, kept, sent_far, sent_rest, table = pl.pallas_call(
        functools.partial(embed_kernel, ring, slots),
        out_shape=[pltpu.HBM((grid_rows, width), BF16)]
        + [shape((count + 1, tile_rows, width)) for count in counts]
        + [shape((4, entries), jnp.int32)],
        grid_spec=pltpu.PrefetchScalarGridSpec(
            num_scalar_prefetch=3,
            grid=(1,),
            in_specs=[in_any] * 3 + [whole(gain), in_any],
            out_specs=[in_any]
            + [in_vmem] * len(counts)
            + [pl.BlockSpec(memory_space=pltpu.SMEM)],
            scratch_shapes=[
                pltpu.VMEM((parts, channels, part_rows), BF16),
                pltpu.VMEM(embed_in.shape, BF16),
                pltpu.VMEM(embed_out.shape, BF16),
                pltpu.VMEM(interp.shape, BF16),
                pltpu.VMEM((part_rows, width), F32),
                pltpu.VMEM((part_rows, width), BF16),
                pltpu.VMEM((part_rows, width), F32),
                pltpu.VMEM((grid_rows, width), BF16),
                pltpu.SemaphoreType.DMA((2 + 3 * parts,)),
            ],
        ),
        compiler_params=params(40),
        cost_estimate=cost(
            2 * grid_rows * width * (channels + width + list_len * tile_rows),
            grid_features,
            interp,
        ),
        name="embed",
    )(lists[0], *map(in_hbm, lists[1:] + (grid_features.T, embed_in, embed_out, gain, interp)))
    other_far = ring.over_core(sent_far)

    dense = (tiles, tile_rows, width)

    def in_order(value, token):
        return pl.pallas_call(
            order_kernel,
            out_shape=shape(value.shape),
            in_specs=[in_any] * 2,
            out_specs=in_any,
            input_output_aliases={0: 0},
            compiler_params=params(1),
            cost_estimate=cost(0),
            name="in_order",
        )(value, token)

    first, second = pl.pallas_call(
        functools.partial(far_kernel, slots, chips),
        out_shape=[shape(dense)] * 2,
        grid_spec=pltpu.PrefetchScalarGridSpec(
            num_scalar_prefetch=1,
            grid=(1,),
            in_specs=[in_vmem] * 2,
            out_specs=[in_vmem] * 2,
            scratch_shapes=[pltpu.VMEM(dense, F32)],
        ),
        compiler_params=params(8),
        cost_estimate=cost(0, kept),
        name="far_sums",
    )(table, kept, other_far)
    other_rest = ring.over_core(in_order(sent_rest, first))
    own = pl.pallas_call(
        functools.partial(own_kernel, slots, chips),
        out_shape=shape((chips - 2,) + dense, F32),
        grid_spec=pltpu.PrefetchScalarGridSpec(
            num_scalar_prefetch=1,
            grid=(chips - 2,),
            in_specs=[in_vmem] * 2,
            out_specs=in_vmem,
        ),
        compiler_params=params(8 if n_band <= 16 else 24),
        cost_estimate=cost(0, kept, kept, kept, kept),
        name="own_sums",
    )(table, kept, other_rest)

    def add_own(group, value, token):
        return pl.pallas_call(
            functools.partial(add_kernel, group),
            out_shape=shape(dense),
            in_specs=[in_vmem] * 2 + [in_any],
            out_specs=in_vmem,
            compiler_params=params(8),
            cost_estimate=cost(0),
            name=f"add_{group}",
        )(own, value, token)

    first, second = ring.over(first, 1), ring.over(second, 1)
    turned = (blk_count, block_rows, list_len * tile_rows)
    per_step = 4
    token = weights = pl.pallas_call(
        turn_kernel,
        out_shape=shape(turned),
        grid=(blk_count // per_step,),
        in_specs=[pl.BlockSpec((per_step,) + interp.shape[1:], lambda i: (i, 0, 0, 0)), in_any],
        out_specs=pl.BlockSpec((per_step,) + turned[1:], lambda i: (i, 0, 0)),
        compiler_params=params(8),
        cost_estimate=cost(0, interp, interp),
        name="turn",
    )(interp, own)
    for group in range(chips - 3, 0, -1):
        if group % 2:
            token = add_own(group, first, token)
            first = ring.over(token, 1)
        else:
            token = add_own(group, second, token)
            second = ring.over(token, 1, int(group == 2))

    mesh_gain = mesh_gain.reshape(1, width)
    mesh_out, piece = pl.pallas_call(
        mesh_kernel,
        out_shape=[shape((node_rows, width))] * 2,
        in_specs=[in_vmem] * 7,
        out_specs=[in_vmem] * 2,
        compiler_params=params(16),
        cost_estimate=cost(4 * node_rows * width * width, mesh_up, mesh_down),
        name="mesh_step",
    )(mesh_latent, mesh_up, mesh_down, mesh_gain, own, first, second)

    pieces, starts = [], []

    def share(index, mine, theirs):
        for across, value in enumerate((mine, ring.over_core(theirs))):
            pieces.append(value)
            starts.append((across * ((chips - 1) * slots + tiles) + index) * tile_rows)

    def pick(chosen, values):
        out = shape((len(chosen) * slots * tile_rows, width))
        mine, theirs = pl.pallas_call(
            functools.partial(pick_kernel, chosen, slots, chips, tile_rows),
            out_shape=[out] * 2,
            grid_spec=pltpu.PrefetchScalarGridSpec(
                num_scalar_prefetch=1,
                grid=(1,),
                in_specs=[in_vmem] * len(values),
                out_specs=[in_vmem] * 2,
            ),
            compiler_params=params(8),
            cost_estimate=cost(0, *values),
            name=f"pick_{chosen[0]}",
        )(table, *values)
        share(chosen[0] * slots, mine, theirs)
        return mine

    first = ring.over(piece, -1)
    second = ring.over(piece, 1, 1)
    token = piece
    for distance in range(1, far):
        first = in_order(first, token)
        onward = ring.over(first, -1)
        second = in_order(second, first)
        if distance < far - 1:
            after = ring.over(second, -1)
        chosen, values = [2 * distance - 1, 2 * distance], [first, second]
        if distance == 1:
            chosen, values = [0] + chosen, [piece] + values
        token = pick(chosen, values)
        first, second = onward, after
    share((chips - 1) * slots, first, first)

    grid_out = pl.pallas_call(
        functools.partial(back_kernel, starts, list_len),
        out_shape=shape((grid_rows, width)),
        grid_spec=pltpu.PrefetchScalarGridSpec(
            num_scalar_prefetch=1,
            grid=(1,),
            in_specs=[in_vmem] + [in_any] * (1 + len(pieces)),
            out_specs=in_any,
            scratch_shapes=[
                pltpu.VMEM((N_CORE * ((chips - 1) * slots + tiles) * tile_rows, width), BF16),
                pltpu.VMEM((grid_rows, width), BF16),
                pltpu.VMEM((BACK_PART * block_rows, width), F32),
                pltpu.VMEM((grid_rows, width), BF16),
                pltpu.SemaphoreType.DMA((len(pieces) + 2 * (blk_count // BACK_PART),)),
            ],
        ),
        compiler_params=params(32),
        cost_estimate=cost(2 * grid_rows * width * list_len * tile_rows, latent, latent, interp),
        name="back",
    )(table, weights, in_hbm(latent), *pieces)
    return (grid_out, mesh_out)


def solution(mesh):
    placed = (
        P(("groups", "band"), None),
        P(("groups", "band"), None),
        P(),
        P(),
        P(),
        P("band", None, None, None),
        P(),
        P(),
        P(),
        P(),
        P(),
    )
    n_y = max(1, 4 // mesh.shape["groups"])
    return jax.shard_map(
        functools.partial(on_device, n_y),
        mesh=mesh,
        in_specs=placed,
        out_specs=(P(("groups", "band"), None), P(("groups", "band"), None)),
        check_vma=False,
    )
```

```python
import functools

import jax
import jax.numpy as jnp
from jax import lax
from jax.experimental import pallas as pl
from jax.experimental.pallas import tpu as pltpu
from jax.sharding import PartitionSpec as P

F32 = jnp.float32
BF16 = jnp.bfloat16
N_CORE = 2
STRIP = 32
PART = 4


def silu(values):
    half = 0.5 * values
    return half * (1.0 + jnp.tanh(half))


def layer_norm(values, gain):
    centred = values - jnp.mean(values, axis=-1, keepdims=True)
    spread = jnp.mean(centred * centred, axis=-1, keepdims=True)
    return centred * lax.rsqrt(spread + 1e-05) * gain


def split(value, size):
    if size & (size - 1) == 0:
        return lax.shift_right_logical(value, size.bit_length() - 1), value & (size - 1)
    return lax.div(value, size), lax.rem(value, size)


class Ring:
    def __init__(self, n_band, n_y, tiles):
        self.n_band, self.n_y, self.tiles = n_band, n_y, tiles
        self.chips = n_band // N_CORE
        self.far = self.chips // 2

    def place(self, index):
        chip, core = split(index, N_CORE)
        z, y = split(chip, self.n_y)
        return z + y * (self.chips - 1 - 2 * z), core

    def index(self, ring, core):
        ring = ring % self.chips
        n_z = self.chips // self.n_y
        z, y = (ring, 0) if ring < n_z else (self.chips - 1 - ring, 1)
        return (z * self.n_y + y) * N_CORE + core

    def over_core(self, value):
        return lax.ppermute(value, "band", [(i, i ^ 1) for i in range(self.n_band)])

    def over(self, value, by, cross=0):
        pairs = []
        for i in range(self.n_band):
            chip, core = divmod(i, N_CORE)
            z, y = divmod(chip, self.n_y)
            ring = z if y == 0 else self.chips - 1 - z
            pairs.append((i, self.index(ring + (-by if core else by), core ^ cross)))
        return lax.ppermute(value, "band", pairs)

    def entry(self, lists_ref, me, block, k):
        owner, tile = split(lists_ref[k, block], self.tiles)
        ring, core = self.place(owner)
        my_ring, my_core = self.place(me)
        ahead = split(ring - my_ring + self.chips, self.chips)[1]
        left = (ahead > self.far).astype(jnp.int32)
        shared = (ahead == 0) | (ahead == self.far)
        handler = jnp.where(shared, core, left)
        distance = jnp.where(ahead > self.far, self.chips - ahead, ahead)
        group = jnp.maximum(2 * distance - 1 + (core ^ handler), 0)
        return handler ^ my_core, group, tile


def strips(rows):
    return [slice(r, r + STRIP) for r in range(rows.start, rows.stop, STRIP)]


def embed_kernel(
    ring, slots, me_ref, lists_ref, mask_ref, x_ref, w1_ref, w2_ref, gain_ref, interp_ref,
    latent_any, kept_ref, far_ref, rest_ref, table_ref, wide, hidden, latent_ref, sems,
):
    step, steps = pl.program_id(0), pl.num_programs(0)
    me = me_ref[0]
    part_blocks, list_len, tile_rows, block_rows = interp_ref.shape
    blk_count = steps * part_blocks
    groups = ring.chips
    part_rows = wide.shape[0]
    chunk = slice(0, part_rows)

    def latent_out(i):
        rows = pl.ds(pl.multiple_of(i * part_rows, part_rows), part_rows)
        return pltpu.make_async_copy(latent_ref.at[rows], latent_any.at[rows], sems.at[i])

    def spot(index, block, k):
        across, group, tile = ring.entry(lists_ref, index, index * blk_count + block, k)
        return across, group, tile, split(block * list_len + k, ring.n_band)[0]

    wide[...] = lax.dot_general(
        x_ref[...], w1_ref[...], (((0,), (0,)), ((), ())), preferred_element_type=F32
    )
    for strip in strips(chunk):
        hidden[strip] = silu(wide[strip]).astype(BF16)
    wide[...] = jnp.dot(hidden[...], w2_ref[...], preferred_element_type=F32)
    for strip in strips(chunk):
        rows = pl.ds(pl.multiple_of(step * part_rows + strip.start, STRIP), STRIP)
        latent_ref[rows] = layer_norm(wide[strip], gain_ref[...]).astype(BF16)
    latent_out(step).start()

    kept_spare, far_spare, rest_spare = (ref.shape[0] - 1 for ref in (kept_ref, far_ref, rest_ref))
    for b in range(part_blocks):
        block = step * part_blocks + b
        weights = interp_ref[b].reshape(list_len * tile_rows, block_rows)
        rows = pl.ds(pl.multiple_of(block * block_rows, block_rows), block_rows)
        part = jnp.dot(weights, latent_ref[rows], preferred_element_type=F32)
        for k in range(list_len):
            entry = block * list_len + k
            across, group, tile, slot = spot(me, block, k)
            place = (across * groups + group) * slots + slot
            mask = mask_ref[k, me * blk_count + block]
            table_ref[0, place] = tile
            found = group * slots + jnp.where(group == groups - 1, tile, slot)
            table_ref[2, entry] = found + across * ((groups - 1) * slots + ring.tiles)
            table_ref[3, entry] = mask
            across, group, tile, slot = spot(me ^ 1, block, k)
            table_ref[1, (across * groups + group) * slots + slot] = tile
            masked = part[k * tile_rows : (k + 1) * tile_rows] * mask.astype(F32)
            masked = masked.astype(BF16)
            kept_ref[jnp.minimum(place, kept_spare)] = masked
            there = place - kept_spare
            rest_ref[jnp.where(there < 0, rest_spare, jnp.minimum(there, rest_spare))] = masked
            beyond = there - rest_spare
            far_ref[jnp.where(beyond < 0, far_spare, beyond)] = masked

    @pl.when(step == steps - 1)
    def _():
        for i in range(sems.shape[0]):
            latent_out(i).wait()


def add_entries(total, table_ref, group, slots, kept, other, groups, first=0):
    for slot in range(slots):
        place = group * slots + slot
        total[table_ref[0, place]] += kept[place].astype(F32)
        total[table_ref[1, groups * slots + place]] += other[place - first * slots].astype(F32)


def far_kernel(slots, groups, table_ref, kept, other, far, before, total):
    for group, out in ((groups - 1, far), (groups - 2, before)):
        total[...] = jnp.zeros_like(total)
        add_entries(total, table_ref, group, slots, kept, other, groups, groups - 2)
        out[...] = total[...].astype(BF16)


def own_kernel(slots, groups, table_ref, kept, other, own):
    group = pl.program_id(0)
    total = own.at[group]
    total[...] = jnp.zeros_like(total)
    add_entries(total, table_ref, group, slots, kept, other, groups)


def add_kernel(group, own, came, token, out):
    del token
    out[...] = (own[group] + came[...].astype(F32)).astype(BF16)


def mesh_kernel(
    latent_ref, up_ref, down_ref, gain_ref, own, came, neighbour, out_ref, piece_ref
):
    total = own[0] + came[...].astype(F32) + neighbour[...].astype(F32)
    mesh_in = latent_ref[...].astype(F32) + total.reshape(latent_ref.shape)
    normed = layer_norm(mesh_in, gain_ref[...]).astype(BF16)
    hidden = silu(jnp.dot(normed, up_ref[...], preferred_element_type=F32)).astype(BF16)
    out = (mesh_in + jnp.dot(hidden, down_ref[...], preferred_element_type=F32)).astype(BF16)
    out_ref[...] = out
    piece_ref[...] = out


def order_kernel(*refs):
    del refs


def pick_kernel(chosen, slots, groups, tile_rows, table_ref, *refs):
    pieces, outs = refs[:-2], refs[-2:]
    for number, group in enumerate(chosen):
        for slot in range(slots):
            for way, out in enumerate(outs):
                tile = table_ref[way, (way * groups + group) * slots + slot]
                rows = pl.ds(pl.multiple_of(tile * tile_rows, tile_rows), tile_rows)
                into = (number * slots + slot) * tile_rows
                out[into : into + tile_rows] = pieces[number][rows]


def turn_kernel(interp_ref, token, out_ref):
    del token
    for b in range(interp_ref.shape[0]):
        out_ref[b] = interp_ref[b].reshape(out_ref.shape[2], out_ref.shape[1]).T


def back_kernel(starts, list_len, table_ref, weights_ref, latent_any, *rest):
    count = len(starts)
    pieces, (out_any, held, latent_ref, total, out_ref, sems) = rest[:count], rest[count:]
    blk_count, block_rows, listed = weights_ref.shape
    tile_rows = listed // list_len
    copies = []

    def copy(source, target):
        copies.append(pltpu.make_async_copy(source, target, sems.at[len(copies)]))
        return copies[-1]

    pieces_in = []
    for piece, start in zip(pieces, starts):
        pieces_in.append(copy(piece, held.at[pl.ds(start, piece.shape[0])]))
    part_rows = PART * block_rows
    parts = [pl.ds(i * part_rows, part_rows) for i in range(blk_count // PART)]
    latent_in = [copy(latent_any.at[rows], latent_ref.at[rows]) for rows in parts]
    outs = [copy(out_ref.at[rows], out_any.at[rows]) for rows in parts]
    for started in pieces_in + latent_in:
        started.start()
    for started in pieces_in:
        started.wait()

    for block in range(blk_count):
        values = []
        for k in range(list_len):
            entry = block * list_len + k
            rows = pl.ds(pl.multiple_of(table_ref[2, entry] * tile_rows, tile_rows), tile_rows)
            value = held[rows]
            values.append(jnp.where(table_ref[3, entry] == 1, value, jnp.zeros_like(value)))
        value = jnp.concatenate(values, axis=0)
        rows = slice(block * block_rows, (block + 1) * block_rows)
        total[rows] = jnp.dot(weights_ref[block], value, preferred_element_type=F32)
        if block % PART == 0:
            latent_in[block // PART].wait()
        for strip in strips(rows):
            out_ref[strip] = (latent_ref[strip].astype(F32) + total[strip]).astype(BF16)
        if block % PART == PART - 1:
            outs[block // PART].start()
    for started in outs:
        started.wait()


def whole(array):
    zeros = (0,) * array.ndim
    return pl.BlockSpec(array.shape, lambda *_: zeros)


def params(mib):
    return pltpu.CompilerParams(vmem_limit_bytes=mib * 1024 * 1024)


def cost(flops, *arrays):
    size = sum(a.size * a.dtype.itemsize for a in arrays)
    return pl.CostEstimate(flops=int(flops), bytes_accessed=int(size), transcendentals=0)


def shape(dims, kind=BF16):
    return jax.ShapeDtypeStruct(dims, kind)


def on_device(
    n_y,
    grid_features,
    mesh_latent,
    embed_in,
    embed_out,
    embed_gain,
    interp,
    block_mask,
    tile_list,
    mesh_up,
    mesh_down,
    mesh_gain,
):
    n_band = lax.axis_size("band")
    blk_count, list_len, tile_rows, block_rows = interp.shape
    channels, width = embed_in.shape
    node_rows = mesh_latent.shape[0]
    tiles = node_rows // tile_rows
    entries = blk_count * list_len
    slots = entries // n_band
    ring = Ring(n_band, n_y, tiles)
    chips, far = ring.chips, ring.far
    lists = (lax.axis_index("band").reshape(1), tile_list.T, block_mask.T)

    def in_hbm(array):
        return pltpu.with_memory_space_constraint(array, pltpu.HBM)

    gain = embed_gain.reshape(1, width)
    in_vmem = pl.BlockSpec(memory_space=pltpu.VMEM)
    in_any = pl.BlockSpec(memory_space=pl.ANY)
    grid_rows = blk_count * block_rows
    parts, part_rows = blk_count // PART, PART * block_rows
    counts = (chips * slots, 2 * slots, (chips - 2) * slots)
    latent, kept, sent_far, sent_rest, table = pl.pallas_call(
        functools.partial(embed_kernel, ring, slots),
        out_shape=[pltpu.HBM((grid_rows, width), BF16)]
        + [shape((count + 1, tile_rows, width)) for count in counts]
        + [shape((4, entries), jnp.int32)],
        grid_spec=pltpu.PrefetchScalarGridSpec(
            num_scalar_prefetch=3,
            grid=(parts,),
            in_specs=[
                pl.BlockSpec((channels, part_rows), lambda i, *_: (0, i)),
                whole(embed_in),
                whole(embed_out),
                whole(gain),
                pl.BlockSpec((PART,) + interp.shape[1:], lambda i, *_: (i, 0, 0, 0)),
            ],
            out_specs=[in_any]
            + [in_vmem] * len(counts)
            + [pl.BlockSpec(memory_space=pltpu.SMEM)],
            scratch_shapes=[
                pltpu.VMEM((part_rows, width), F32),
                pltpu.VMEM((part_rows, width), BF16),
                pltpu.VMEM((grid_rows, width), BF16),
                pltpu.SemaphoreType.DMA((parts,)),
            ],
        ),
        compiler_params=params(40),
        cost_estimate=cost(
            2 * grid_rows * width * (channels + width + list_len * tile_rows),
            grid_features,
            interp,
        ),
        name="embed",
    )(lists[0], *map(in_hbm, lists[1:] + (grid_features.T, embed_in, embed_out, gain, interp)))
    other_far = ring.over_core(sent_far)

    dense = (tiles, tile_rows, width)

    def in_order(value, token):
        return pl.pallas_call(
            order_kernel,
            out_shape=shape(value.shape),
            in_specs=[in_any] * 2,
            out_specs=in_any,
            input_output_aliases={0: 0},
            compiler_params=params(1),
            cost_estimate=cost(0),
            name="in_order",
        )(value, token)

    first, second = pl.pallas_call(
        functools.partial(far_kernel, slots, chips),
        out_shape=[shape(dense)] * 2,
        grid_spec=pltpu.PrefetchScalarGridSpec(
            num_scalar_prefetch=1,
            grid=(1,),
            in_specs=[in_vmem] * 2,
            out_specs=[in_vmem] * 2,
            scratch_shapes=[pltpu.VMEM(dense, F32)],
        ),
        compiler_params=params(8),
        cost_estimate=cost(0, kept),
        name="far_sums",
    )(table, kept, other_far)
    other_rest = ring.over_core(in_order(sent_rest, first))
    own = pl.pallas_call(
        functools.partial(own_kernel, slots, chips),
        out_shape=shape((chips - 2,) + dense, F32),
        grid_spec=pltpu.PrefetchScalarGridSpec(
            num_scalar_prefetch=1,
            grid=(chips - 2,),
            in_specs=[in_vmem] * 2,
            out_specs=in_vmem,
        ),
        compiler_params=params(8 if n_band <= 16 else 24),
        cost_estimate=cost(0, kept, kept, kept, kept),
        name="own_sums",
    )(table, kept, other_rest)

    def add_own(group, value, token):
        return pl.pallas_call(
            functools.partial(add_kernel, group),
            out_shape=shape(dense),
            in_specs=[in_vmem] * 2 + [in_any],
            out_specs=in_vmem,
            compiler_params=params(8),
            cost_estimate=cost(0),
            name=f"add_{group}",
        )(own, value, token)

    first, second = ring.over(first, 1), ring.over(second, 1)
    turned = (blk_count, block_rows, list_len * tile_rows)
    per_step = 4
    token = weights = pl.pallas_call(
        turn_kernel,
        out_shape=shape(turned),
        grid=(blk_count // per_step,),
        in_specs=[pl.BlockSpec((per_step,) + interp.shape[1:], lambda i: (i, 0, 0, 0)), in_any],
        out_specs=pl.BlockSpec((per_step,) + turned[1:], lambda i: (i, 0, 0)),
        compiler_params=params(8),
        cost_estimate=cost(0, interp, interp),
        name="turn",
    )(interp, own)
    for group in range(chips - 3, 0, -1):
        if group % 2:
            token = add_own(group, first, token)
            first = ring.over(token, 1)
        else:
            token = add_own(group, second, token)
            second = ring.over(token, 1, int(group == 2))

    mesh_gain = mesh_gain.reshape(1, width)
    mesh_out, piece = pl.pallas_call(
        mesh_kernel,
        out_shape=[shape((node_rows, width))] * 2,
        in_specs=[in_vmem] * 7,
        out_specs=[in_vmem] * 2,
        compiler_params=params(16),
        cost_estimate=cost(4 * node_rows * width * width, mesh_up, mesh_down),
        name="mesh_step",
    )(mesh_latent, mesh_up, mesh_down, mesh_gain, own, first, second)

    pieces, starts = [], []

    def share(index, mine, theirs):
        for across, value in enumerate((mine, ring.over_core(theirs))):
            pieces.append(value)
            starts.append((across * ((chips - 1) * slots + tiles) + index) * tile_rows)

    def pick(chosen, values):
        out = shape((len(chosen) * slots * tile_rows, width))
        mine, theirs = pl.pallas_call(
            functools.partial(pick_kernel, chosen, slots, chips, tile_rows),
            out_shape=[out] * 2,
            grid_spec=pltpu.PrefetchScalarGridSpec(
                num_scalar_prefetch=1,
                grid=(1,),
                in_specs=[in_vmem] * len(values),
                out_specs=[in_vmem] * 2,
            ),
            compiler_params=params(8),
            cost_estimate=cost(0, *values),
            name=f"pick_{chosen[0]}",
        )(table, *values)
        share(chosen[0] * slots, mine, theirs)
        return mine

    first = ring.over(piece, -1)
    second = ring.over(piece, 1, 1)
    token = piece
    for distance in range(1, far):
        first = in_order(first, token)
        onward = ring.over(first, -1)
        second = in_order(second, first)
        if distance < far - 1:
            after = ring.over(second, -1)
        chosen, values = [2 * distance - 1, 2 * distance], [first, second]
        if distance == 1:
            chosen, values = [0] + chosen, [piece] + values
        token = pick(chosen, values)
        first, second = onward, after
    share((chips - 1) * slots, first, first)

    grid_out = pl.pallas_call(
        functools.partial(back_kernel, starts, list_len),
        out_shape=shape((grid_rows, width)),
        grid_spec=pltpu.PrefetchScalarGridSpec(
            num_scalar_prefetch=1,
            grid=(1,),
            in_specs=[in_vmem] + [in_any] * (1 + len(pieces)),
            out_specs=in_any,
            scratch_shapes=[
                pltpu.VMEM((N_CORE * ((chips - 1) * slots + tiles) * tile_rows, width), BF16),
                pltpu.VMEM((grid_rows, width), BF16),
                pltpu.VMEM((grid_rows, width), F32),
                pltpu.VMEM((grid_rows, width), BF16),
                pltpu.SemaphoreType.DMA((len(pieces) + 2 * parts,)),
            ],
        ),
        compiler_params=params(32),
        cost_estimate=cost(2 * grid_rows * width * list_len * tile_rows, latent, latent, interp),
        name="back",
    )(table, weights, in_hbm(latent), *pieces)
    return (grid_out, mesh_out)


def solution(mesh):
    placed = (
        P(("groups", "band"), None),
        P(("groups", "band"), None),
        P(),
        P(),
        P(),
        P("band", None, None, None),
        P(),
        P(),
        P(),
        P(),
        P(),
    )
    n_y = max(1, 4 // mesh.shape["groups"])
    return jax.shard_map(
        functools.partial(on_device, n_y),
        mesh=mesh,
        in_specs=placed,
        out_specs=(P(("groups", "band"), None), P(("groups", "band"), None)),
        check_vma=False,
    )
```

```python
import functools

import jax
import jax.numpy as jnp
from jax import lax
from jax.experimental import pallas as pl
from jax.experimental.pallas import tpu as pltpu
from jax.sharding import PartitionSpec as P

F32 = jnp.float32
BF16 = jnp.bfloat16
N_CORE = 2
STRIP = 32
PART = 2
BACK_PART = 4


def silu(values):
    half = 0.5 * values
    return half * (1.0 + jnp.tanh(half))


def layer_norm(values, gain):
    centred = values - jnp.mean(values, axis=-1, keepdims=True)
    spread = jnp.mean(centred * centred, axis=-1, keepdims=True)
    return centred * lax.rsqrt(spread + 1e-05) * gain


def split(value, size):
    if size & (size - 1) == 0:
        return lax.shift_right_logical(value, size.bit_length() - 1), value & (size - 1)
    return lax.div(value, size), lax.rem(value, size)


class Ring:
    def __init__(self, n_band, n_y, tiles):
        self.n_band, self.n_y, self.tiles = n_band, n_y, tiles
        self.chips = n_band // N_CORE
        self.far = self.chips // 2

    def place(self, index):
        chip, core = split(index, N_CORE)
        z, y = split(chip, self.n_y)
        return z + y * (self.chips - 1 - 2 * z), core

    def index(self, ring, core):
        ring = ring % self.chips
        n_z = self.chips // self.n_y
        z, y = (ring, 0) if ring < n_z else (self.chips - 1 - ring, 1)
        return (z * self.n_y + y) * N_CORE + core

    def over_core(self, value):
        return lax.ppermute(value, "band", [(i, i ^ 1) for i in range(self.n_band)])

    def over(self, value, right):
        pairs = []
        for i in range(self.n_band):
            chip, core = divmod(i, N_CORE)
            z, y = divmod(chip, self.n_y)
            ring = z if y == 0 else self.chips - 1 - z
            pairs.append((i, self.index(ring + (1 if core == right else -1), 1 - core)))
        return lax.ppermute(value, "band", pairs)

    def over_first(self, value, distance):
        return self.over(value, distance % 2)

    def over_second(self, value, distance):
        return self.over(value, (distance + 1) % 2)

    def entry(self, lists_ref, me, block, k):
        owner, tile = split(lists_ref[k, block], self.tiles)
        ring, core = self.place(owner)
        my_ring, my_core = self.place(me)
        ahead = split(ring - my_ring + self.chips, self.chips)[1]
        left = (ahead > self.far).astype(jnp.int32)
        distance = jnp.where(ahead > self.far, self.chips - ahead, ahead)
        shared = (ahead == 0) | (ahead == self.far)
        stream = jnp.where(shared, 0, core ^ left)
        group = jnp.maximum(2 * distance - 1 + stream, 0)
        return ((distance + core) & 1) ^ my_core, group, tile


def strips(rows):
    return [slice(r, r + STRIP) for r in range(rows.start, rows.stop, STRIP)]


def embed_kernel(
    ring, per_step, slots, me_ref, lists_ref, mask_ref,
    x_ref, w1_ref, w2_ref, gain_ref, interp_ref,
    latent_ref, kept_ref, far_ref, rest_ref, table_ref, wide, hidden,
):
    step = pl.program_id(0)
    me = me_ref[0]
    list_len, tile_rows, block_rows = interp_ref.shape[1:]
    blk_count = pl.num_programs(0) * per_step
    groups = ring.chips

    def spot(index, block, k):
        across, group, tile = ring.entry(lists_ref, index, index * blk_count + block, k)
        slot = split(block * list_len + k, ring.n_band)[0]
        return across, group, tile, slot

    part_rows = PART * block_rows
    spans = [slice(i * part_rows, (i + 1) * part_rows) for i in range(per_step // PART)]
    for rows in spans:
        wide[rows] = lax.dot_general(
            x_ref[:, rows], w1_ref[...], (((0,), (0,)), ((), ())), preferred_element_type=F32
        )
    for rows in spans:
        for strip in strips(rows):
            hidden[strip] = silu(wide[strip]).astype(BF16)
        wide[rows] = jnp.dot(hidden[rows], w2_ref[...], preferred_element_type=F32)
    kept_spare, far_spare, rest_spare = (ref.shape[0] - 1 for ref in (kept_ref, far_ref, rest_ref))
    for number, rows in enumerate(spans):
        for strip in strips(rows):
            latent_ref[strip] = layer_norm(wide[strip], gain_ref[...]).astype(BF16)
        for b in range(number * PART, (number + 1) * PART):
            block = step * per_step + b
            weights = interp_ref[b].reshape(list_len * tile_rows, block_rows)
            latent = latent_ref[b * block_rows : (b + 1) * block_rows]
            part = jnp.dot(weights, latent, preferred_element_type=F32)
            for k in range(list_len):
                across, group, tile, slot = spot(me, block, k)
                place = (across * groups + group) * slots + slot
                mask = mask_ref[k, me * blk_count + block]
                table_ref[0, place] = tile
                found = group * slots + jnp.where(group == groups - 1, tile, slot)
                table_ref[2, block * list_len + k] = found + across * (
                    (groups - 1) * slots + ring.tiles
                )
                table_ref[3, block * list_len + k] = mask
                across, group, tile, slot = spot(me ^ 1, block, k)
                table_ref[1, (across * groups + group) * slots + slot] = tile
                masked = part[k * tile_rows : (k + 1) * tile_rows] * mask.astype(F32)
                masked = masked.astype(BF16)
                kept_ref[jnp.minimum(place, kept_spare)] = masked
                there = place - kept_spare
                rest_ref[jnp.where(there < 0, rest_spare, jnp.minimum(there, rest_spare))] = masked
                beyond = there - rest_spare
                far_ref[jnp.where(beyond < 0, far_spare, beyond)] = masked


def add_entries(total, table_ref, group, slots, kept, other, groups, first=0):
    for slot in range(slots):
        place = group * slots + slot
        total[table_ref[0, place]] += kept[place].astype(F32)
        total[table_ref[1, groups * slots + place]] += other[place - first * slots].astype(F32)


def far_kernel(slots, groups, table_ref, kept, other, far, before, total):
    for group, out in ((groups - 1, far), (groups - 2, before)):
        total[...] = jnp.zeros_like(total)
        add_entries(total, table_ref, group, slots, kept, other, groups, groups - 2)
        out[...] = total[...].astype(BF16)


def own_kernel(slots, groups, table_ref, kept, other, own):
    group = pl.program_id(0)
    total = own.at[group]
    total[...] = jnp.zeros_like(total)
    add_entries(total, table_ref, group, slots, kept, other, groups)


def add_kernel(group, own, came, token, out):
    del token
    out[...] = (own[group] + came[...].astype(F32)).astype(BF16)


def mesh_kernel(
    latent_ref, up_ref, down_ref, gain_ref, own, came, neighbour, out_ref, piece_ref
):
    total = own[0] + came[...].astype(F32) + neighbour[...].astype(F32)
    mesh_in = latent_ref[...].astype(F32) + total.reshape(latent_ref.shape)
    normed = layer_norm(mesh_in, gain_ref[...]).astype(BF16)
    hidden = silu(jnp.dot(normed, up_ref[...], preferred_element_type=F32)).astype(BF16)
    out = (mesh_in + jnp.dot(hidden, down_ref[...], preferred_element_type=F32)).astype(BF16)
    out_ref[...] = out
    piece_ref[...] = out


def order_kernel(*refs):
    del refs


def pick_kernel(chosen, slots, groups, tile_rows, table_ref, *refs):
    pieces, outs = refs[:-2], refs[-2:]
    for number, group in enumerate(chosen):
        for slot in range(slots):
            for way, out in enumerate(outs):
                tile = table_ref[way, (way * groups + group) * slots + slot]
                rows = pl.ds(pl.multiple_of(tile * tile_rows, tile_rows), tile_rows)
                into = (number * slots + slot) * tile_rows
                out[into : into + tile_rows] = pieces[number][rows]


def turn_kernel(interp_ref, token, out_ref):
    del token
    for b in range(interp_ref.shape[0]):
        out_ref[b] = interp_ref[b].reshape(out_ref.shape[2], out_ref.shape[1]).T


def back_kernel(starts, list_len, table_ref, weights_ref, latent_any, *rest):
    count = len(starts)
    pieces, (out_any, held, latent_ref, total, out_ref, sems) = rest[:count], rest[count:]
    blk_count, block_rows, listed = weights_ref.shape
    tile_rows = listed // list_len
    copies = []

    def copy(source, target):
        copies.append(pltpu.make_async_copy(source, target, sems.at[len(copies)]))
        return copies[-1]

    pieces_in = []
    for piece, start in zip(pieces, starts):
        pieces_in.append(copy(piece, held.at[pl.ds(start, piece.shape[0])]))
    part_rows = BACK_PART * block_rows
    parts = [pl.ds(i * part_rows, part_rows) for i in range(blk_count // BACK_PART)]
    latent_in = [copy(latent_any.at[rows], latent_ref.at[rows]) for rows in parts]
    outs = [copy(out_ref.at[rows], out_any.at[rows]) for rows in parts]
    for started in pieces_in + latent_in:
        started.start()
    for started in pieces_in:
        started.wait()

    for block in range(blk_count):
        values = []
        for k in range(list_len):
            entry = block * list_len + k
            rows = pl.ds(pl.multiple_of(table_ref[2, entry] * tile_rows, tile_rows), tile_rows)
            value = held[rows]
            values.append(jnp.where(table_ref[3, entry] == 1, value, jnp.zeros_like(value)))
        value = jnp.concatenate(values, axis=0)
        rows = slice(block * block_rows, (block + 1) * block_rows)
        total[rows] = jnp.dot(weights_ref[block], value, preferred_element_type=F32)
        if block % BACK_PART == 0:
            latent_in[block // BACK_PART].wait()
        for strip in strips(rows):
            out_ref[strip] = (latent_ref[strip].astype(F32) + total[strip]).astype(BF16)
        if block % BACK_PART == BACK_PART - 1:
            outs[block // BACK_PART].start()
    for started in outs:
        started.wait()


def whole(array):
    zeros = (0,) * array.ndim
    return pl.BlockSpec(array.shape, lambda *_: zeros)


def params(mib):
    return pltpu.CompilerParams(vmem_limit_bytes=mib * 1024 * 1024)


def cost(flops, *arrays):
    size = sum(a.size * a.dtype.itemsize for a in arrays)
    return pl.CostEstimate(flops=int(flops), bytes_accessed=int(size), transcendentals=0)


def shape(dims, kind=BF16):
    return jax.ShapeDtypeStruct(dims, kind)


def on_device(
    n_y,
    grid_features,
    mesh_latent,
    embed_in,
    embed_out,
    embed_gain,
    interp,
    block_mask,
    tile_list,
    mesh_up,
    mesh_down,
    mesh_gain,
):
    n_band = lax.axis_size("band")
    blk_count, list_len, tile_rows, block_rows = interp.shape
    channels, width = embed_in.shape
    node_rows = mesh_latent.shape[0]
    tiles = node_rows // tile_rows
    entries = blk_count * list_len
    slots = entries // n_band
    ring = Ring(n_band, n_y, tiles)
    chips, far = ring.chips, ring.far
    lists = (lax.axis_index("band").reshape(1), tile_list.T, block_mask.T)

    def in_hbm(array):
        return pltpu.with_memory_space_constraint(array, pltpu.HBM)

    gain = embed_gain.reshape(1, width)
    in_vmem = pl.BlockSpec(memory_space=pltpu.VMEM)
    in_any = pl.BlockSpec(memory_space=pl.ANY)
    grid_rows = blk_count * block_rows
    per_step = 4
    rows = per_step * block_rows
    counts = (chips * slots, 2 * slots, (chips - 2) * slots)
    latent, kept, sent_far, sent_rest, table = pl.pallas_call(
        functools.partial(embed_kernel, ring, per_step, slots),
        out_shape=[pltpu.HBM((blk_count * block_rows, width), BF16)]
        + [shape((count + 1, tile_rows, width)) for count in counts]
        + [shape((4, entries), jnp.int32)],
        grid_spec=pltpu.PrefetchScalarGridSpec(
            num_scalar_prefetch=3,
            grid=(blk_count // per_step,),
            in_specs=[
                pl.BlockSpec((channels, rows), lambda i, *_: (0, i)),
                whole(embed_in),
                whole(embed_out),
                whole(gain),
                pl.BlockSpec((per_step,) + interp.shape[1:], lambda i, *_: (i, 0, 0, 0)),
            ],
            out_specs=[pl.BlockSpec((rows, width), lambda i, *_: (i, 0))]
            + [pl.BlockSpec(memory_space=pltpu.VMEM)] * len(counts)
            + [pl.BlockSpec(memory_space=pltpu.SMEM)],
            scratch_shapes=[pltpu.VMEM((rows, width), F32), pltpu.VMEM((rows, width), BF16)],
        ),
        compiler_params=params(24),
        cost_estimate=cost(
            2 * blk_count * block_rows * width * (channels + width + list_len * tile_rows),
            grid_features,
            interp,
        ),
        name="embed",
    )(lists[0], *map(in_hbm, lists[1:] + (grid_features.T, embed_in, embed_out, gain, interp)))
    other_far = ring.over_core(sent_far)

    dense = (tiles, tile_rows, width)

    def in_order(value, token):
        return pl.pallas_call(
            order_kernel,
            out_shape=shape(value.shape),
            in_specs=[in_any] * 2,
            out_specs=in_any,
            input_output_aliases={0: 0},
            compiler_params=params(1),
            cost_estimate=cost(0),
            name="in_order",
        )(value, token)

    first, second = pl.pallas_call(
        functools.partial(far_kernel, slots, chips),
        out_shape=[shape(dense)] * 2,
        grid_spec=pltpu.PrefetchScalarGridSpec(
            num_scalar_prefetch=1,
            grid=(1,),
            in_specs=[in_vmem] * 2,
            out_specs=[in_vmem] * 2,
            scratch_shapes=[pltpu.VMEM(dense, F32)],
        ),
        compiler_params=params(8),
        cost_estimate=cost(0, kept),
        name="far_sums",
    )(table, kept, other_far)
    other_rest = ring.over_core(in_order(sent_rest, first))
    own = pl.pallas_call(
        functools.partial(own_kernel, slots, chips),
        out_shape=shape((chips - 2,) + dense, F32),
        grid_spec=pltpu.PrefetchScalarGridSpec(
            num_scalar_prefetch=1,
            grid=(chips - 2,),
            in_specs=[in_vmem] * 2,
            out_specs=in_vmem,
        ),
        compiler_params=params(8 if n_band <= 16 else 24),
        cost_estimate=cost(0, kept, kept, kept, kept),
        name="own_sums",
    )(table, kept, other_rest)

    def add_own(group, value, token):
        return pl.pallas_call(
            functools.partial(add_kernel, group),
            out_shape=shape(dense),
            in_specs=[in_vmem] * 2 + [in_any],
            out_specs=in_vmem,
            compiler_params=params(8),
            cost_estimate=cost(0),
            name=f"add_{group}",
        )(own, value, token)

    first, second = ring.over_first(first, far), ring.over_second(second, far - 1)
    turned = (blk_count, block_rows, list_len * tile_rows)
    per_step = 4
    token = weights = pl.pallas_call(
        turn_kernel,
        out_shape=shape(turned),
        grid=(blk_count // per_step,),
        in_specs=[pl.BlockSpec((per_step,) + interp.shape[1:], lambda i: (i, 0, 0, 0)), in_any],
        out_specs=pl.BlockSpec((per_step,) + turned[1:], lambda i: (i, 0, 0)),
        compiler_params=params(8),
        cost_estimate=cost(0, interp, interp),
        name="turn",
    )(interp, own)
    for group in range(chips - 3, 0, -1):
        distance = (group + 1) // 2
        if group % 2:
            token = add_own(group, first, token)
            first = ring.over_first(token, distance)
        else:
            token = add_own(group, second, token)
            second = ring.over_second(token, distance)

    mesh_gain = mesh_gain.reshape(1, width)
    mesh_out, piece = pl.pallas_call(
        mesh_kernel,
        out_shape=[shape((node_rows, width))] * 2,
        in_specs=[in_vmem] * 7,
        out_specs=[in_vmem] * 2,
        compiler_params=params(16),
        cost_estimate=cost(4 * node_rows * width * width, mesh_up, mesh_down),
        name="mesh_step",
    )(mesh_latent, mesh_up, mesh_down, mesh_gain, own, first, second)

    pieces, starts = [], []

    def share(index, mine, theirs):
        for across, value in enumerate((mine, ring.over_core(theirs))):
            pieces.append(value)
            starts.append((across * ((chips - 1) * slots + tiles) + index) * tile_rows)

    def pick(chosen, values):
        out = shape((len(chosen) * slots * tile_rows, width))
        mine, theirs = pl.pallas_call(
            functools.partial(pick_kernel, chosen, slots, chips, tile_rows),
            out_shape=[out] * 2,
            grid_spec=pltpu.PrefetchScalarGridSpec(
                num_scalar_prefetch=1,
                grid=(1,),
                in_specs=[in_vmem] * len(values),
                out_specs=[in_vmem] * 2,
            ),
            compiler_params=params(8),
            cost_estimate=cost(0, *values),
            name=f"pick_{chosen[0]}",
        )(table, *values)
        share(chosen[0] * slots, mine, theirs)
        return mine

    first, second = ring.over_first(piece, 1), ring.over_second(piece, 1)
    token = piece
    for distance in range(1, far):
        first = in_order(first, token)
        onward = ring.over_first(first, distance + 1)
        second = in_order(second, first)
        if distance < far - 1:
            after = ring.over_second(second, distance + 1)
        chosen, values = [2 * distance - 1, 2 * distance], [first, second]
        if distance == 1:
            chosen, values = [0] + chosen, [piece] + values
        token = pick(chosen, values)
        first, second = onward, after
    share((chips - 1) * slots, first, first)

    grid_out = pl.pallas_call(
        functools.partial(back_kernel, starts, list_len),
        out_shape=shape((grid_rows, width)),
        grid_spec=pltpu.PrefetchScalarGridSpec(
            num_scalar_prefetch=1,
            grid=(1,),
            in_specs=[in_vmem] + [in_any] * (1 + len(pieces)),
            out_specs=in_any,
            scratch_shapes=[
                pltpu.VMEM((N_CORE * ((chips - 1) * slots + tiles) * tile_rows, width), BF16),
                pltpu.VMEM((grid_rows, width), BF16),
                pltpu.VMEM((grid_rows, width), F32),
                pltpu.VMEM((grid_rows, width), BF16),
                pltpu.SemaphoreType.DMA((len(pieces) + 2 * (blk_count // BACK_PART),)),
            ],
        ),
        compiler_params=params(32),
        cost_estimate=cost(2 * grid_rows * width * list_len * tile_rows, latent, latent, interp),
        name="back",
    )(table, weights, in_hbm(latent), *pieces)
    return (grid_out, mesh_out)


def solution(mesh):
    placed = (
        P(("groups", "band"), None),
        P(("groups", "band"), None),
        P(),
        P(),
        P(),
        P("band", None, None, None),
        P(),
        P(),
        P(),
        P(),
        P(),
    )
    n_y = max(1, 4 // mesh.shape["groups"])
    return jax.shard_map(
        functools.partial(on_device, n_y),
        mesh=mesh,
        in_specs=placed,
        out_specs=(P(("groups", "band"), None), P(("groups", "band"), None)),
        check_vma=False,
    )
```

```python
import functools

import jax
import jax.numpy as jnp
from jax import lax
from jax.experimental import pallas as pl
from jax.experimental.pallas import tpu as pltpu
from jax.sharding import PartitionSpec as P

F32 = jnp.float32
BF16 = jnp.bfloat16
N_CORE = 2
STRIP = 32
PART = 2
BACK_PART = 4


def silu(values):
    half = 0.5 * values
    return half * (1.0 + jnp.tanh(half))


def layer_norm(values, gain):
    centred = values - jnp.mean(values, axis=-1, keepdims=True)
    spread = jnp.mean(centred * centred, axis=-1, keepdims=True)
    return centred * lax.rsqrt(spread + 1e-05) * gain


def split(value, size):
    if size & (size - 1) == 0:
        return lax.shift_right_logical(value, size.bit_length() - 1), value & (size - 1)
    return lax.div(value, size), lax.rem(value, size)


class Ring:
    def __init__(self, n_band, n_y, tiles):
        self.n_band, self.n_y, self.tiles = n_band, n_y, tiles
        self.chips = n_band // N_CORE
        self.far = self.chips // 2

    def place(self, index):
        chip, core = split(index, N_CORE)
        z, y = split(chip, self.n_y)
        return z + y * (self.chips - 1 - 2 * z), core

    def index(self, ring, core):
        ring = ring % self.chips
        n_z = self.chips // self.n_y
        z, y = (ring, 0) if ring < n_z else (self.chips - 1 - ring, 1)
        return (z * self.n_y + y) * N_CORE + core

    def over_core(self, value):
        return lax.ppermute(value, "band", [(i, i ^ 1) for i in range(self.n_band)])

    def over(self, value, right):
        pairs = []
        for i in range(self.n_band):
            chip, core = divmod(i, N_CORE)
            z, y = divmod(chip, self.n_y)
            ring = z if y == 0 else self.chips - 1 - z
            pairs.append((i, self.index(ring + (1 if core == right else -1), 1 - core)))
        return lax.ppermute(value, "band", pairs)

    def over_first(self, value, distance):
        return self.over(value, distance % 2)

    def over_second(self, value, distance):
        return self.over(value, (distance + 1) % 2)

    def entry(self, lists_ref, me, block, k):
        owner, tile = split(lists_ref[k, block], self.tiles)
        ring, core = self.place(owner)
        my_ring, my_core = self.place(me)
        ahead = split(ring - my_ring + self.chips, self.chips)[1]
        left = (ahead > self.far).astype(jnp.int32)
        distance = jnp.where(ahead > self.far, self.chips - ahead, ahead)
        shared = (ahead == 0) | (ahead == self.far)
        stream = jnp.where(shared, 0, core ^ left)
        group = jnp.maximum(2 * distance - 1 + stream, 0)
        return ((distance + core) & 1) ^ my_core, group, tile


def strips(rows):
    return [slice(r, r + STRIP) for r in range(rows.start, rows.stop, STRIP)]


def embed_kernel(
    ring, per_step, slots, me_ref, lists_ref, mask_ref,
    x_ref, w1_ref, w2_ref, gain_ref, interp_ref,
    latent_ref, kept_ref, far_ref, rest_ref, table_ref, wide, hidden,
):
    step = pl.program_id(0)
    me = me_ref[0]
    list_len, tile_rows, block_rows = interp_ref.shape[1:]
    blk_count = pl.num_programs(0) * per_step
    groups = ring.chips

    def spot(index, block, k):
        across, group, tile = ring.entry(lists_ref, index, index * blk_count + block, k)
        slot = split(block * list_len + k, ring.n_band)[0]
        return across, group, tile, slot

    part_rows = PART * block_rows
    spans = [slice(i * part_rows, (i + 1) * part_rows) for i in range(per_step // PART)]
    for rows in spans:
        wide[rows] = lax.dot_general(
            x_ref[:, rows], w1_ref[...], (((0,), (0,)), ((), ())), preferred_element_type=F32
        )
    for rows in spans:
        for strip in strips(rows):
            hidden[strip] = silu(wide[strip]).astype(BF16)
        wide[rows] = jnp.dot(hidden[rows], w2_ref[...], preferred_element_type=F32)
    kept_spare, far_spare, rest_spare = (ref.shape[0] - 1 for ref in (kept_ref, far_ref, rest_ref))
    for number, rows in enumerate(spans):
        for strip in strips(rows):
            latent_ref[strip] = layer_norm(wide[strip], gain_ref[...]).astype(BF16)
        for b in range(number * PART, (number + 1) * PART):
            block = step * per_step + b
            weights = interp_ref[b].reshape(list_len * tile_rows, block_rows)
            latent = latent_ref[b * block_rows : (b + 1) * block_rows]
            part = jnp.dot(weights, latent, preferred_element_type=F32)
            for k in range(list_len):
                across, group, tile, slot = spot(me, block, k)
                place = (across * groups + group) * slots + slot
                mask = mask_ref[k, me * blk_count + block]
                table_ref[0, place] = tile
                beyond = group == groups - 1
                near = (across * (groups - 1) + group) * slots + slot
                table_ref[2, block * list_len + k] = jnp.where(beyond, tile, near)
                table_ref[3, block * list_len + k] = mask * jnp.where(beyond, 2 + across, 1)
                across, group, tile, slot = spot(me ^ 1, block, k)
                table_ref[1, (across * groups + group) * slots + slot] = tile
                masked = part[k * tile_rows : (k + 1) * tile_rows] * mask.astype(F32)
                masked = masked.astype(BF16)
                kept_ref[jnp.minimum(place, kept_spare)] = masked
                there = place - kept_spare
                rest_ref[jnp.where(there < 0, rest_spare, jnp.minimum(there, rest_spare))] = masked
                beyond = there - rest_spare
                far_ref[jnp.where(beyond < 0, far_spare, beyond)] = masked


def add_entries(total, table_ref, group, slots, kept, other, groups, first=0):
    for slot in range(slots):
        place = group * slots + slot
        total[table_ref[0, place]] += kept[place].astype(F32)
        total[table_ref[1, groups * slots + place]] += other[place - first * slots].astype(F32)


def far_kernel(slots, groups, table_ref, kept, other, far, before, total):
    for group, out in ((groups - 1, far), (groups - 2, before)):
        total[...] = jnp.zeros_like(total)
        add_entries(total, table_ref, group, slots, kept, other, groups, groups - 2)
        out[...] = total[...].astype(BF16)


def own_kernel(slots, groups, table_ref, kept, other, own):
    group = pl.program_id(0)
    total = own.at[group]
    total[...] = jnp.zeros_like(total)
    add_entries(total, table_ref, group, slots, kept, other, groups)


def add_kernel(group, own, came, token, out):
    del token
    out[...] = (own[group] + came[...].astype(F32)).astype(BF16)


def mesh_kernel(
    latent_ref, up_ref, down_ref, gain_ref, own, came, neighbour, out_ref, first_ref, second_ref
):
    total = own[0] + came[...].astype(F32) + neighbour[...].astype(F32)
    mesh_in = latent_ref[...].astype(F32) + total.reshape(latent_ref.shape)
    normed = layer_norm(mesh_in, gain_ref[...]).astype(BF16)
    hidden = silu(jnp.dot(normed, up_ref[...], preferred_element_type=F32)).astype(BF16)
    out = (mesh_in + jnp.dot(hidden, down_ref[...], preferred_element_type=F32)).astype(BF16)
    out_ref[...] = out
    first_ref[...] = out
    second_ref[...] = out


def order_kernel(*refs):
    del refs


def pick_kernel(chosen, slots, groups, tile_rows, table_ref, *refs):
    pieces, outs = refs[:-2], refs[-2:]
    for number, group in enumerate(chosen):
        for slot in range(slots):
            for way, out in enumerate(outs):
                tile = table_ref[way, (way * groups + group) * slots + slot]
                rows = pl.ds(pl.multiple_of(tile * tile_rows, tile_rows), tile_rows)
                into = (number * slots + slot) * tile_rows
                out[into : into + tile_rows] = pieces[number][rows]


def turn_kernel(interp_ref, token, out_ref):
    del token
    for b in range(interp_ref.shape[0]):
        out_ref[b] = interp_ref[b].reshape(out_ref.shape[2], out_ref.shape[1]).T


def join_kernel(*refs):
    pieces, out = refs[:-1], refs[-1]
    start = 0
    for piece in pieces:
        out[start : start + piece.shape[0]] = piece[...]
        start += piece.shape[0]


def back_kernel(
    list_len, table_ref, weights_ref, near_ref, mine_ref, theirs_ref, latent_any,
    out_any, latent_ref, total, out_ref, sems,
):
    blk_count, block_rows, listed = weights_ref.shape
    tile_rows = listed // list_len
    part_rows = BACK_PART * block_rows
    parts = [pl.ds(i * part_rows, part_rows) for i in range(blk_count // BACK_PART)]
    latent_in, outs = [], []
    for i, rows in enumerate(parts):
        latent_in.append(
            pltpu.make_async_copy(latent_any.at[rows], latent_ref.at[rows], sems.at[i])
        )
        outs.append(
            pltpu.make_async_copy(out_ref.at[rows], out_any.at[rows], sems.at[len(parts) + i])
        )
    for copy in latent_in:
        copy.start()

    def rows_at(tile):
        return pl.ds(pl.multiple_of(tile * tile_rows, tile_rows), tile_rows)

    for block in range(blk_count):
        values = []
        for k in range(list_len):
            entry = block * list_len + k
            place, kind = table_ref[2, entry], table_ref[3, entry]
            here = jnp.where(kind > 1, 0, place)
            beyond = jnp.where(kind > 1, place, 0)
            value = near_ref[rows_at(here)]
            value = jnp.where(kind == 2, mine_ref[rows_at(beyond)], value)
            value = jnp.where(kind == 3, theirs_ref[rows_at(beyond)], value)
            values.append(jnp.where(kind > 0, value, jnp.zeros_like(value)))
        value = jnp.concatenate(values, axis=0)
        rows = slice(block * block_rows, (block + 1) * block_rows)
        total[rows] = jnp.dot(weights_ref[block], value, preferred_element_type=F32)
        if block % BACK_PART == 0:
            latent_in[block // BACK_PART].wait()
        for strip in strips(rows):
            out_ref[strip] = (latent_ref[strip].astype(F32) + total[strip]).astype(BF16)
        if block % BACK_PART == BACK_PART - 1:
            outs[block // BACK_PART].start()
    for copy in outs:
        copy.wait()


def whole(array):
    zeros = (0,) * array.ndim
    return pl.BlockSpec(array.shape, lambda *_: zeros)


def params(mib):
    return pltpu.CompilerParams(vmem_limit_bytes=mib * 1024 * 1024)


def cost(flops, *arrays):
    size = sum(a.size * a.dtype.itemsize for a in arrays)
    return pl.CostEstimate(flops=int(flops), bytes_accessed=int(size), transcendentals=0)


def shape(dims, kind=BF16):
    return jax.ShapeDtypeStruct(dims, kind)


def on_device(
    n_y,
    grid_features,
    mesh_latent,
    embed_in,
    embed_out,
    embed_gain,
    interp,
    block_mask,
    tile_list,
    mesh_up,
    mesh_down,
    mesh_gain,
):
    n_band = lax.axis_size("band")
    blk_count, list_len, tile_rows, block_rows = interp.shape
    channels, width = embed_in.shape
    node_rows = mesh_latent.shape[0]
    tiles = node_rows // tile_rows
    entries = blk_count * list_len
    slots = entries // n_band
    ring = Ring(n_band, n_y, tiles)
    chips, far = ring.chips, ring.far
    lists = (lax.axis_index("band").reshape(1), tile_list.T, block_mask.T)

    def in_hbm(array):
        return pltpu.with_memory_space_constraint(array, pltpu.HBM)

    gain = embed_gain.reshape(1, width)
    in_vmem = pl.BlockSpec(memory_space=pltpu.VMEM)
    in_any = pl.BlockSpec(memory_space=pl.ANY)
    grid_rows = blk_count * block_rows
    per_step = 4
    rows = per_step * block_rows
    counts = (chips * slots, 2 * slots, (chips - 2) * slots)
    latent, kept, sent_far, sent_rest, table = pl.pallas_call(
        functools.partial(embed_kernel, ring, per_step, slots),
        out_shape=[pltpu.HBM((blk_count * block_rows, width), BF16)]
        + [shape((count + 1, tile_rows, width)) for count in counts]
        + [shape((4, entries), jnp.int32)],
        grid_spec=pltpu.PrefetchScalarGridSpec(
            num_scalar_prefetch=3,
            grid=(blk_count // per_step,),
            in_specs=[
                pl.BlockSpec((channels, rows), lambda i, *_: (0, i)),
                whole(embed_in),
                whole(embed_out),
                whole(gain),
                pl.BlockSpec((per_step,) + interp.shape[1:], lambda i, *_: (i, 0, 0, 0)),
            ],
            out_specs=[pl.BlockSpec((rows, width), lambda i, *_: (i, 0))]
            + [pl.BlockSpec(memory_space=pltpu.VMEM)] * len(counts)
            + [pl.BlockSpec(memory_space=pltpu.SMEM)],
            scratch_shapes=[pltpu.VMEM((rows, width), F32), pltpu.VMEM((rows, width), BF16)],
        ),
        compiler_params=params(24),
        cost_estimate=cost(
            2 * blk_count * block_rows * width * (channels + width + list_len * tile_rows),
            grid_features,
            interp,
        ),
        name="embed",
    )(lists[0], *map(in_hbm, lists[1:] + (grid_features.T, embed_in, embed_out, gain, interp)))
    other_far = ring.over_core(sent_far)

    dense = (tiles, tile_rows, width)

    def in_order(value, token):
        return pl.pallas_call(
            order_kernel,
            out_shape=shape(value.shape),
            in_specs=[in_any] * 2,
            out_specs=in_any,
            input_output_aliases={0: 0},
            compiler_params=params(1),
            cost_estimate=cost(0),
            name="in_order",
        )(value, token)

    first, second = pl.pallas_call(
        functools.partial(far_kernel, slots, chips),
        out_shape=[shape(dense)] * 2,
        grid_spec=pltpu.PrefetchScalarGridSpec(
            num_scalar_prefetch=1,
            grid=(1,),
            in_specs=[in_vmem] * 2,
            out_specs=[in_vmem] * 2,
            scratch_shapes=[pltpu.VMEM(dense, F32)],
        ),
        compiler_params=params(8),
        cost_estimate=cost(0, kept),
        name="far_sums",
    )(table, kept, other_far)
    other_rest = ring.over_core(in_order(sent_rest, first))
    own = pl.pallas_call(
        functools.partial(own_kernel, slots, chips),
        out_shape=shape((chips - 2,) + dense, F32),
        grid_spec=pltpu.PrefetchScalarGridSpec(
            num_scalar_prefetch=1,
            grid=(chips - 2,),
            in_specs=[in_vmem] * 2,
            out_specs=in_vmem,
        ),
        compiler_params=params(8 if n_band <= 16 else 24),
        cost_estimate=cost(0, kept, kept, kept, kept),
        name="own_sums",
    )(table, kept, other_rest)

    def add_own(group, value, token):
        return pl.pallas_call(
            functools.partial(add_kernel, group),
            out_shape=shape(dense),
            in_specs=[in_vmem] * 2 + [in_any],
            out_specs=in_vmem,
            compiler_params=params(8),
            cost_estimate=cost(0),
            name=f"add_{group}",
        )(own, value, token)

    first, second = ring.over_first(first, far), ring.over_second(second, far - 1)
    turned = (blk_count, block_rows, list_len * tile_rows)
    per_step = 4
    token = weights = pl.pallas_call(
        turn_kernel,
        out_shape=shape(turned),
        grid=(blk_count // per_step,),
        in_specs=[pl.BlockSpec((per_step,) + interp.shape[1:], lambda i: (i, 0, 0, 0)), in_any],
        out_specs=pl.BlockSpec((per_step,) + turned[1:], lambda i: (i, 0, 0)),
        compiler_params=params(8),
        cost_estimate=cost(0, interp, interp),
        name="turn",
    )(interp, own)
    for group in range(chips - 3, 0, -1):
        distance = (group + 1) // 2
        if group % 2:
            token = add_own(group, first, token)
            first = ring.over_first(token, distance)
        else:
            token = add_own(group, second, token)
            second = ring.over_second(token, distance)

    mesh_gain = mesh_gain.reshape(1, width)
    mesh_out, piece, again = pl.pallas_call(
        mesh_kernel,
        out_shape=[shape((node_rows, width))] * 3,
        in_specs=[in_vmem] * 7,
        out_specs=[in_vmem] * 3,
        compiler_params=params(16),
        cost_estimate=cost(4 * node_rows * width * width, mesh_up, mesh_down),
        name="mesh_step",
    )(mesh_latent, mesh_up, mesh_down, mesh_gain, own, first, second)

    mine, theirs = [], []

    def pick(chosen, values):
        out = shape((len(chosen) * slots * tile_rows, width))
        picked = pl.pallas_call(
            functools.partial(pick_kernel, chosen, slots, chips, tile_rows),
            out_shape=[out] * 2,
            grid_spec=pltpu.PrefetchScalarGridSpec(
                num_scalar_prefetch=1,
                grid=(1,),
                in_specs=[in_vmem] * len(values),
                out_specs=[in_vmem] * 2,
            ),
            compiler_params=params(8),
            cost_estimate=cost(0, *values),
            name=f"pick_{chosen[0]}",
        )(table, *values)
        mine.append(picked[0])
        theirs.append(ring.over_core(picked[1]))

    first = ring.over_first(piece, 1)
    pick([0], [piece])
    second = ring.over_second(in_order(again, theirs[0]), 1)
    token = mine[0]
    for distance in range(1, far):
        first = in_order(first, token)
        onward = ring.over_first(first, distance + 1)
        second = in_order(second, first)
        if distance < far - 1:
            after = ring.over_second(second, distance + 1)
        pick([2 * distance - 1, 2 * distance], [first, second])
        token = mine[-1]
        first, second = onward, after
    tiles_far = [first, ring.over_core(first)]
    near = mine + theirs
    joined = pl.pallas_call(
        join_kernel,
        out_shape=shape((sum(piece.shape[0] for piece in near), width)),
        in_specs=[in_vmem] * len(near),
        out_specs=in_vmem,
        compiler_params=params(8),
        cost_estimate=cost(0, *near),
        name="join",
    )(*near)

    grid_out = pl.pallas_call(
        functools.partial(back_kernel, list_len),
        out_shape=shape((grid_rows, width)),
        grid_spec=pltpu.PrefetchScalarGridSpec(
            num_scalar_prefetch=1,
            grid=(1,),
            in_specs=[in_vmem] * 4 + [in_any],
            out_specs=in_any,
            scratch_shapes=[
                pltpu.VMEM((grid_rows, width), BF16),
                pltpu.VMEM((grid_rows, width), F32),
                pltpu.VMEM((grid_rows, width), BF16),
                pltpu.SemaphoreType.DMA((2 * (blk_count // BACK_PART),)),
            ],
        ),
        compiler_params=params(32),
        cost_estimate=cost(2 * grid_rows * width * list_len * tile_rows, latent, latent, interp),
        name="back",
    )(table, weights, joined, *tiles_far, in_hbm(latent))
    return (grid_out, mesh_out)


def solution(mesh):
    placed = (
        P(("groups", "band"), None),
        P(("groups", "band"), None),
        P(),
        P(),
        P(),
        P("band", None, None, None),
        P(),
        P(),
        P(),
        P(),
        P(),
    )
    n_y = max(1, 4 // mesh.shape["groups"])
    return jax.shard_map(
        functools.partial(on_device, n_y),
        mesh=mesh,
        in_specs=placed,
        out_specs=(P(("groups", "band"), None), P(("groups", "band"), None)),
        check_vma=False,
    )
```

```python
import functools

import jax
import jax.numpy as jnp
from jax import lax
from jax.experimental import pallas as pl
from jax.experimental.pallas import tpu as pltpu
from jax.sharding import PartitionSpec as P

F32 = jnp.float32
BF16 = jnp.bfloat16
N_CORE = 2
STRIP = 32
PART = 2
BACK_PART = 2


def silu(values):
    half = 0.5 * values
    return half * (1.0 + jnp.tanh(half))


def layer_norm(values, gain):
    centred = values - jnp.mean(values, axis=-1, keepdims=True)
    spread = jnp.mean(centred * centred, axis=-1, keepdims=True)
    return centred * lax.rsqrt(spread + 1e-05) * gain


def split(value, size):
    if size & (size - 1) == 0:
        return lax.shift_right_logical(value, size.bit_length() - 1), value & (size - 1)
    return lax.div(value, size), lax.rem(value, size)


class Ring:
    def __init__(self, n_band, n_y, tiles):
        self.n_band, self.n_y, self.tiles = n_band, n_y, tiles
        self.chips = n_band // N_CORE
        self.far = self.chips // 2

    def place(self, index):
        chip, core = split(index, N_CORE)
        z, y = split(chip, self.n_y)
        return z + y * (self.chips - 1 - 2 * z), core

    def index(self, ring, core):
        ring = ring % self.chips
        n_z = self.chips // self.n_y
        z, y = (ring, 0) if ring < n_z else (self.chips - 1 - ring, 1)
        return (z * self.n_y + y) * N_CORE + core

    def over_core(self, value):
        return lax.ppermute(value, "band", [(i, i ^ 1) for i in range(self.n_band)])

    def over(self, value, right):
        pairs = []
        for i in range(self.n_band):
            chip, core = divmod(i, N_CORE)
            z, y = divmod(chip, self.n_y)
            ring = z if y == 0 else self.chips - 1 - z
            pairs.append((i, self.index(ring + (1 if core == right else -1), 1 - core)))
        return lax.ppermute(value, "band", pairs)

    def over_first(self, value, distance):
        return self.over(value, distance % 2)

    def over_second(self, value, distance):
        return self.over(value, (distance + 1) % 2)

    def entry(self, lists_ref, me, block, k):
        owner, tile = split(lists_ref[k, block], self.tiles)
        ring, core = self.place(owner)
        my_ring, my_core = self.place(me)
        ahead = split(ring - my_ring + self.chips, self.chips)[1]
        left = (ahead > self.far).astype(jnp.int32)
        distance = jnp.where(ahead > self.far, self.chips - ahead, ahead)
        shared = (ahead == 0) | (ahead == self.far)
        stream = jnp.where(shared, 0, core ^ left)
        group = jnp.maximum(2 * distance - 1 + stream, 0)
        return ((distance + core) & 1) ^ my_core, group, tile


def strips(rows):
    return [slice(r, r + STRIP) for r in range(rows.start, rows.stop, STRIP)]


def embed_kernel(
    ring, per_step, slots, me_ref, lists_ref, mask_ref,
    x_ref, w1_ref, w2_ref, gain_ref, interp_ref,
    latent_ref, near_ref, far_ref, table_ref, wide, hidden,
):
    step = pl.program_id(0)
    me = me_ref[0]
    list_len, tile_rows, block_rows = interp_ref.shape[1:]
    blk_count = pl.num_programs(0) * per_step
    groups = ring.chips

    def spot(index, block, k):
        across, group, tile = ring.entry(lists_ref, index, index * blk_count + block, k)
        slot = split(block * list_len + k, ring.n_band)[0]
        return across, group, tile, slot

    part_rows = PART * block_rows
    spans = [slice(i * part_rows, (i + 1) * part_rows) for i in range(per_step // PART)]
    for rows in spans:
        wide[rows] = lax.dot_general(
            x_ref[:, rows], w1_ref[...], (((0,), (0,)), ((), ())), preferred_element_type=F32
        )
    for rows in spans:
        for strip in strips(rows):
            hidden[strip] = silu(wide[strip]).astype(BF16)
        wide[rows] = jnp.dot(hidden[rows], w2_ref[...], preferred_element_type=F32)
    near_spare, far_spare = near_ref.shape[0] - 1, far_ref.shape[0] - 1
    for number, rows in enumerate(spans):
        for strip in strips(rows):
            latent_ref[strip] = layer_norm(wide[strip], gain_ref[...]).astype(BF16)
        for b in range(number * PART, (number + 1) * PART):
            block = step * per_step + b
            weights = interp_ref[b].reshape(list_len * tile_rows, block_rows)
            latent = latent_ref[b * block_rows : (b + 1) * block_rows]
            part = jnp.dot(weights, latent, preferred_element_type=F32)
            for k in range(list_len):
                across, group, tile, slot = spot(me, block, k)
                place = (across * groups + group) * slots + slot
                mask = mask_ref[k, me * blk_count + block]
                table_ref[0, place] = tile
                beyond = group == groups - 1
                near = (across * (groups - 1) + group) * slots + slot
                table_ref[2, block * list_len + k] = jnp.where(beyond, tile, near)
                table_ref[3, block * list_len + k] = mask * jnp.where(beyond, 2 + across, 1)
                across, group, tile, slot = spot(me ^ 1, block, k)
                table_ref[1, (across * groups + group) * slots + slot] = tile
                masked = part[k * tile_rows : (k + 1) * tile_rows] * mask.astype(F32)
                masked = masked.astype(BF16)
                near_ref[jnp.minimum(place, near_spare)] = masked
                far_ref[jnp.where(place < near_spare, far_spare, place - near_spare)] = masked


def add_entries(total, table_ref, group, slots, kept, other, groups, first):
    for slot in range(slots):
        place = group * slots + slot
        total[table_ref[0, place]] += kept[place].astype(F32)
        total[table_ref[1, groups * slots + place]] += other[place + first * slots].astype(F32)


def far_kernel(slots, groups, table_ref, kept, other, far, before, same, total):
    del same
    for group, out in ((groups - 1, far), (groups - 2, before)):
        total[...] = jnp.zeros_like(total)
        add_entries(total, table_ref, group, slots, kept, other, groups, 2 - groups)
        out[...] = total[...].astype(BF16)


def own_kernel(slots, groups, table_ref, kept, other, own):
    group = pl.program_id(0)
    total = own.at[group]
    total[...] = jnp.zeros_like(total)
    add_entries(total, table_ref, group, slots, kept, other, groups, groups)


def add_kernel(group, own, came, token, out):
    del token
    out[...] = (own[group] + came[...].astype(F32)).astype(BF16)


def mesh_kernel(
    latent_ref, up_ref, down_ref, gain_ref, own, came, neighbour, out_ref, first_ref, second_ref
):
    total = own[0] + came[...].astype(F32) + neighbour[...].astype(F32)
    mesh_in = latent_ref[...].astype(F32) + total.reshape(latent_ref.shape)
    normed = layer_norm(mesh_in, gain_ref[...]).astype(BF16)
    hidden = silu(jnp.dot(normed, up_ref[...], preferred_element_type=F32)).astype(BF16)
    out = (mesh_in + jnp.dot(hidden, down_ref[...], preferred_element_type=F32)).astype(BF16)
    out_ref[...] = out
    first_ref[...] = out
    second_ref[...] = out


def order_kernel(*refs):
    del refs


def pick_kernel(chosen, slots, groups, tile_rows, table_ref, *refs):
    pieces, outs = refs[:-2], refs[-2:]
    for number, group in enumerate(chosen):
        for slot in range(slots):
            for way, out in enumerate(outs):
                tile = table_ref[way, (way * groups + group) * slots + slot]
                rows = pl.ds(pl.multiple_of(tile * tile_rows, tile_rows), tile_rows)
                into = (number * slots + slot) * tile_rows
                out[into : into + tile_rows] = pieces[number][rows]


def turn_kernel(interp_ref, token, out_ref):
    del token
    for b in range(interp_ref.shape[0]):
        out_ref[b] = interp_ref[b].reshape(out_ref.shape[2], out_ref.shape[1]).T


def join_kernel(*refs):
    pieces, out = refs[:-1], refs[-1]
    start = 0
    for piece in pieces:
        out[start : start + piece.shape[0]] = piece[...]
        start += piece.shape[0]


def back_kernel(
    list_len, table_ref, weights_ref, near_ref, mine_ref, theirs_ref, latent_any,
    out_any, latent_ref, total, out_ref, sems,
):
    blk_count, block_rows, listed = weights_ref.shape
    tile_rows = listed // list_len
    part_rows = BACK_PART * block_rows
    parts = [pl.ds(i * part_rows, part_rows) for i in range(blk_count // BACK_PART)]
    latent_in, outs = [], []
    for i, rows in enumerate(parts):
        latent_in.append(
            pltpu.make_async_copy(latent_any.at[rows], latent_ref.at[rows], sems.at[i])
        )
        outs.append(
            pltpu.make_async_copy(out_ref.at[rows], out_any.at[rows], sems.at[len(parts) + i])
        )
    for copy in latent_in:
        copy.start()

    def rows_at(tile):
        return pl.ds(pl.multiple_of(tile * tile_rows, tile_rows), tile_rows)

    for block in range(blk_count):
        values = []
        for k in range(list_len):
            entry = block * list_len + k
            place, kind = table_ref[2, entry], table_ref[3, entry]
            here = jnp.where(kind > 1, 0, place)
            beyond = jnp.where(kind > 1, place, 0)
            value = near_ref[rows_at(here)]
            value = jnp.where(kind == 2, mine_ref[rows_at(beyond)], value)
            value = jnp.where(kind == 3, theirs_ref[rows_at(beyond)], value)
            values.append(jnp.where(kind > 0, value, jnp.zeros_like(value)))
        value = jnp.concatenate(values, axis=0)
        rows = slice(block * block_rows, (block + 1) * block_rows)
        total[rows] = jnp.dot(weights_ref[block], value, preferred_element_type=F32)
        if block % BACK_PART == 0:
            latent_in[block // BACK_PART].wait()
        for strip in strips(rows):
            out_ref[strip] = (latent_ref[strip].astype(F32) + total[strip]).astype(BF16)
        if block % BACK_PART == BACK_PART - 1:
            outs[block // BACK_PART].start()
    for copy in outs:
        copy.wait()


def whole(array):
    zeros = (0,) * array.ndim
    return pl.BlockSpec(array.shape, lambda *_: zeros)


def params(mib):
    return pltpu.CompilerParams(vmem_limit_bytes=mib * 1024 * 1024)


def cost(flops, *arrays):
    size = sum(a.size * a.dtype.itemsize for a in arrays)
    return pl.CostEstimate(flops=int(flops), bytes_accessed=int(size), transcendentals=0)


def shape(dims, kind=BF16):
    return jax.ShapeDtypeStruct(dims, kind)


def on_device(
    n_y,
    grid_features,
    mesh_latent,
    embed_in,
    embed_out,
    embed_gain,
    interp,
    block_mask,
    tile_list,
    mesh_up,
    mesh_down,
    mesh_gain,
):
    n_band = lax.axis_size("band")
    blk_count, list_len, tile_rows, block_rows = interp.shape
    channels, width = embed_in.shape
    node_rows = mesh_latent.shape[0]
    tiles = node_rows // tile_rows
    entries = blk_count * list_len
    slots = entries // n_band
    ring = Ring(n_band, n_y, tiles)
    chips, far = ring.chips, ring.far
    lists = (lax.axis_index("band").reshape(1), tile_list.T, block_mask.T)

    def in_hbm(array):
        return pltpu.with_memory_space_constraint(array, pltpu.HBM)

    gain = embed_gain.reshape(1, width)
    in_vmem = pl.BlockSpec(memory_space=pltpu.VMEM)
    in_any = pl.BlockSpec(memory_space=pl.ANY)
    grid_rows = blk_count * block_rows
    per_step = 4
    rows = per_step * block_rows
    counts = ((2 * chips - 2) * slots, 2 * slots)
    latent, near, sent_far, table = pl.pallas_call(
        functools.partial(embed_kernel, ring, per_step, slots),
        out_shape=[pltpu.HBM((blk_count * block_rows, width), BF16)]
        + [shape((count + 1, tile_rows, width)) for count in counts]
        + [shape((4, entries), jnp.int32)],
        grid_spec=pltpu.PrefetchScalarGridSpec(
            num_scalar_prefetch=3,
            grid=(blk_count // per_step,),
            in_specs=[
                pl.BlockSpec((channels, rows), lambda i, *_: (0, i)),
                whole(embed_in),
                whole(embed_out),
                whole(gain),
                pl.BlockSpec((per_step,) + interp.shape[1:], lambda i, *_: (i, 0, 0, 0)),
            ],
            out_specs=[pl.BlockSpec((rows, width), lambda i, *_: (i, 0))]
            + [pl.BlockSpec(memory_space=pltpu.VMEM)] * len(counts)
            + [pl.BlockSpec(memory_space=pltpu.SMEM)],
            scratch_shapes=[pltpu.VMEM((rows, width), F32), pltpu.VMEM((rows, width), BF16)],
        ),
        compiler_params=params(24),
        cost_estimate=cost(
            2 * blk_count * block_rows * width * (channels + width + list_len * tile_rows),
            grid_features,
            interp,
        ),
        name="embed",
    )(lists[0], *map(in_hbm, lists[1:] + (grid_features.T, embed_in, embed_out, gain, interp)))
    other_far = ring.over_core(sent_far)

    dense = (tiles, tile_rows, width)

    def in_order(value, token):
        return pl.pallas_call(
            order_kernel,
            out_shape=shape(value.shape),
            in_specs=[in_any] * 2,
            out_specs=in_any,
            input_output_aliases={0: 0},
            compiler_params=params(1),
            cost_estimate=cost(0),
            name="in_order",
        )(value, token)

    first, second, near = pl.pallas_call(
        functools.partial(far_kernel, slots, chips),
        out_shape=[shape(dense)] * 2 + [shape(near.shape)],
        grid_spec=pltpu.PrefetchScalarGridSpec(
            num_scalar_prefetch=1,
            grid=(1,),
            in_specs=[in_vmem] * 2,
            out_specs=[in_vmem] * 3,
            scratch_shapes=[pltpu.VMEM(dense, F32)],
        ),
        input_output_aliases={1: 2},
        compiler_params=params(8),
        cost_estimate=cost(0, near),
        name="far_sums",
    )(table, near, other_far)
    other = ring.over_core(near)
    own = pl.pallas_call(
        functools.partial(own_kernel, slots, chips),
        out_shape=shape((chips - 2,) + dense, F32),
        grid_spec=pltpu.PrefetchScalarGridSpec(
            num_scalar_prefetch=1,
            grid=(chips - 2,),
            in_specs=[in_vmem] * 2,
            out_specs=in_vmem,
        ),
        compiler_params=params(8 if n_band <= 16 else 24),
        cost_estimate=cost(0, near, near),
        name="own_sums",
    )(table, near, other)

    def add_own(group, value, token):
        return pl.pallas_call(
            functools.partial(add_kernel, group),
            out_shape=shape(dense),
            in_specs=[in_vmem] * 2 + [in_any],
            out_specs=in_vmem,
            compiler_params=params(8),
            cost_estimate=cost(0),
            name=f"add_{group}",
        )(own, value, token)

    first, second = ring.over_first(first, far), ring.over_second(second, far - 1)
    turned = (blk_count, block_rows, list_len * tile_rows)
    per_step = 4
    token = weights = pl.pallas_call(
        turn_kernel,
        out_shape=shape(turned),
        grid=(blk_count // per_step,),
        in_specs=[pl.BlockSpec((per_step,) + interp.shape[1:], lambda i: (i, 0, 0, 0)), in_any],
        out_specs=pl.BlockSpec((per_step,) + turned[1:], lambda i: (i, 0, 0)),
        compiler_params=params(8),
        cost_estimate=cost(0, interp, interp),
        name="turn",
    )(interp, own)
    for group in range(chips - 3, 0, -1):
        distance = (group + 1) // 2
        if group % 2:
            token = add_own(group, first, token)
            first = ring.over_first(token, distance)
        else:
            token = add_own(group, second, token)
            second = ring.over_second(token, distance)

    mesh_gain = mesh_gain.reshape(1, width)
    mesh_out, piece, again = pl.pallas_call(
        mesh_kernel,
        out_shape=[shape((node_rows, width))] * 3,
        in_specs=[in_vmem] * 7,
        out_specs=[in_vmem] * 3,
        compiler_params=params(16),
        cost_estimate=cost(4 * node_rows * width * width, mesh_up, mesh_down),
        name="mesh_step",
    )(mesh_latent, mesh_up, mesh_down, mesh_gain, own, first, second)

    mine, theirs = [], []

    def pick(chosen, values):
        out = shape((len(chosen) * slots * tile_rows, width))
        picked = pl.pallas_call(
            functools.partial(pick_kernel, chosen, slots, chips, tile_rows),
            out_shape=[out] * 2,
            grid_spec=pltpu.PrefetchScalarGridSpec(
                num_scalar_prefetch=1,
                grid=(1,),
                in_specs=[in_vmem] * len(values),
                out_specs=[in_vmem] * 2,
            ),
            compiler_params=params(8),
            cost_estimate=cost(0, *values),
            name=f"pick_{chosen[0]}",
        )(table, *values)
        mine.append(picked[0])
        theirs.append(ring.over_core(picked[1]))

    first = ring.over_first(piece, 1)
    pick([0], [piece])
    second = ring.over_second(in_order(again, theirs[0]), 1)
    token = mine[0]
    for distance in range(1, far):
        first = in_order(first, token)
        onward = ring.over_first(first, distance + 1)
        second = in_order(second, first)
        if distance < far - 1:
            after = ring.over_second(second, distance + 1)
        pick([2 * distance - 1, 2 * distance], [first, second])
        token = mine[-1]
        first, second = onward, after
    tiles_far = [first, ring.over_core(first)]
    parts = mine + theirs
    joined = pl.pallas_call(
        join_kernel,
        out_shape=shape((sum(part.shape[0] for part in parts), width)),
        in_specs=[in_vmem] * len(parts),
        out_specs=in_vmem,
        compiler_params=params(8),
        cost_estimate=cost(0, *parts),
        name="join",
    )(*parts)

    grid_out = pl.pallas_call(
        functools.partial(back_kernel, list_len),
        out_shape=shape((grid_rows, width)),
        grid_spec=pltpu.PrefetchScalarGridSpec(
            num_scalar_prefetch=1,
            grid=(1,),
            in_specs=[in_vmem] * 4 + [in_any],
            out_specs=in_any,
            scratch_shapes=[
                pltpu.VMEM((grid_rows, width), BF16),
                pltpu.VMEM((grid_rows, width), F32),
                pltpu.VMEM((grid_rows, width), BF16),
                pltpu.SemaphoreType.DMA((2 * (blk_count // BACK_PART),)),
            ],
        ),
        compiler_params=params(32),
        cost_estimate=cost(2 * grid_rows * width * list_len * tile_rows, latent, latent, interp),
        name="back",
    )(table, weights, joined, *tiles_far, in_hbm(latent))
    return (grid_out, mesh_out)


def solution(mesh):
    placed = (
        P(("groups", "band"), None),
        P(("groups", "band"), None),
        P(),
        P(),
        P(),
        P("band", None, None, None),
        P(),
        P(),
        P(),
        P(),
        P(),
    )
    n_y = max(1, 4 // mesh.shape["groups"])
    return jax.shard_map(
        functools.partial(on_device, n_y),
        mesh=mesh,
        in_specs=placed,
        out_specs=(P(("groups", "band"), None), P(("groups", "band"), None)),
        check_vma=False,
    )
```

```python
import functools

import jax
import jax.numpy as jnp
from jax import lax
from jax.experimental import pallas as pl
from jax.experimental.pallas import tpu as pltpu
from jax.sharding import PartitionSpec as P

F32 = jnp.float32
BF16 = jnp.bfloat16
N_CORE = 2
STRIP = 32
PART = 2
BACK_PART = 4


def silu(values):
    half = 0.5 * values
    return half * (1.0 + jnp.tanh(half))


def layer_norm(values, gain):
    centred = values - jnp.mean(values, axis=-1, keepdims=True)
    spread = jnp.mean(centred * centred, axis=-1, keepdims=True)
    return centred * lax.rsqrt(spread + 1e-05) * gain


def split(value, size):
    if size & (size - 1) == 0:
        return lax.shift_right_logical(value, size.bit_length() - 1), value & (size - 1)
    return lax.div(value, size), lax.rem(value, size)


class Ring:
    def __init__(self, n_band, n_y, tiles):
        self.n_band, self.n_y, self.tiles = n_band, n_y, tiles
        self.chips = n_band // N_CORE
        self.far = self.chips // 2

    def place(self, index):
        chip, core = split(index, N_CORE)
        z, y = split(chip, self.n_y)
        return z + y * (self.chips - 1 - 2 * z), core

    def index(self, ring, core):
        ring = ring % self.chips
        n_z = self.chips // self.n_y
        z, y = (ring, 0) if ring < n_z else (self.chips - 1 - ring, 1)
        return (z * self.n_y + y) * N_CORE + core

    def over_core(self, value):
        return lax.ppermute(value, "band", [(i, i ^ 1) for i in range(self.n_band)])

    def over(self, value, right):
        pairs = []
        for i in range(self.n_band):
            chip, core = divmod(i, N_CORE)
            z, y = divmod(chip, self.n_y)
            ring = z if y == 0 else self.chips - 1 - z
            pairs.append((i, self.index(ring + (1 if core == right else -1), 1 - core)))
        return lax.ppermute(value, "band", pairs)

    def over_first(self, value, distance):
        return self.over(value, distance % 2)

    def over_second(self, value, distance):
        return self.over(value, (distance + 1) % 2)

    def seen(self, owner, me):
        ring, core = self.place(owner)
        my_ring, my_core = self.place(me)
        ahead = split(ring - my_ring + self.chips, self.chips)[1]
        left = (ahead > self.far).astype(jnp.int32)
        distance = jnp.where(ahead > self.far, self.chips - ahead, ahead)
        shared = (ahead == 0) | (ahead == self.far)
        stream = jnp.where(shared, 0, core ^ left)
        group = jnp.maximum(2 * distance - 1 + stream, 0)
        return ((distance + core) & 1) ^ my_core, group


def strips(rows):
    return [slice(r, r + STRIP) for r in range(rows.start, rows.stop, STRIP)]


def embed_kernel(
    ring, per_step, slots, me_ref, lists_ref, mask_ref,
    x_ref, w1_ref, w2_ref, gain_ref, interp_ref,
    latent_ref, near_ref, far_ref, table_ref, wide, hidden, owners_ref,
):
    step = pl.program_id(0)
    me = me_ref[0]
    list_len, tile_rows, block_rows = interp_ref.shape[1:]
    blk_count = pl.num_programs(0) * per_step
    groups = ring.chips

    @pl.when(step == 0)
    def _():
        def note(owner, carry):
            across, group = ring.seen(owner, me)
            owners_ref[0, owner] = (across * groups + group) * slots
            owners_ref[1, owner] = ((across ^ 1) * groups + group) * slots
            return carry

        lax.fori_loop(0, ring.n_band, note, 0)

    def spot(who, block, k):
        owner, tile = split(lists_ref[k, (me ^ who) * blk_count + block], ring.tiles)
        slot = split(block * list_len + k, ring.n_band)[0]
        return owners_ref[who, owner] + slot, tile

    part_rows = PART * block_rows
    spans = [slice(i * part_rows, (i + 1) * part_rows) for i in range(per_step // PART)]
    for rows in spans:
        wide[rows] = lax.dot_general(
            x_ref[:, rows], w1_ref[...], (((0,), (0,)), ((), ())), preferred_element_type=F32
        )
    for rows in spans:
        for strip in strips(rows):
            hidden[strip] = silu(wide[strip]).astype(BF16)
        wide[rows] = jnp.dot(hidden[rows], w2_ref[...], preferred_element_type=F32)
    near_spare, far_spare = near_ref.shape[0] - 1, far_ref.shape[0] - 1
    for number, rows in enumerate(spans):
        for strip in strips(rows):
            latent_ref[strip] = layer_norm(wide[strip], gain_ref[...]).astype(BF16)
        for b in range(number * PART, (number + 1) * PART):
            block = step * per_step + b
            weights = interp_ref[b].reshape(list_len * tile_rows, block_rows)
            latent = latent_ref[b * block_rows : (b + 1) * block_rows]
            part = jnp.dot(weights, latent, preferred_element_type=F32)
            for k in range(list_len):
                place, tile = spot(0, block, k)
                mask = mask_ref[k, me * blk_count + block]
                table_ref[0, place] = tile
                across = (place >= groups * slots).astype(jnp.int32)
                near = place - across * slots
                beyond = place - across * groups * slots >= (groups - 1) * slots
                table_ref[2, block * list_len + k] = jnp.where(beyond, tile, near)
                table_ref[3, block * list_len + k] = mask * jnp.where(beyond, 2 + across, 1)
                there, its_tile = spot(1, block, k)
                table_ref[1, there] = its_tile
                masked = part[k * tile_rows : (k + 1) * tile_rows] * mask.astype(F32)
                masked = masked.astype(BF16)
                near_ref[jnp.minimum(place, near_spare)] = masked
                far_ref[jnp.where(place < near_spare, far_spare, place - near_spare)] = masked


def add_entries(total, table_ref, group, slots, kept, other, groups, first):
    for slot in range(slots):
        place = group * slots + slot
        total[table_ref[0, place]] += kept[place].astype(F32)
        total[table_ref[1, groups * slots + place]] += other[place + first * slots].astype(F32)


def far_kernel(slots, groups, table_ref, kept, other, far, before, same, total):
    del same
    for group, out in ((groups - 1, far), (groups - 2, before)):
        total[...] = jnp.zeros_like(total)
        add_entries(total, table_ref, group, slots, kept, other, groups, 2 - groups)
        out[...] = total[...].astype(BF16)


def own_kernel(slots, groups, table_ref, kept, other, own):
    group = pl.program_id(0)
    total = own.at[group]
    total[...] = jnp.zeros_like(total)
    add_entries(total, table_ref, group, slots, kept, other, groups, groups)


def add_kernel(group, own, came, token, out):
    del token
    out[...] = (own[group] + came[...].astype(F32)).astype(BF16)


def mesh_kernel(
    latent_ref, up_ref, down_ref, gain_ref, own, came, neighbour, out_ref, first_ref, second_ref
):
    total = own[0] + came[...].astype(F32) + neighbour[...].astype(F32)
    mesh_in = latent_ref[...].astype(F32) + total.reshape(latent_ref.shape)
    normed = layer_norm(mesh_in, gain_ref[...]).astype(BF16)
    hidden = silu(jnp.dot(normed, up_ref[...], preferred_element_type=F32)).astype(BF16)
    out = (mesh_in + jnp.dot(hidden, down_ref[...], preferred_element_type=F32)).astype(BF16)
    out_ref[...] = out
    first_ref[...] = out
    second_ref[...] = out


def order_kernel(*refs):
    del refs


def pick_kernel(chosen, slots, groups, tile_rows, table_ref, *refs):
    pieces, outs = refs[:-2], refs[-2:]
    for number, group in enumerate(chosen):
        for slot in range(slots):
            for way, out in enumerate(outs):
                tile = table_ref[way, (way * groups + group) * slots + slot]
                rows = pl.ds(pl.multiple_of(tile * tile_rows, tile_rows), tile_rows)
                into = (number * slots + slot) * tile_rows
                out[into : into + tile_rows] = pieces[number][rows]


def turn_kernel(interp_ref, token, out_ref):
    del token
    for b in range(interp_ref.shape[0]):
        out_ref[b] = interp_ref[b].reshape(out_ref.shape[2], out_ref.shape[1]).T


def join_kernel(*refs):
    pieces, out = refs[:-1], refs[-1]
    start = 0
    for piece in pieces:
        out[start : start + piece.shape[0]] = piece[...]
        start += piece.shape[0]


def back_kernel(
    list_len, table_ref, weights_ref, near_ref, mine_ref, theirs_ref, latent_any,
    out_any, latent_ref, total, out_ref, sems,
):
    blk_count, block_rows, listed = weights_ref.shape
    tile_rows = listed // list_len
    part_rows = BACK_PART * block_rows
    parts = [pl.ds(i * part_rows, part_rows) for i in range(blk_count // BACK_PART)]
    latent_in, outs = [], []
    for i, rows in enumerate(parts):
        latent_in.append(
            pltpu.make_async_copy(latent_any.at[rows], latent_ref.at[rows], sems.at[i])
        )
        outs.append(
            pltpu.make_async_copy(out_ref.at[rows], out_any.at[rows], sems.at[len(parts) + i])
        )
    for copy in latent_in:
        copy.start()

    def rows_at(tile):
        return pl.ds(pl.multiple_of(tile * tile_rows, tile_rows), tile_rows)

    for block in range(blk_count):
        values = []
        for k in range(list_len):
            entry = block * list_len + k
            place, kind = table_ref[2, entry], table_ref[3, entry]
            here = jnp.where(kind > 1, 0, place)
            beyond = jnp.where(kind > 1, place, 0)
            value = near_ref[rows_at(here)]
            value = jnp.where(kind == 2, mine_ref[rows_at(beyond)], value)
            value = jnp.where(kind == 3, theirs_ref[rows_at(beyond)], value)
            values.append(jnp.where(kind > 0, value, jnp.zeros_like(value)))
        value = jnp.concatenate(values, axis=0)
        rows = slice(block * block_rows, (block + 1) * block_rows)
        total[rows] = jnp.dot(weights_ref[block], value, preferred_element_type=F32)
        if block % BACK_PART == 0:
            latent_in[block // BACK_PART].wait()
        for strip in strips(rows):
            out_ref[strip] = (latent_ref[strip].astype(F32) + total[strip]).astype(BF16)
        if block % BACK_PART == BACK_PART - 1:
            outs[block // BACK_PART].start()
    for copy in outs:
        copy.wait()


def whole(array):
    zeros = (0,) * array.ndim
    return pl.BlockSpec(array.shape, lambda *_: zeros)


def params(mib):
    return pltpu.CompilerParams(vmem_limit_bytes=mib * 1024 * 1024)


def cost(flops, *arrays):
    size = sum(a.size * a.dtype.itemsize for a in arrays)
    return pl.CostEstimate(flops=int(flops), bytes_accessed=int(size), transcendentals=0)


def shape(dims, kind=BF16):
    return jax.ShapeDtypeStruct(dims, kind)


def on_device(
    n_y,
    grid_features,
    mesh_latent,
    embed_in,
    embed_out,
    embed_gain,
    interp,
    block_mask,
    tile_list,
    mesh_up,
    mesh_down,
    mesh_gain,
):
    n_band = lax.axis_size("band")
    blk_count, list_len, tile_rows, block_rows = interp.shape
    channels, width = embed_in.shape
    node_rows = mesh_latent.shape[0]
    tiles = node_rows // tile_rows
    entries = blk_count * list_len
    slots = entries // n_band
    ring = Ring(n_band, n_y, tiles)
    chips, far = ring.chips, ring.far
    lists = (lax.axis_index("band").reshape(1), tile_list.T, block_mask.T)

    def in_hbm(array):
        return pltpu.with_memory_space_constraint(array, pltpu.HBM)

    gain = embed_gain.reshape(1, width)
    in_vmem = pl.BlockSpec(memory_space=pltpu.VMEM)
    in_any = pl.BlockSpec(memory_space=pl.ANY)
    grid_rows = blk_count * block_rows
    per_step = 4
    rows = per_step * block_rows
    counts = ((2 * chips - 2) * slots, 2 * slots)
    latent, near, sent_far, table = pl.pallas_call(
        functools.partial(embed_kernel, ring, per_step, slots),
        out_shape=[pltpu.HBM((blk_count * block_rows, width), BF16)]
        + [shape((count + 1, tile_rows, width)) for count in counts]
        + [shape((4, entries), jnp.int32)],
        grid_spec=pltpu.PrefetchScalarGridSpec(
            num_scalar_prefetch=3,
            grid=(blk_count // per_step,),
            in_specs=[
                pl.BlockSpec((channels, rows), lambda i, *_: (0, i)),
                whole(embed_in),
                whole(embed_out),
                whole(gain),
                pl.BlockSpec((per_step,) + interp.shape[1:], lambda i, *_: (i, 0, 0, 0)),
            ],
            out_specs=[pl.BlockSpec((rows, width), lambda i, *_: (i, 0))]
            + [pl.BlockSpec(memory_space=pltpu.VMEM)] * len(counts)
            + [pl.BlockSpec(memory_space=pltpu.SMEM)],
            scratch_shapes=[
                pltpu.VMEM((rows, width), F32),
                pltpu.VMEM((rows, width), BF16),
                pltpu.SMEM((2, n_band), jnp.int32),
            ],
        ),
        compiler_params=params(24),
        cost_estimate=cost(
            2 * blk_count * block_rows * width * (channels + width + list_len * tile_rows),
            grid_features,
            interp,
        ),
        name="embed",
    )(lists[0], *map(in_hbm, lists[1:] + (grid_features.T, embed_in, embed_out, gain, interp)))
    other_far = ring.over_core(sent_far)

    dense = (tiles, tile_rows, width)

    def in_order(value, token):
        return pl.pallas_call(
            order_kernel,
            out_shape=shape(value.shape),
            in_specs=[in_any] * 2,
            out_specs=in_any,
            input_output_aliases={0: 0},
            compiler_params=params(1),
            cost_estimate=cost(0),
            name="in_order",
        )(value, token)

    first, second, near = pl.pallas_call(
        functools.partial(far_kernel, slots, chips),
        out_shape=[shape(dense)] * 2 + [shape(near.shape)],
        grid_spec=pltpu.PrefetchScalarGridSpec(
            num_scalar_prefetch=1,
            grid=(1,),
            in_specs=[in_vmem] * 2,
            out_specs=[in_vmem] * 3,
            scratch_shapes=[pltpu.VMEM(dense, F32)],
        ),
        input_output_aliases={1: 2},
        compiler_params=params(8),
        cost_estimate=cost(0, near),
        name="far_sums",
    )(table, near, other_far)
    other = ring.over_core(near)
    own = pl.pallas_call(
        functools.partial(own_kernel, slots, chips),
        out_shape=shape((chips - 2,) + dense, F32),
        grid_spec=pltpu.PrefetchScalarGridSpec(
            num_scalar_prefetch=1,
            grid=(chips - 2,),
            in_specs=[in_vmem] * 2,
            out_specs=in_vmem,
        ),
        compiler_params=params(8 if n_band <= 16 else 24),
        cost_estimate=cost(0, near, near),
        name="own_sums",
    )(table, near, other)

    def add_own(group, value, token):
        return pl.pallas_call(
            functools.partial(add_kernel, group),
            out_shape=shape(dense),
            in_specs=[in_vmem] * 2 + [in_any],
            out_specs=in_vmem,
            compiler_params=params(8),
            cost_estimate=cost(0),
            name=f"add_{group}",
        )(own, value, token)

    first, second = ring.over_first(first, far), ring.over_second(second, far - 1)
    turned = (blk_count, block_rows, list_len * tile_rows)
    per_step = 4
    token = weights = pl.pallas_call(
        turn_kernel,
        out_shape=shape(turned),
        grid=(blk_count // per_step,),
        in_specs=[pl.BlockSpec((per_step,) + interp.shape[1:], lambda i: (i, 0, 0, 0)), in_any],
        out_specs=pl.BlockSpec((per_step,) + turned[1:], lambda i: (i, 0, 0)),
        compiler_params=params(8),
        cost_estimate=cost(0, interp, interp),
        name="turn",
    )(interp, own)
    for group in range(chips - 3, 0, -1):
        distance = (group + 1) // 2
        if group % 2:
            token = add_own(group, first, token)
            first = ring.over_first(token, distance)
        else:
            token = add_own(group, second, token)
            second = ring.over_second(token, distance)

    mesh_gain = mesh_gain.reshape(1, width)
    mesh_out, piece, again = pl.pallas_call(
        mesh_kernel,
        out_shape=[shape((node_rows, width))] * 3,
        in_specs=[in_vmem] * 7,
        out_specs=[in_vmem] * 3,
        compiler_params=params(16),
        cost_estimate=cost(4 * node_rows * width * width, mesh_up, mesh_down),
        name="mesh_step",
    )(mesh_latent, mesh_up, mesh_down, mesh_gain, own, first, second)

    mine, theirs = [], []

    def pick(chosen, values):
        out = shape((len(chosen) * slots * tile_rows, width))
        picked = pl.pallas_call(
            functools.partial(pick_kernel, chosen, slots, chips, tile_rows),
            out_shape=[out] * 2,
            grid_spec=pltpu.PrefetchScalarGridSpec(
                num_scalar_prefetch=1,
                grid=(1,),
                in_specs=[in_vmem] * len(values),
                out_specs=[in_vmem] * 2,
            ),
            compiler_params=params(8),
            cost_estimate=cost(0, *values),
            name=f"pick_{chosen[0]}",
        )(table, *values)
        mine.append(picked[0])
        theirs.append(ring.over_core(picked[1]))

    first = ring.over_first(piece, 1)
    pick([0], [piece])
    second = ring.over_second(in_order(again, theirs[0]), 1)
    token = mine[0]
    for distance in range(1, far):
        first = in_order(first, token)
        onward = ring.over_first(first, distance + 1)
        second = in_order(second, first)
        if distance < far - 1:
            after = ring.over_second(second, distance + 1)
        pick([2 * distance - 1, 2 * distance], [first, second])
        token = mine[-1]
        first, second = onward, after
    tiles_far = [first, ring.over_core(first)]
    parts = mine + theirs
    joined = pl.pallas_call(
        join_kernel,
        out_shape=shape((sum(part.shape[0] for part in parts), width)),
        in_specs=[in_vmem] * len(parts),
        out_specs=in_vmem,
        compiler_params=params(8),
        cost_estimate=cost(0, *parts),
        name="join",
    )(*parts)

    grid_out = pl.pallas_call(
        functools.partial(back_kernel, list_len),
        out_shape=shape((grid_rows, width)),
        grid_spec=pltpu.PrefetchScalarGridSpec(
            num_scalar_prefetch=1,
            grid=(1,),
            in_specs=[in_vmem] * 4 + [in_any],
            out_specs=in_any,
            scratch_shapes=[
                pltpu.VMEM((grid_rows, width), BF16),
                pltpu.VMEM((grid_rows, width), F32),
                pltpu.VMEM((grid_rows, width), BF16),
                pltpu.SemaphoreType.DMA((2 * (blk_count // BACK_PART),)),
            ],
        ),
        compiler_params=params(32),
        cost_estimate=cost(2 * grid_rows * width * list_len * tile_rows, latent, latent, interp),
        name="back",
    )(table, weights, joined, *tiles_far, in_hbm(latent))
    return (grid_out, mesh_out)


def solution(mesh):
    placed = (
        P(("groups", "band"), None),
        P(("groups", "band"), None),
        P(),
        P(),
        P(),
        P("band", None, None, None),
        P(),
        P(),
        P(),
        P(),
        P(),
    )
    n_y = max(1, 4 // mesh.shape["groups"])
    return jax.shard_map(
        functools.partial(on_device, n_y),
        mesh=mesh,
        in_specs=placed,
        out_specs=(P(("groups", "band"), None), P(("groups", "band"), None)),
        check_vma=False,
    )
```

```python
import functools

import jax
import jax.numpy as jnp
from jax import lax
from jax.experimental import pallas as pl
from jax.experimental.pallas import tpu as pltpu
from jax.sharding import PartitionSpec as P

F32 = jnp.float32
BF16 = jnp.bfloat16
N_CORE = 2
STRIP = 32
PART = 2
BACK_PART = 4


def silu(values):
    half = 0.5 * values
    return half * (1.0 + jnp.tanh(half))


def layer_norm(values, gain):
    centred = values - jnp.mean(values, axis=-1, keepdims=True)
    spread = jnp.mean(centred * centred, axis=-1, keepdims=True)
    return centred * lax.rsqrt(spread + 1e-05) * gain


def split(value, size):
    if size & (size - 1) == 0:
        return lax.shift_right_logical(value, size.bit_length() - 1), value & (size - 1)
    return lax.div(value, size), lax.rem(value, size)


class Ring:
    def __init__(self, n_band, n_y, tiles):
        self.n_band, self.n_y, self.tiles = n_band, n_y, tiles
        self.chips = n_band // N_CORE
        self.far = self.chips // 2

    def place(self, index):
        chip, core = split(index, N_CORE)
        z, y = split(chip, self.n_y)
        return z + y * (self.chips - 1 - 2 * z), core

    def index(self, ring, core):
        ring = ring % self.chips
        n_z = self.chips // self.n_y
        z, y = (ring, 0) if ring < n_z else (self.chips - 1 - ring, 1)
        return (z * self.n_y + y) * N_CORE + core

    def over_core(self, value):
        return lax.ppermute(value, "band", [(i, i ^ 1) for i in range(self.n_band)])

    def over(self, value, right):
        pairs = []
        for i in range(self.n_band):
            chip, core = divmod(i, N_CORE)
            z, y = divmod(chip, self.n_y)
            ring = z if y == 0 else self.chips - 1 - z
            pairs.append((i, self.index(ring + (1 if core == right else -1), 1 - core)))
        return lax.ppermute(value, "band", pairs)

    def over_first(self, value, distance):
        return self.over(value, distance % 2)

    def over_second(self, value, distance):
        return self.over(value, (distance + 1) % 2)

    def seen(self, owner, me):
        ring, core = self.place(owner)
        my_ring, my_core = self.place(me)
        ahead = split(ring - my_ring + self.chips, self.chips)[1]
        left = (ahead > self.far).astype(jnp.int32)
        distance = jnp.where(ahead > self.far, self.chips - ahead, ahead)
        shared = (ahead == 0) | (ahead == self.far)
        stream = jnp.where(shared, 0, core ^ left)
        group = jnp.maximum(2 * distance - 1 + stream, 0)
        return ((distance + core) & 1) ^ my_core, group


def strips(rows):
    return [slice(r, r + STRIP) for r in range(rows.start, rows.stop, STRIP)]


def embed_kernel(
    ring, per_step, slots, me_ref, lists_ref, mask_ref,
    x_ref, w1_ref, w2_ref, gain_ref, interp_ref,
    latent_ref, near_ref, far_ref, table_ref, wide, hidden, owners_ref,
):
    step = pl.program_id(0)
    me = me_ref[0]
    list_len, tile_rows, block_rows = interp_ref.shape[1:]
    blk_count = pl.num_programs(0) * per_step
    groups = ring.chips

    @pl.when(step == 0)
    def _():
        def note(owner, carry):
            across, group = ring.seen(owner, me)
            owners_ref[0, owner] = (across * groups + group) * slots
            owners_ref[1, owner] = ((across ^ 1) * groups + group) * slots
            return carry

        lax.fori_loop(0, ring.n_band, note, 0)

    def spot(who, block, k):
        owner, tile = split(lists_ref[k, (me ^ who) * blk_count + block], ring.tiles)
        slot = split(block * list_len + k, ring.n_band)[0]
        return owners_ref[who, owner] + slot, tile

    part_rows = PART * block_rows
    spans = [slice(i * part_rows, (i + 1) * part_rows) for i in range(per_step // PART)]
    for rows in spans:
        wide[rows] = lax.dot_general(
            x_ref[:, rows], w1_ref[...], (((0,), (0,)), ((), ())), preferred_element_type=F32
        )
    for rows in spans:
        for strip in strips(rows):
            hidden[strip] = silu(wide[strip]).astype(BF16)
        wide[rows] = jnp.dot(hidden[rows], w2_ref[...], preferred_element_type=F32)
    near_spare, far_spare = near_ref.shape[0] - 1, far_ref.shape[0] - 1
    for number, rows in enumerate(spans):
        for strip in strips(rows):
            latent_ref[strip] = layer_norm(wide[strip], gain_ref[...]).astype(BF16)
        for b in range(number * PART, (number + 1) * PART):
            block = step * per_step + b
            weights = interp_ref[b].reshape(list_len * tile_rows, block_rows)
            latent = latent_ref[b * block_rows : (b + 1) * block_rows]
            part = jnp.dot(weights, latent, preferred_element_type=F32)
            for k in range(list_len):
                place, tile = spot(0, block, k)
                mask = mask_ref[k, me * blk_count + block]
                table_ref[0, place] = tile
                table_ref[2, place] = block * list_len + k
                table_ref[3, block * list_len + k] = mask
                there, its_tile = spot(1, block, k)
                table_ref[1, there] = its_tile
                masked = part[k * tile_rows : (k + 1) * tile_rows] * mask.astype(F32)
                masked = masked.astype(BF16)
                near_ref[jnp.minimum(place, near_spare)] = masked
                far_ref[jnp.where(place < near_spare, far_spare, place - near_spare)] = masked


def add_entries(total, table_ref, group, slots, kept, other, groups, first):
    for slot in range(slots):
        place = group * slots + slot
        total[table_ref[0, place]] += kept[place].astype(F32)
        total[table_ref[1, groups * slots + place]] += other[place + first * slots].astype(F32)


def far_kernel(group, slots, groups, table_ref, kept, other, *rest):
    out, _, total = rest[-3:]
    total[...] = jnp.zeros_like(total)
    add_entries(total, table_ref, group, slots, kept, other, groups, 2 - groups)
    out[...] = total[...].astype(BF16)


def own_kernel(slots, groups, table_ref, kept, other, own):
    group = pl.program_id(0)
    total = own.at[group]
    total[...] = jnp.zeros_like(total)
    add_entries(total, table_ref, group, slots, kept, other, groups, groups)


def add_kernel(group, own, came, token, out):
    del token
    out[...] = (own[group] + came[...].astype(F32)).astype(BF16)


def mesh_kernel(
    latent_ref, up_ref, down_ref, gain_ref, own, came, neighbour, out_ref, first_ref, second_ref
):
    total = own[0] + came[...].astype(F32) + neighbour[...].astype(F32)
    mesh_in = latent_ref[...].astype(F32) + total.reshape(latent_ref.shape)
    normed = layer_norm(mesh_in, gain_ref[...]).astype(BF16)
    hidden = silu(jnp.dot(normed, up_ref[...], preferred_element_type=F32)).astype(BF16)
    out = (mesh_in + jnp.dot(hidden, down_ref[...], preferred_element_type=F32)).astype(BF16)
    out_ref[...] = out
    first_ref[...] = out
    second_ref[...] = out


def order_kernel(*refs):
    del refs


def pick_kernel(chosen, slots, groups, tile_rows, table_ref, *refs):
    pieces, outs = refs[:-2], refs[-2:]
    for number, group in enumerate(chosen):
        for slot in range(slots):
            for way, out in enumerate(outs):
                tile = table_ref[way, (way * groups + group) * slots + slot]
                rows = pl.ds(pl.multiple_of(tile * tile_rows, tile_rows), tile_rows)
                into = (number * slots + slot) * tile_rows
                out[into : into + tile_rows] = pieces[number][rows]


def turn_kernel(interp_ref, token, out_ref):
    del token
    for b in range(interp_ref.shape[0]):
        out_ref[b] = interp_ref[b].reshape(out_ref.shape[2], out_ref.shape[1]).T


def join_kernel(slots, groups, tile_rows, table_ref, *refs):
    parts, out = refs[:-1], refs[-1]
    for across in range(N_CORE):
        place = across * groups * slots
        for part in parts[across * len(parts) // N_CORE : (across + 1) * len(parts) // N_CORE]:
            for start in range(0, part.shape[0], tile_rows):
                entry = table_ref[2, place]
                value = part[start : start + tile_rows]
                listed = table_ref[3, entry] == 1
                rows = pl.ds(pl.multiple_of(entry * tile_rows, tile_rows), tile_rows)
                out[rows] = jnp.where(listed, value, jnp.zeros_like(value))
                place += 1


def back_kernel(
    slots, groups, list_len, table_ref, weights_ref, tiles_ref, mine_ref, theirs_ref, latent_any,
    out_any, same, latent_ref, total, out_ref, sems,
):
    del same
    blk_count, block_rows, listed = weights_ref.shape
    tile_rows = listed // list_len
    part_rows = BACK_PART * block_rows
    parts = [pl.ds(i * part_rows, part_rows) for i in range(blk_count // BACK_PART)]
    latent_in, outs = [], []
    for i, rows in enumerate(parts):
        latent_in.append(
            pltpu.make_async_copy(latent_any.at[rows], latent_ref.at[rows], sems.at[i])
        )
        outs.append(
            pltpu.make_async_copy(out_ref.at[rows], out_any.at[rows], sems.at[len(parts) + i])
        )
    for copy in latent_in:
        copy.start()

    def rows_at(tile):
        return pl.ds(pl.multiple_of(tile * tile_rows, tile_rows), tile_rows)

    for across, block_ref in enumerate((mine_ref, theirs_ref)):
        for slot in range(slots):
            place = ((across + 1) * groups - 1) * slots + slot
            entry = table_ref[2, place]
            value = block_ref[rows_at(table_ref[0, place])]
            value = jnp.where(table_ref[3, entry] == 1, value, jnp.zeros_like(value))
            tiles_ref[rows_at(entry)] = value

    for block in range(blk_count):
        value = tiles_ref[block * listed : (block + 1) * listed]
        rows = slice(block * block_rows, (block + 1) * block_rows)
        total[rows] = jnp.dot(weights_ref[block], value, preferred_element_type=F32)
        if block % BACK_PART == 0:
            latent_in[block // BACK_PART].wait()
        for strip in strips(rows):
            out_ref[strip] = (latent_ref[strip].astype(F32) + total[strip]).astype(BF16)
        if block % BACK_PART == BACK_PART - 1:
            outs[block // BACK_PART].start()
    for copy in outs:
        copy.wait()


def whole(array):
    zeros = (0,) * array.ndim
    return pl.BlockSpec(array.shape, lambda *_: zeros)


def params(mib):
    return pltpu.CompilerParams(vmem_limit_bytes=mib * 1024 * 1024)


def cost(flops, *arrays):
    size = sum(a.size * a.dtype.itemsize for a in arrays)
    return pl.CostEstimate(flops=int(flops), bytes_accessed=int(size), transcendentals=0)


def shape(dims, kind=BF16):
    return jax.ShapeDtypeStruct(dims, kind)


def on_device(
    n_y,
    grid_features,
    mesh_latent,
    embed_in,
    embed_out,
    embed_gain,
    interp,
    block_mask,
    tile_list,
    mesh_up,
    mesh_down,
    mesh_gain,
):
    n_band = lax.axis_size("band")
    blk_count, list_len, tile_rows, block_rows = interp.shape
    channels, width = embed_in.shape
    node_rows = mesh_latent.shape[0]
    tiles = node_rows // tile_rows
    entries = blk_count * list_len
    slots = entries // n_band
    ring = Ring(n_band, n_y, tiles)
    chips, far = ring.chips, ring.far
    lists = (lax.axis_index("band").reshape(1), tile_list.T, block_mask.T)

    def in_hbm(array):
        return pltpu.with_memory_space_constraint(array, pltpu.HBM)

    gain = embed_gain.reshape(1, width)
    in_vmem = pl.BlockSpec(memory_space=pltpu.VMEM)
    in_any = pl.BlockSpec(memory_space=pl.ANY)
    grid_rows = blk_count * block_rows
    per_step = 4
    rows = per_step * block_rows
    counts = ((2 * chips - 2) * slots, 2 * slots)
    latent, near, sent_far, table = pl.pallas_call(
        functools.partial(embed_kernel, ring, per_step, slots),
        out_shape=[pltpu.HBM((blk_count * block_rows, width), BF16)]
        + [shape((count + 1, tile_rows, width)) for count in counts]
        + [shape((4, entries), jnp.int32)],
        grid_spec=pltpu.PrefetchScalarGridSpec(
            num_scalar_prefetch=3,
            grid=(blk_count // per_step,),
            in_specs=[
                pl.BlockSpec((channels, rows), lambda i, *_: (0, i)),
                whole(embed_in),
                whole(embed_out),
                whole(gain),
                pl.BlockSpec((per_step,) + interp.shape[1:], lambda i, *_: (i, 0, 0, 0)),
            ],
            out_specs=[pl.BlockSpec((rows, width), lambda i, *_: (i, 0))]
            + [pl.BlockSpec(memory_space=pltpu.VMEM)] * len(counts)
            + [pl.BlockSpec(memory_space=pltpu.SMEM)],
            scratch_shapes=[
                pltpu.VMEM((rows, width), F32),
                pltpu.VMEM((rows, width), BF16),
                pltpu.SMEM((2, n_band), jnp.int32),
            ],
        ),
        compiler_params=params(24),
        cost_estimate=cost(
            2 * blk_count * block_rows * width * (channels + width + list_len * tile_rows),
            grid_features,
            interp,
        ),
        name="embed",
    )(lists[0], *map(in_hbm, lists[1:] + (grid_features.T, embed_in, embed_out, gain, interp)))
    other_far = ring.over_core(sent_far)

    dense = (tiles, tile_rows, width)

    def in_order(value, token):
        return pl.pallas_call(
            order_kernel,
            out_shape=shape(value.shape),
            in_specs=[in_any] * 2,
            out_specs=in_any,
            input_output_aliases={0: 0},
            compiler_params=params(1),
            cost_estimate=cost(0),
            name="in_order",
        )(value, token)


    def far_sums(group, near, *token):
        handed, spec = (token[0], in_any) if token else (near, in_vmem)
        return pl.pallas_call(
            functools.partial(far_kernel, group, slots, chips),
            out_shape=[shape(dense), shape(handed.shape)],
            grid_spec=pltpu.PrefetchScalarGridSpec(
                num_scalar_prefetch=1,
                grid=(1,),
                in_specs=[in_vmem] * 2 + [in_any] * len(token),
                out_specs=[in_vmem, spec],
                scratch_shapes=[pltpu.VMEM(dense, F32)],
            ),
            input_output_aliases={3 if token else 1: 1},
            compiler_params=params(8),
            cost_estimate=cost(0),
            name=f"far_{group}",
        )(table, near, other_far, *token)

    first, near = far_sums(chips - 1, near)
    first = ring.over_first(first, far)
    second, other = far_sums(chips - 2, near, ring.over_core(near))
    second = ring.over_second(second, far - 1)
    own = pl.pallas_call(
        functools.partial(own_kernel, slots, chips),
        out_shape=shape((chips - 2,) + dense, F32),
        grid_spec=pltpu.PrefetchScalarGridSpec(
            num_scalar_prefetch=1,
            grid=(chips - 2,),
            in_specs=[in_vmem] * 2,
            out_specs=in_vmem,
        ),
        compiler_params=params(8 if n_band <= 16 else 24),
        cost_estimate=cost(0, near, near),
        name="own_sums",
    )(table, near, other)

    def add_own(group, value, token):
        return pl.pallas_call(
            functools.partial(add_kernel, group),
            out_shape=shape(dense),
            in_specs=[in_vmem] * 2 + [in_any],
            out_specs=in_vmem,
            compiler_params=params(8),
            cost_estimate=cost(0),
            name=f"add_{group}",
        )(own, value, token)

    turned = (blk_count, block_rows, list_len * tile_rows)
    per_step = 4
    token = weights = pl.pallas_call(
        turn_kernel,
        out_shape=shape(turned),
        grid=(blk_count // per_step,),
        in_specs=[pl.BlockSpec((per_step,) + interp.shape[1:], lambda i: (i, 0, 0, 0)), in_any],
        out_specs=pl.BlockSpec((per_step,) + turned[1:], lambda i: (i, 0, 0)),
        compiler_params=params(8),
        cost_estimate=cost(0, interp, interp),
        name="turn",
    )(interp, own)
    for group in range(chips - 3, 0, -1):
        distance = (group + 1) // 2
        if group % 2:
            token = add_own(group, first, token)
            first = ring.over_first(token, distance)
        else:
            token = add_own(group, second, token)
            second = ring.over_second(token, distance)

    mesh_gain = mesh_gain.reshape(1, width)
    mesh_out, piece, again = pl.pallas_call(
        mesh_kernel,
        out_shape=[shape((node_rows, width))] * 3,
        in_specs=[in_vmem] * 7,
        out_specs=[in_vmem] * 3,
        compiler_params=params(16),
        cost_estimate=cost(4 * node_rows * width * width, mesh_up, mesh_down),
        name="mesh_step",
    )(mesh_latent, mesh_up, mesh_down, mesh_gain, own, first, second)

    mine, theirs = [], []

    def pick(chosen, values):
        out = shape((len(chosen) * slots * tile_rows, width))
        picked = pl.pallas_call(
            functools.partial(pick_kernel, chosen, slots, chips, tile_rows),
            out_shape=[out] * 2,
            grid_spec=pltpu.PrefetchScalarGridSpec(
                num_scalar_prefetch=1,
                grid=(1,),
                in_specs=[in_vmem] * len(values),
                out_specs=[in_vmem] * 2,
            ),
            compiler_params=params(8),
            cost_estimate=cost(0, *values),
            name=f"pick_{chosen[0]}",
        )(table, *values)
        mine.append(picked[0])
        theirs.append(ring.over_core(picked[1]))

    first = ring.over_first(piece, 1)
    pick([0], [piece])
    second = ring.over_second(in_order(again, theirs[0]), 1)
    token = mine[0]
    for distance in range(1, far):
        first = in_order(first, token)
        onward = ring.over_first(first, distance + 1)
        second = in_order(second, first)
        if distance < far - 1:
            after = ring.over_second(second, distance + 1)
        pick([2 * distance - 1, 2 * distance], [first, second])
        token = mine[-1]
        first, second = onward, after
    tiles_far = [first, ring.over_core(first)]
    parts = mine + theirs
    by_entry = shape((entries * tile_rows, width))
    joined = pl.pallas_call(
        functools.partial(join_kernel, slots, chips, tile_rows),
        out_shape=by_entry,
        grid_spec=pltpu.PrefetchScalarGridSpec(
            num_scalar_prefetch=1,
            grid=(1,),
            in_specs=[in_vmem] * len(parts),
            out_specs=in_vmem,
        ),
        compiler_params=params(8),
        cost_estimate=cost(0, *parts),
        name="join",
    )(table, *parts)

    grid_out, _ = pl.pallas_call(
        functools.partial(back_kernel, slots, chips, list_len),
        out_shape=[shape((grid_rows, width)), by_entry],
        grid_spec=pltpu.PrefetchScalarGridSpec(
            num_scalar_prefetch=1,
            grid=(1,),
            in_specs=[in_vmem] * 4 + [in_any],
            out_specs=[in_any, in_vmem],
            scratch_shapes=[
                pltpu.VMEM((grid_rows, width), BF16),
                pltpu.VMEM((grid_rows, width), F32),
                pltpu.VMEM((grid_rows, width), BF16),
                pltpu.SemaphoreType.DMA((2 * (blk_count // BACK_PART),)),
            ],
        ),
        input_output_aliases={2: 1},
        compiler_params=params(32),
        cost_estimate=cost(2 * grid_rows * width * list_len * tile_rows, latent, latent, interp),
        name="back",
    )(table, weights, joined, *tiles_far, in_hbm(latent))
    return (grid_out, mesh_out)


def solution(mesh):
    placed = (
        P(("groups", "band"), None),
        P(("groups", "band"), None),
        P(),
        P(),
        P(),
        P("band", None, None, None),
        P(),
        P(),
        P(),
        P(),
        P(),
    )
    n_y = max(1, 4 // mesh.shape["groups"])
    return jax.shard_map(
        functools.partial(on_device, n_y),
        mesh=mesh,
        in_specs=placed,
        out_specs=(P(("groups", "band"), None), P(("groups", "band"), None)),
        check_vma=False,
    )
```

```python
import functools

import jax
import jax.numpy as jnp
from jax import lax
from jax.experimental import pallas as pl
from jax.experimental.pallas import tpu as pltpu
from jax.sharding import PartitionSpec as P

F32 = jnp.float32
BF16 = jnp.bfloat16
N_CORE = 2
STRIP = 32
PART = 2
BACK_PART = 4


def silu(values):
    half = 0.5 * values
    return half * (1.0 + jnp.tanh(half))


def layer_norm(values, gain):
    centred = values - jnp.mean(values, axis=-1, keepdims=True)
    spread = jnp.mean(centred * centred, axis=-1, keepdims=True)
    return centred * lax.rsqrt(spread + 1e-05) * gain


def split(value, size):
    if size & (size - 1) == 0:
        return lax.shift_right_logical(value, size.bit_length() - 1), value & (size - 1)
    return lax.div(value, size), lax.rem(value, size)


class Ring:
    def __init__(self, n_band, n_y, tiles):
        self.n_band, self.n_y, self.tiles = n_band, n_y, tiles
        self.chips = n_band // N_CORE
        self.far = self.chips // 2

    def place(self, index):
        chip, core = split(index, N_CORE)
        z, y = split(chip, self.n_y)
        return z + y * (self.chips - 1 - 2 * z), core

    def index(self, ring, core):
        ring = ring % self.chips
        n_z = self.chips // self.n_y
        z, y = (ring, 0) if ring < n_z else (self.chips - 1 - ring, 1)
        return (z * self.n_y + y) * N_CORE + core

    def over_core(self, value):
        return lax.ppermute(value, "band", [(i, i ^ 1) for i in range(self.n_band)])

    def over(self, value, right):
        pairs = []
        for i in range(self.n_band):
            chip, core = divmod(i, N_CORE)
            z, y = divmod(chip, self.n_y)
            ring = z if y == 0 else self.chips - 1 - z
            pairs.append((i, self.index(ring + (1 if core == right else -1), 1 - core)))
        return lax.ppermute(value, "band", pairs)

    def over_first(self, value, distance):
        return self.over(value, distance % 2)

    def over_second(self, value, distance):
        return self.over(value, (distance + 1) % 2)

    def seen(self, owner, me):
        ring, core = self.place(owner)
        my_ring, my_core = self.place(me)
        ahead = split(ring - my_ring + self.chips, self.chips)[1]
        left = (ahead > self.far).astype(jnp.int32)
        distance = jnp.where(ahead > self.far, self.chips - ahead, ahead)
        shared = (ahead == 0) | (ahead == self.far)
        stream = jnp.where(shared, 0, core ^ left)
        group = jnp.maximum(2 * distance - 1 + stream, 0)
        return ((distance + core) & 1) ^ my_core, group


def strips(rows):
    return [slice(r, r + STRIP) for r in range(rows.start, rows.stop, STRIP)]


def embed_kernel(
    ring, per_step, slots, me_ref, lists_ref, mask_ref,
    x_ref, w1_ref, w2_ref, gain_ref, interp_ref,
    latent_ref, near_ref, far_ref, table_ref, wide, hidden, owners_ref, places_ref,
):
    step = pl.program_id(0)
    me = me_ref[0]
    list_len, tile_rows, block_rows = interp_ref.shape[1:]
    blk_count = pl.num_programs(0) * per_step
    groups = ring.chips

    @pl.when(step == 0)
    def _():
        def note(owner, carry):
            across, group = ring.seen(owner, me)
            owners_ref[0, owner] = (across * groups + group) * slots
            owners_ref[1, owner] = ((across ^ 1) * groups + group) * slots
            return carry

        lax.fori_loop(0, ring.n_band, note, 0)

    def spot(who, block, k):
        owner, tile = split(lists_ref[k, (me ^ who) * blk_count + block], ring.tiles)
        slot = split(block * list_len + k, ring.n_band)[0]
        return owners_ref[who, owner] + slot, tile

    near_spare, far_spare = near_ref.shape[0] - 1, far_ref.shape[0] - 1
    for b in range(per_step):
        block = step * per_step + b
        for k in range(list_len):
            entry = block * list_len + k
            place, tile = spot(0, block, k)
            mask = mask_ref[k, me * blk_count + block]
            table_ref[0, place] = tile
            across = (place >= groups * slots).astype(jnp.int32)
            near = place - across * slots
            beyond = place - across * groups * slots >= (groups - 1) * slots
            table_ref[2, entry] = jnp.where(beyond, tile, near)
            table_ref[3, entry] = mask * jnp.where(beyond, 2 + across, 1)
            there, its_tile = spot(1, block, k)
            table_ref[1, there] = its_tile
            places_ref[0, b * list_len + k] = jnp.minimum(place, near_spare)
            places_ref[1, b * list_len + k] = jnp.where(
                place < near_spare, far_spare, place - near_spare
            )
            places_ref[2, b * list_len + k] = mask

    part_rows = PART * block_rows
    spans = [slice(i * part_rows, (i + 1) * part_rows) for i in range(per_step // PART)]
    for rows in spans:
        wide[rows] = lax.dot_general(
            x_ref[:, rows], w1_ref[...], (((0,), (0,)), ((), ())), preferred_element_type=F32
        )
    for rows in spans:
        for strip in strips(rows):
            hidden[strip] = silu(wide[strip]).astype(BF16)
        wide[rows] = jnp.dot(hidden[rows], w2_ref[...], preferred_element_type=F32)
    for number, rows in enumerate(spans):
        for strip in strips(rows):
            latent_ref[strip] = layer_norm(wide[strip], gain_ref[...]).astype(BF16)
        for b in range(number * PART, (number + 1) * PART):
            weights = interp_ref[b].reshape(list_len * tile_rows, block_rows)
            latent = latent_ref[b * block_rows : (b + 1) * block_rows]
            part = jnp.dot(weights, latent, preferred_element_type=F32)
            for k in range(list_len):
                number_here = b * list_len + k
                mask = places_ref[2, number_here].astype(F32)
                masked = (part[k * tile_rows : (k + 1) * tile_rows] * mask).astype(BF16)
                near_ref[places_ref[0, number_here]] = masked
                far_ref[places_ref[1, number_here]] = masked


def add_entries(total, table_ref, group, slots, kept, other, groups, first):
    for slot in range(slots):
        place = group * slots + slot
        total[table_ref[0, place]] += kept[place].astype(F32)
        total[table_ref[1, groups * slots + place]] += other[place + first * slots].astype(F32)


def far_kernel(slots, groups, table_ref, kept, other, far, before, same, total):
    del same
    for group, out in ((groups - 1, far), (groups - 2, before)):
        total[...] = jnp.zeros_like(total)
        add_entries(total, table_ref, group, slots, kept, other, groups, 2 - groups)
        out[...] = total[...].astype(BF16)


def own_kernel(slots, groups, table_ref, kept, other, own):
    group = pl.program_id(0)
    total = own.at[group]
    total[...] = jnp.zeros_like(total)
    add_entries(total, table_ref, group, slots, kept, other, groups, groups)


def add_kernel(group, own, came, token, out):
    del token
    out[...] = (own[group] + came[...].astype(F32)).astype(BF16)


def mesh_kernel(
    latent_ref, up_ref, down_ref, gain_ref, own, came, neighbour, first_ref, second_ref
):
    total = own[0] + came[...].astype(F32) + neighbour[...].astype(F32)
    mesh_in = latent_ref[...].astype(F32) + total.reshape(latent_ref.shape)
    normed = layer_norm(mesh_in, gain_ref[...]).astype(BF16)
    hidden = silu(jnp.dot(normed, up_ref[...], preferred_element_type=F32)).astype(BF16)
    out = (mesh_in + jnp.dot(hidden, down_ref[...], preferred_element_type=F32)).astype(BF16)
    first_ref[...] = out
    second_ref[...] = out


def order_kernel(*refs):
    del refs


def pick_kernel(chosen, slots, groups, tile_rows, table_ref, *refs):
    pieces, outs = refs[: len(chosen)], refs[len(chosen) :]
    for out in outs[2:]:
        out[...] = pieces[0][...]
    for number, group in enumerate(chosen):
        for slot in range(slots):
            for way, out in enumerate(outs[:2]):
                tile = table_ref[way, (way * groups + group) * slots + slot]
                rows = pl.ds(pl.multiple_of(tile * tile_rows, tile_rows), tile_rows)
                into = (number * slots + slot) * tile_rows
                out[into : into + tile_rows] = pieces[number][rows]


def turn_kernel(interp_ref, token, out_ref):
    del token
    for b in range(interp_ref.shape[0]):
        out_ref[b] = interp_ref[b].reshape(out_ref.shape[2], out_ref.shape[1]).T


def join_kernel(*refs):
    pieces, out = refs[:-1], refs[-1]
    start = 0
    for piece in pieces:
        out[start : start + piece.shape[0]] = piece[...]
        start += piece.shape[0]


def back_kernel(
    list_len, table_ref, weights_ref, near_ref, mine_ref, theirs_ref, latent_any,
    out_any, latent_ref, total, out_ref, sems,
):
    blk_count, block_rows, listed = weights_ref.shape
    tile_rows = listed // list_len
    part_rows = BACK_PART * block_rows
    parts = [pl.ds(i * part_rows, part_rows) for i in range(blk_count // BACK_PART)]
    latent_in, outs = [], []
    for i, rows in enumerate(parts):
        latent_in.append(
            pltpu.make_async_copy(latent_any.at[rows], latent_ref.at[rows], sems.at[i])
        )
        outs.append(
            pltpu.make_async_copy(out_ref.at[rows], out_any.at[rows], sems.at[len(parts) + i])
        )
    for copy in latent_in:
        copy.start()

    def rows_at(tile):
        return pl.ds(pl.multiple_of(tile * tile_rows, tile_rows), tile_rows)

    for block in range(blk_count):
        values = []
        for k in range(list_len):
            entry = block * list_len + k
            place, kind = table_ref[2, entry], table_ref[3, entry]
            here = jnp.where(kind > 1, 0, place)
            beyond = jnp.where(kind > 1, place, 0)
            value = near_ref[rows_at(here)]
            value = jnp.where(kind == 2, mine_ref[rows_at(beyond)], value)
            value = jnp.where(kind == 3, theirs_ref[rows_at(beyond)], value)
            values.append(jnp.where(kind > 0, value, jnp.zeros_like(value)))
        value = jnp.concatenate(values, axis=0)
        rows = slice(block * block_rows, (block + 1) * block_rows)
        total[rows] = jnp.dot(weights_ref[block], value, preferred_element_type=F32)
        if block % BACK_PART == 0:
            latent_in[block // BACK_PART].wait()
        for strip in strips(rows):
            out_ref[strip] = (latent_ref[strip].astype(F32) + total[strip]).astype(BF16)
        if block % BACK_PART == BACK_PART - 1:
            outs[block // BACK_PART].start()
    for copy in outs:
        copy.wait()


def whole(array):
    zeros = (0,) * array.ndim
    return pl.BlockSpec(array.shape, lambda *_: zeros)


def params(mib):
    return pltpu.CompilerParams(vmem_limit_bytes=mib * 1024 * 1024)


def cost(flops, *arrays):
    size = sum(a.size * a.dtype.itemsize for a in arrays)
    return pl.CostEstimate(flops=int(flops), bytes_accessed=int(size), transcendentals=0)


def shape(dims, kind=BF16):
    return jax.ShapeDtypeStruct(dims, kind)


def on_device(
    n_y,
    grid_features,
    mesh_latent,
    embed_in,
    embed_out,
    embed_gain,
    interp,
    block_mask,
    tile_list,
    mesh_up,
    mesh_down,
    mesh_gain,
):
    n_band = lax.axis_size("band")
    blk_count, list_len, tile_rows, block_rows = interp.shape
    channels, width = embed_in.shape
    node_rows = mesh_latent.shape[0]
    tiles = node_rows // tile_rows
    entries = blk_count * list_len
    slots = entries // n_band
    ring = Ring(n_band, n_y, tiles)
    chips, far = ring.chips, ring.far
    lists = (lax.axis_index("band").reshape(1), tile_list.T, block_mask.T)

    def in_hbm(array):
        return pltpu.with_memory_space_constraint(array, pltpu.HBM)

    gain = embed_gain.reshape(1, width)
    in_vmem = pl.BlockSpec(memory_space=pltpu.VMEM)
    in_any = pl.BlockSpec(memory_space=pl.ANY)
    grid_rows = blk_count * block_rows
    per_step = 4
    rows = per_step * block_rows
    counts = ((2 * chips - 2) * slots, 2 * slots)
    latent, near, sent_far, table = pl.pallas_call(
        functools.partial(embed_kernel, ring, per_step, slots),
        out_shape=[pltpu.HBM((blk_count * block_rows, width), BF16)]
        + [shape((count + 1, tile_rows, width)) for count in counts]
        + [shape((4, entries), jnp.int32)],
        grid_spec=pltpu.PrefetchScalarGridSpec(
            num_scalar_prefetch=3,
            grid=(blk_count // per_step,),
            in_specs=[
                pl.BlockSpec((channels, rows), lambda i, *_: (0, i)),
                whole(embed_in),
                whole(embed_out),
                whole(gain),
                pl.BlockSpec((per_step,) + interp.shape[1:], lambda i, *_: (i, 0, 0, 0)),
            ],
            out_specs=[pl.BlockSpec((rows, width), lambda i, *_: (i, 0))]
            + [pl.BlockSpec(memory_space=pltpu.VMEM)] * len(counts)
            + [pl.BlockSpec(memory_space=pltpu.SMEM)],
            scratch_shapes=[
                pltpu.VMEM((rows, width), F32),
                pltpu.VMEM((rows, width), BF16),
                pltpu.SMEM((2, n_band), jnp.int32),
                pltpu.SMEM((3, per_step * list_len), jnp.int32),
            ],
        ),
        compiler_params=params(24),
        cost_estimate=cost(
            2 * blk_count * block_rows * width * (channels + width + list_len * tile_rows),
            grid_features,
            interp,
        ),
        name="embed",
    )(lists[0], *map(in_hbm, lists[1:] + (grid_features.T, embed_in, embed_out, gain, interp)))
    other_far = ring.over_core(sent_far)

    dense = (tiles, tile_rows, width)

    def in_order(value, token):
        return pl.pallas_call(
            order_kernel,
            out_shape=shape(value.shape),
            in_specs=[in_any] * 2,
            out_specs=in_any,
            input_output_aliases={0: 0},
            compiler_params=params(1),
            cost_estimate=cost(0),
            name="in_order",
        )(value, token)

    first, second, near = pl.pallas_call(
        functools.partial(far_kernel, slots, chips),
        out_shape=[shape(dense)] * 2 + [shape(near.shape)],
        grid_spec=pltpu.PrefetchScalarGridSpec(
            num_scalar_prefetch=1,
            grid=(1,),
            in_specs=[in_vmem] * 2,
            out_specs=[in_vmem] * 3,
            scratch_shapes=[pltpu.VMEM(dense, F32)],
        ),
        input_output_aliases={1: 2},
        compiler_params=params(8),
        cost_estimate=cost(0, near),
        name="far_sums",
    )(table, near, other_far)
    other = ring.over_core(near)
    own = pl.pallas_call(
        functools.partial(own_kernel, slots, chips),
        out_shape=shape((chips - 2,) + dense, F32),
        grid_spec=pltpu.PrefetchScalarGridSpec(
            num_scalar_prefetch=1,
            grid=(chips - 2,),
            in_specs=[in_vmem] * 2,
            out_specs=in_vmem,
        ),
        compiler_params=params(8 if n_band <= 16 else 24),
        cost_estimate=cost(0, near, near),
        name="own_sums",
    )(table, near, other)

    def add_own(group, value, token):
        return pl.pallas_call(
            functools.partial(add_kernel, group),
            out_shape=shape(dense),
            in_specs=[in_vmem] * 2 + [in_any],
            out_specs=in_vmem,
            compiler_params=params(8),
            cost_estimate=cost(0),
            name=f"add_{group}",
        )(own, value, token)

    first, second = ring.over_first(first, far), ring.over_second(second, far - 1)
    turned = (blk_count, block_rows, list_len * tile_rows)
    per_step = 4
    token = weights = pl.pallas_call(
        turn_kernel,
        out_shape=shape(turned),
        grid=(blk_count // per_step,),
        in_specs=[pl.BlockSpec((per_step,) + interp.shape[1:], lambda i: (i, 0, 0, 0)), in_any],
        out_specs=pl.BlockSpec((per_step,) + turned[1:], lambda i: (i, 0, 0)),
        compiler_params=params(8),
        cost_estimate=cost(0, interp, interp),
        name="turn",
    )(interp, own)
    for group in range(chips - 3, 0, -1):
        distance = (group + 1) // 2
        if group % 2:
            token = add_own(group, first, token)
            first = ring.over_first(token, distance)
        else:
            token = add_own(group, second, token)
            second = ring.over_second(token, distance)

    mesh_gain = mesh_gain.reshape(1, width)
    piece, again = pl.pallas_call(
        mesh_kernel,
        out_shape=[shape((node_rows, width))] * 2,
        in_specs=[in_vmem] * 7,
        out_specs=[in_vmem] * 2,
        compiler_params=params(16),
        cost_estimate=cost(4 * node_rows * width * width, mesh_up, mesh_down),
        name="mesh_step",
    )(mesh_latent, mesh_up, mesh_down, mesh_gain, own, first, second)

    mine, theirs = [], []

    def pick(chosen, values):
        outs = [shape((len(chosen) * slots * tile_rows, width))] * 2
        if chosen == [0]:
            outs.append(shape((node_rows, width)))
        picked = pl.pallas_call(
            functools.partial(pick_kernel, chosen, slots, chips, tile_rows),
            out_shape=outs,
            grid_spec=pltpu.PrefetchScalarGridSpec(
                num_scalar_prefetch=1,
                grid=(1,),
                in_specs=[in_vmem] * len(values),
                out_specs=[in_vmem] * len(outs),
            ),
            compiler_params=params(8),
            cost_estimate=cost(0, *values),
            name=f"pick_{chosen[0]}",
        )(table, *values)
        mine.append(picked[0])
        theirs.append(ring.over_core(picked[1]))
        return picked[-1]

    first = ring.over_first(piece, 1)
    mesh_out = pick([0], [piece])
    second = ring.over_second(in_order(again, theirs[0]), 1)
    token = mine[0]
    for distance in range(1, far):
        first = in_order(first, token)
        onward = ring.over_first(first, distance + 1)
        second = in_order(second, first)
        if distance < far - 1:
            after = ring.over_second(second, distance + 1)
        pick([2 * distance - 1, 2 * distance], [first, second])
        token = mine[-1]
        first, second = onward, after
    tiles_far = [first, ring.over_core(first)]
    parts = mine + theirs
    joined = pl.pallas_call(
        join_kernel,
        out_shape=shape((sum(part.shape[0] for part in parts), width)),
        in_specs=[in_vmem] * len(parts),
        out_specs=in_vmem,
        compiler_params=params(8),
        cost_estimate=cost(0, *parts),
        name="join",
    )(*parts)

    grid_out = pl.pallas_call(
        functools.partial(back_kernel, list_len),
        out_shape=shape((grid_rows, width)),
        grid_spec=pltpu.PrefetchScalarGridSpec(
            num_scalar_prefetch=1,
            grid=(1,),
            in_specs=[in_vmem] * 4 + [in_any],
            out_specs=in_any,
            scratch_shapes=[
                pltpu.VMEM((grid_rows, width), BF16),
                pltpu.VMEM((grid_rows, width), F32),
                pltpu.VMEM((grid_rows, width), BF16),
                pltpu.SemaphoreType.DMA((2 * (blk_count // BACK_PART),)),
            ],
        ),
        compiler_params=params(32),
        cost_estimate=cost(2 * grid_rows * width * list_len * tile_rows, latent, latent, interp),
        name="back",
    )(table, weights, joined, *tiles_far, in_hbm(latent))
    return (grid_out, mesh_out)


def solution(mesh):
    placed = (
        P(("groups", "band"), None),
        P(("groups", "band"), None),
        P(),
        P(),
        P(),
        P("band", None, None, None),
        P(),
        P(),
        P(),
        P(),
        P(),
    )
    n_y = max(1, 4 // mesh.shape["groups"])
    return jax.shard_map(
        functools.partial(on_device, n_y),
        mesh=mesh,
        in_specs=placed,
        out_specs=(P(("groups", "band"), None), P(("groups", "band"), None)),
        check_vma=False,
    )
```

```python
import functools

import jax
import jax.numpy as jnp
from jax import lax
from jax.experimental import pallas as pl
from jax.experimental.pallas import tpu as pltpu
from jax.sharding import PartitionSpec as P

F32 = jnp.float32
BF16 = jnp.bfloat16
N_CORE = 2
STRIP = 32
PART = 4
BACK_PART = 4


def silu(values):
    half = 0.5 * values
    return half * (1.0 + jnp.tanh(half))


def layer_norm(values, gain):
    centred = values - jnp.mean(values, axis=-1, keepdims=True)
    spread = jnp.mean(centred * centred, axis=-1, keepdims=True)
    return centred * lax.rsqrt(spread + 1e-05) * gain


def split(value, size):
    if size & (size - 1) == 0:
        return lax.shift_right_logical(value, size.bit_length() - 1), value & (size - 1)
    return lax.div(value, size), lax.rem(value, size)


class Ring:
    def __init__(self, n_band, n_y, tiles):
        self.n_band, self.n_y, self.tiles = n_band, n_y, tiles
        self.chips = n_band // N_CORE
        self.far = self.chips // 2

    def place(self, index):
        chip, core = split(index, N_CORE)
        z, y = split(chip, self.n_y)
        return z + y * (self.chips - 1 - 2 * z), core

    def index(self, ring, core):
        ring = ring % self.chips
        n_z = self.chips // self.n_y
        z, y = (ring, 0) if ring < n_z else (self.chips - 1 - ring, 1)
        return (z * self.n_y + y) * N_CORE + core

    def over_core(self, value):
        return lax.ppermute(value, "band", [(i, i ^ 1) for i in range(self.n_band)])

    def over(self, value, right):
        pairs = []
        for i in range(self.n_band):
            chip, core = divmod(i, N_CORE)
            z, y = divmod(chip, self.n_y)
            ring = z if y == 0 else self.chips - 1 - z
            pairs.append((i, self.index(ring + (1 if core == right else -1), 1 - core)))
        return lax.ppermute(value, "band", pairs)

    def over_first(self, value, distance):
        return self.over(value, distance % 2)

    def over_second(self, value, distance):
        return self.over(value, (distance + 1) % 2)

    def seen(self, owner, me):
        ring, core = self.place(owner)
        my_ring, my_core = self.place(me)
        ahead = split(ring - my_ring + self.chips, self.chips)[1]
        left = (ahead > self.far).astype(jnp.int32)
        distance = jnp.where(ahead > self.far, self.chips - ahead, ahead)
        shared = (ahead == 0) | (ahead == self.far)
        stream = jnp.where(shared, 0, core ^ left)
        group = jnp.maximum(2 * distance - 1 + stream, 0)
        return ((distance + core) & 1) ^ my_core, group


def strips(rows):
    return [slice(r, r + STRIP) for r in range(rows.start, rows.stop, STRIP)]


def embed_kernel(
    ring, per_step, slots, me_ref, lists_ref, mask_ref,
    x_ref, w1_ref, w2_ref, gain_ref, interp_ref,
    latent_ref, near_ref, far_ref, table_ref, wide, hidden, owners_ref, places_ref,
):
    step = pl.program_id(0)
    me = me_ref[0]
    list_len, tile_rows, block_rows = interp_ref.shape[1:]
    blk_count = pl.num_programs(0) * per_step
    groups = ring.chips

    @pl.when(step == 0)
    def _():
        def note(owner, carry):
            across, group = ring.seen(owner, me)
            owners_ref[0, owner] = (across * groups + group) * slots
            owners_ref[1, owner] = ((across ^ 1) * groups + group) * slots
            return carry

        lax.fori_loop(0, ring.n_band, note, 0)

    def spot(who, block, k):
        owner, tile = split(lists_ref[k, (me ^ who) * blk_count + block], ring.tiles)
        slot = split(block * list_len + k, ring.n_band)[0]
        return owners_ref[who, owner] + slot, tile

    near_spare, far_spare = near_ref.shape[0] - 1, far_ref.shape[0] - 1
    for b in range(per_step):
        block = step * per_step + b
        for k in range(list_len):
            entry = block * list_len + k
            place, tile = spot(0, block, k)
            mask = mask_ref[k, me * blk_count + block]
            table_ref[0, place] = tile
            across = (place >= groups * slots).astype(jnp.int32)
            near = place - across * slots
            beyond = place - across * groups * slots >= (groups - 1) * slots
            table_ref[2, entry] = jnp.where(beyond, tile, near)
            table_ref[3, entry] = mask * jnp.where(beyond, 2 + across, 1)
            there, its_tile = spot(1, block, k)
            table_ref[1, there] = its_tile
            places_ref[0, b * list_len + k] = jnp.minimum(place, near_spare)
            places_ref[1, b * list_len + k] = jnp.where(
                place < near_spare, far_spare, place - near_spare
            )
            places_ref[2, b * list_len + k] = mask

    part_rows = PART * block_rows
    spans = [slice(i * part_rows, (i + 1) * part_rows) for i in range(per_step // PART)]
    for rows in spans:
        wide[rows] = lax.dot_general(
            x_ref[:, rows], w1_ref[...], (((0,), (0,)), ((), ())), preferred_element_type=F32
        )
    for rows in spans:
        for strip in strips(rows):
            hidden[strip] = silu(wide[strip]).astype(BF16)
        wide[rows] = jnp.dot(hidden[rows], w2_ref[...], preferred_element_type=F32)
    for number, rows in enumerate(spans):
        for strip in strips(rows):
            latent_ref[strip] = layer_norm(wide[strip], gain_ref[...]).astype(BF16)
        for b in range(number * PART, (number + 1) * PART):
            weights = interp_ref[b].reshape(list_len * tile_rows, block_rows)
            latent = latent_ref[b * block_rows : (b + 1) * block_rows]
            part = jnp.dot(weights, latent, preferred_element_type=F32)
            for k in range(list_len):
                number_here = b * list_len + k
                mask = places_ref[2, number_here].astype(F32)
                masked = (part[k * tile_rows : (k + 1) * tile_rows] * mask).astype(BF16)
                near_ref[places_ref[0, number_here]] = masked
                far_ref[places_ref[1, number_here]] = masked


def add_entries(total, table_ref, group, slots, kept, other, groups, first):
    for slot in range(slots):
        place = group * slots + slot
        total[table_ref[0, place]] += kept[place].astype(F32)
        total[table_ref[1, groups * slots + place]] += other[place + first * slots].astype(F32)


def far_kernel(slots, groups, table_ref, kept, other, far, before, same, total):
    del same
    for group, out in ((groups - 1, far), (groups - 2, before)):
        total[...] = jnp.zeros_like(total)
        add_entries(total, table_ref, group, slots, kept, other, groups, 2 - groups)
        out[...] = total[...].astype(BF16)


def own_kernel(slots, groups, table_ref, kept, other, own):
    group = pl.program_id(0)
    total = own.at[group]
    total[...] = jnp.zeros_like(total)
    add_entries(total, table_ref, group, slots, kept, other, groups, groups)


def add_kernel(group, own, came, token, out):
    del token
    out[...] = (own[group] + came[...].astype(F32)).astype(BF16)


def mesh_kernel(
    latent_ref, up_ref, down_ref, gain_ref, own, came, neighbour, first_ref, second_ref
):
    total = own[0] + came[...].astype(F32) + neighbour[...].astype(F32)
    mesh_in = latent_ref[...].astype(F32) + total.reshape(latent_ref.shape)
    normed = layer_norm(mesh_in, gain_ref[...]).astype(BF16)
    hidden = silu(jnp.dot(normed, up_ref[...], preferred_element_type=F32)).astype(BF16)
    out = (mesh_in + jnp.dot(hidden, down_ref[...], preferred_element_type=F32)).astype(BF16)
    first_ref[...] = out
    second_ref[...] = out


def order_kernel(*refs):
    del refs


def pick_kernel(chosen, slots, groups, tile_rows, table_ref, *refs):
    pieces, outs = refs[: len(chosen)], refs[len(chosen) :]
    for out in outs[2:]:
        out[...] = pieces[0][...]
    for number, group in enumerate(chosen):
        for slot in range(slots):
            for way, out in enumerate(outs[:2]):
                tile = table_ref[way, (way * groups + group) * slots + slot]
                rows = pl.ds(pl.multiple_of(tile * tile_rows, tile_rows), tile_rows)
                into = (number * slots + slot) * tile_rows
                out[into : into + tile_rows] = pieces[number][rows]


def turn_kernel(interp_ref, token, out_ref):
    del token
    for b in range(interp_ref.shape[0]):
        out_ref[b] = interp_ref[b].reshape(out_ref.shape[2], out_ref.shape[1]).T


def join_kernel(*refs):
    pieces, out = refs[:-1], refs[-1]
    start = 0
    for piece in pieces:
        out[start : start + piece.shape[0]] = piece[...]
        start += piece.shape[0]


def back_kernel(
    list_len, table_ref, weights_ref, near_ref, mine_ref, theirs_ref, latent_any,
    out_any, latent_ref, total, out_ref, sems,
):
    blk_count, block_rows, listed = weights_ref.shape
    tile_rows = listed // list_len
    part_rows = BACK_PART * block_rows
    parts = [pl.ds(i * part_rows, part_rows) for i in range(blk_count // BACK_PART)]
    latent_in, outs = [], []
    for i, rows in enumerate(parts):
        latent_in.append(
            pltpu.make_async_copy(latent_any.at[rows], latent_ref.at[rows], sems.at[i])
        )
        outs.append(
            pltpu.make_async_copy(out_ref.at[rows], out_any.at[rows], sems.at[len(parts) + i])
        )
    for copy in latent_in:
        copy.start()

    def rows_at(tile):
        return pl.ds(pl.multiple_of(tile * tile_rows, tile_rows), tile_rows)

    for block in range(blk_count):
        values = []
        for k in range(list_len):
            entry = block * list_len + k
            place, kind = table_ref[2, entry], table_ref[3, entry]
            here = jnp.where(kind > 1, 0, place)
            beyond = jnp.where(kind > 1, place, 0)
            value = near_ref[rows_at(here)]
            value = jnp.where(kind == 2, mine_ref[rows_at(beyond)], value)
            value = jnp.where(kind == 3, theirs_ref[rows_at(beyond)], value)
            values.append(jnp.where(kind > 0, value, jnp.zeros_like(value)))
        value = jnp.concatenate(values, axis=0)
        rows = slice(block * block_rows, (block + 1) * block_rows)
        total[rows] = jnp.dot(weights_ref[block], value, preferred_element_type=F32)
        if block % BACK_PART == 0:
            latent_in[block // BACK_PART].wait()
        for strip in strips(rows):
            out_ref[strip] = (latent_ref[strip].astype(F32) + total[strip]).astype(BF16)
        if block % BACK_PART == BACK_PART - 1:
            outs[block // BACK_PART].start()
    for copy in outs:
        copy.wait()


def whole(array):
    zeros = (0,) * array.ndim
    return pl.BlockSpec(array.shape, lambda *_: zeros)


def params(mib):
    return pltpu.CompilerParams(vmem_limit_bytes=mib * 1024 * 1024)


def cost(flops, *arrays):
    size = sum(a.size * a.dtype.itemsize for a in arrays)
    return pl.CostEstimate(flops=int(flops), bytes_accessed=int(size), transcendentals=0)


def shape(dims, kind=BF16):
    return jax.ShapeDtypeStruct(dims, kind)


def on_device(
    n_y,
    grid_features,
    mesh_latent,
    embed_in,
    embed_out,
    embed_gain,
    interp,
    block_mask,
    tile_list,
    mesh_up,
    mesh_down,
    mesh_gain,
):
    n_band = lax.axis_size("band")
    blk_count, list_len, tile_rows, block_rows = interp.shape
    channels, width = embed_in.shape
    node_rows = mesh_latent.shape[0]
    tiles = node_rows // tile_rows
    entries = blk_count * list_len
    slots = entries // n_band
    ring = Ring(n_band, n_y, tiles)
    chips, far = ring.chips, ring.far
    lists = (lax.axis_index("band").reshape(1), tile_list.T, block_mask.T)

    def in_hbm(array):
        return pltpu.with_memory_space_constraint(array, pltpu.HBM)

    gain = embed_gain.reshape(1, width)
    in_vmem = pl.BlockSpec(memory_space=pltpu.VMEM)
    in_any = pl.BlockSpec(memory_space=pl.ANY)
    grid_rows = blk_count * block_rows
    per_step = 4
    rows = per_step * block_rows
    counts = ((2 * chips - 2) * slots, 2 * slots)
    latent, near, sent_far, table = pl.pallas_call(
        functools.partial(embed_kernel, ring, per_step, slots),
        out_shape=[pltpu.HBM((blk_count * block_rows, width), BF16)]
        + [shape((count + 1, tile_rows, width)) for count in counts]
        + [shape((4, entries), jnp.int32)],
        grid_spec=pltpu.PrefetchScalarGridSpec(
            num_scalar_prefetch=3,
            grid=(blk_count // per_step,),
            in_specs=[
                pl.BlockSpec((channels, rows), lambda i, *_: (0, i)),
                whole(embed_in),
                whole(embed_out),
                whole(gain),
                pl.BlockSpec((per_step,) + interp.shape[1:], lambda i, *_: (i, 0, 0, 0)),
            ],
            out_specs=[pl.BlockSpec((rows, width), lambda i, *_: (i, 0))]
            + [pl.BlockSpec(memory_space=pltpu.VMEM)] * len(counts)
            + [pl.BlockSpec(memory_space=pltpu.SMEM)],
            scratch_shapes=[
                pltpu.VMEM((rows, width), F32),
                pltpu.VMEM((rows, width), BF16),
                pltpu.SMEM((2, n_band), jnp.int32),
                pltpu.SMEM((3, per_step * list_len), jnp.int32),
            ],
        ),
        compiler_params=params(24),
        cost_estimate=cost(
            2 * blk_count * block_rows * width * (channels + width + list_len * tile_rows),
            grid_features,
            interp,
        ),
        name="embed",
    )(lists[0], *map(in_hbm, lists[1:] + (grid_features.T, embed_in, embed_out, gain, interp)))
    other_far = ring.over_core(sent_far)

    dense = (tiles, tile_rows, width)

    def in_order(value, token):
        return pl.pallas_call(
            order_kernel,
            out_shape=shape(value.shape),
            in_specs=[in_any] * 2,
            out_specs=in_any,
            input_output_aliases={0: 0},
            compiler_params=params(1),
            cost_estimate=cost(0),
            name="in_order",
        )(value, token)

    first, second, near = pl.pallas_call(
        functools.partial(far_kernel, slots, chips),
        out_shape=[shape(dense)] * 2 + [shape(near.shape)],
        grid_spec=pltpu.PrefetchScalarGridSpec(
            num_scalar_prefetch=1,
            grid=(1,),
            in_specs=[in_vmem] * 2,
            out_specs=[in_vmem] * 3,
            scratch_shapes=[pltpu.VMEM(dense, F32)],
        ),
        input_output_aliases={1: 2},
        compiler_params=params(8),
        cost_estimate=cost(0, near),
        name="far_sums",
    )(table, near, other_far)
    other = ring.over_core(near)
    own = pl.pallas_call(
        functools.partial(own_kernel, slots, chips),
        out_shape=shape((chips - 2,) + dense, F32),
        grid_spec=pltpu.PrefetchScalarGridSpec(
            num_scalar_prefetch=1,
            grid=(chips - 2,),
            in_specs=[in_vmem] * 2,
            out_specs=in_vmem,
        ),
        compiler_params=params(8 if n_band <= 16 else 24),
        cost_estimate=cost(0, near, near),
        name="own_sums",
    )(table, near, other)

    def add_own(group, value, token):
        return pl.pallas_call(
            functools.partial(add_kernel, group),
            out_shape=shape(dense),
            in_specs=[in_vmem] * 2 + [in_any],
            out_specs=in_vmem,
            compiler_params=params(8),
            cost_estimate=cost(0),
            name=f"add_{group}",
        )(own, value, token)

    first, second = ring.over_first(first, far), ring.over_second(second, far - 1)
    turned = (blk_count, block_rows, list_len * tile_rows)
    per_step = 4
    token = weights = pl.pallas_call(
        turn_kernel,
        out_shape=shape(turned),
        grid=(blk_count // per_step,),
        in_specs=[pl.BlockSpec((per_step,) + interp.shape[1:], lambda i: (i, 0, 0, 0)), in_any],
        out_specs=pl.BlockSpec((per_step,) + turned[1:], lambda i: (i, 0, 0)),
        compiler_params=params(8),
        cost_estimate=cost(0, interp, interp),
        name="turn",
    )(interp, own)
    for group in range(chips - 3, 0, -1):
        distance = (group + 1) // 2
        if group % 2:
            token = add_own(group, first, token)
            first = ring.over_first(token, distance)
        else:
            token = add_own(group, second, token)
            second = ring.over_second(token, distance)

    mesh_gain = mesh_gain.reshape(1, width)
    piece, again = pl.pallas_call(
        mesh_kernel,
        out_shape=[shape((node_rows, width))] * 2,
        in_specs=[in_vmem] * 7,
        out_specs=[in_vmem] * 2,
        compiler_params=params(16),
        cost_estimate=cost(4 * node_rows * width * width, mesh_up, mesh_down),
        name="mesh_step",
    )(mesh_latent, mesh_up, mesh_down, mesh_gain, own, first, second)

    mine, theirs = [], []

    def pick(chosen, values):
        outs = [shape((len(chosen) * slots * tile_rows, width))] * 2
        if chosen == [0]:
            outs.append(shape((node_rows, width)))
        picked = pl.pallas_call(
            functools.partial(pick_kernel, chosen, slots, chips, tile_rows),
            out_shape=outs,
            grid_spec=pltpu.PrefetchScalarGridSpec(
                num_scalar_prefetch=1,
                grid=(1,),
                in_specs=[in_vmem] * len(values),
                out_specs=[in_vmem] * len(outs),
            ),
            compiler_params=params(8),
            cost_estimate=cost(0, *values),
            name=f"pick_{chosen[0]}",
        )(table, *values)
        mine.append(picked[0])
        theirs.append(ring.over_core(picked[1]))
        return picked[-1]

    first = ring.over_first(piece, 1)
    mesh_out = pick([0], [piece])
    second = ring.over_second(in_order(again, theirs[0]), 1)
    token = mine[0]
    for distance in range(1, far):
        first = in_order(first, token)
        onward = ring.over_first(first, distance + 1)
        second = in_order(second, first)
        if distance < far - 1:
            after = ring.over_second(second, distance + 1)
        pick([2 * distance - 1, 2 * distance], [first, second])
        token = mine[-1]
        first, second = onward, after
    tiles_far = [first, ring.over_core(first)]
    parts = mine + theirs
    joined = pl.pallas_call(
        join_kernel,
        out_shape=shape((sum(part.shape[0] for part in parts), width)),
        in_specs=[in_vmem] * len(parts),
        out_specs=in_vmem,
        compiler_params=params(8),
        cost_estimate=cost(0, *parts),
        name="join",
    )(*parts)

    grid_out = pl.pallas_call(
        functools.partial(back_kernel, list_len),
        out_shape=shape((grid_rows, width)),
        grid_spec=pltpu.PrefetchScalarGridSpec(
            num_scalar_prefetch=1,
            grid=(1,),
            in_specs=[in_vmem] * 4 + [in_any],
            out_specs=in_any,
            scratch_shapes=[
                pltpu.VMEM((grid_rows, width), BF16),
                pltpu.VMEM((grid_rows, width), F32),
                pltpu.VMEM((grid_rows, width), BF16),
                pltpu.SemaphoreType.DMA((2 * (blk_count // BACK_PART),)),
            ],
        ),
        compiler_params=params(32),
        cost_estimate=cost(2 * grid_rows * width * list_len * tile_rows, latent, latent, interp),
        name="back",
    )(table, weights, joined, *tiles_far, in_hbm(latent))
    return (grid_out, mesh_out)


def solution(mesh):
    placed = (
        P(("groups", "band"), None),
        P(("groups", "band"), None),
        P(),
        P(),
        P(),
        P("band", None, None, None),
        P(),
        P(),
        P(),
        P(),
        P(),
    )
    n_y = max(1, 4 // mesh.shape["groups"])
    return jax.shard_map(
        functools.partial(on_device, n_y),
        mesh=mesh,
        in_specs=placed,
        out_specs=(P(("groups", "band"), None), P(("groups", "band"), None)),
        check_vma=False,
    )
```

```python
import functools

import jax
import jax.numpy as jnp
from jax import lax
from jax.experimental import pallas as pl
from jax.experimental.pallas import tpu as pltpu
from jax.sharding import PartitionSpec as P

F32 = jnp.float32
BF16 = jnp.bfloat16
N_CORE = 2
STRIP = 32
PART = 2
BACK_PART = 4


def silu(values):
    half = 0.5 * values
    return half * (1.0 + jnp.tanh(half))


def layer_norm(values, gain):
    centred = values - jnp.mean(values, axis=-1, keepdims=True)
    spread = jnp.mean(centred * centred, axis=-1, keepdims=True)
    return centred * lax.rsqrt(spread + 1e-05) * gain


def split(value, size):
    if size & (size - 1) == 0:
        return lax.shift_right_logical(value, size.bit_length() - 1), value & (size - 1)
    return lax.div(value, size), lax.rem(value, size)


class Ring:
    def __init__(self, n_band, n_y, tiles):
        self.n_band, self.n_y, self.tiles = n_band, n_y, tiles
        self.chips = n_band // N_CORE
        self.far = self.chips // 2

    def place(self, index):
        chip, core = split(index, N_CORE)
        z, y = split(chip, self.n_y)
        return z + y * (self.chips - 1 - 2 * z), core

    def index(self, ring, core):
        ring = ring % self.chips
        n_z = self.chips // self.n_y
        z, y = (ring, 0) if ring < n_z else (self.chips - 1 - ring, 1)
        return (z * self.n_y + y) * N_CORE + core

    def over_core(self, value):
        return lax.ppermute(value, "band", [(i, i ^ 1) for i in range(self.n_band)])

    def over(self, value, right):
        pairs = []
        for i in range(self.n_band):
            chip, core = divmod(i, N_CORE)
            z, y = divmod(chip, self.n_y)
            ring = z if y == 0 else self.chips - 1 - z
            pairs.append((i, self.index(ring + (1 if core == right else -1), 1 - core)))
        return lax.ppermute(value, "band", pairs)

    def over_first(self, value, distance):
        return self.over(value, distance % 2)

    def over_second(self, value, distance):
        return self.over(value, (distance + 1) % 2)

    def seen(self, owner, me):
        ring, core = self.place(owner)
        my_ring, my_core = self.place(me)
        ahead = split(ring - my_ring + self.chips, self.chips)[1]
        left = (ahead > self.far).astype(jnp.int32)
        distance = jnp.where(ahead > self.far, self.chips - ahead, ahead)
        shared = (ahead == 0) | (ahead == self.far)
        stream = jnp.where(shared, 0, core ^ left)
        group = jnp.maximum(2 * distance - 1 + stream, 0)
        return ((distance + core) & 1) ^ my_core, group


def strips(rows):
    return [slice(r, r + STRIP) for r in range(rows.start, rows.stop, STRIP)]


def embed_kernel(
    ring, per_step, slots, me_ref, lists_ref, mask_ref,
    x_ref, w1_ref, w2_ref, gain_ref, interp_ref,
    latent_ref, near_ref, far_ref, table_ref, wide, hidden, owners_ref, places_ref,
):
    step = pl.program_id(0)
    me = me_ref[0]
    list_len, tile_rows, block_rows = interp_ref.shape[1:]
    blk_count = pl.num_programs(0) * per_step
    groups = ring.chips

    @pl.when(step == 0)
    def _():
        def note(owner, carry):
            across, group = ring.seen(owner, me)
            owners_ref[0, owner] = (across * groups + group) * slots
            owners_ref[1, owner] = ((across ^ 1) * groups + group) * slots
            return carry

        lax.fori_loop(0, ring.n_band, note, 0)

    def spot(who, block, k):
        owner, tile = split(lists_ref[k, (me ^ who) * blk_count + block], ring.tiles)
        slot = split(block * list_len + k, ring.n_band)[0]
        return owners_ref[who, owner] + slot, tile

    near_spare, far_spare = near_ref.shape[0] - 1, far_ref.shape[0] - 1
    for b in range(per_step):
        block = step * per_step + b
        for k in range(list_len):
            entry = block * list_len + k
            place, tile = spot(0, block, k)
            mask = mask_ref[k, me * blk_count + block]
            table_ref[0, place] = tile
            across = (place >= groups * slots).astype(jnp.int32)
            near = place - across * slots
            beyond = place - across * groups * slots >= (groups - 1) * slots
            table_ref[2, entry] = jnp.where(beyond, tile, near)
            table_ref[3, entry] = mask * jnp.where(beyond, 2 + across, 1)
            there, its_tile = spot(1, block, k)
            table_ref[1, there] = its_tile
            places_ref[0, b * list_len + k] = jnp.minimum(place, near_spare)
            places_ref[1, b * list_len + k] = jnp.where(
                place < near_spare, far_spare, place - near_spare
            )
            places_ref[2, b * list_len + k] = mask

    part_rows = PART * block_rows
    spans = [slice(i * part_rows, (i + 1) * part_rows) for i in range(per_step // PART)]
    for rows in spans:
        wide[rows] = lax.dot_general(
            x_ref[:, rows], w1_ref[...], (((0,), (0,)), ((), ())), preferred_element_type=F32
        )
    for rows in spans:
        for strip in strips(rows):
            hidden[strip] = silu(wide[strip]).astype(BF16)
        wide[rows] = jnp.dot(hidden[rows], w2_ref[...], preferred_element_type=F32)
    for number, rows in enumerate(spans):
        for strip in strips(rows):
            latent_ref[strip] = layer_norm(wide[strip], gain_ref[...]).astype(BF16)
        for b in range(number * PART, (number + 1) * PART):
            weights = interp_ref[b].reshape(list_len * tile_rows, block_rows)
            latent = latent_ref[b * block_rows : (b + 1) * block_rows]
            part = jnp.dot(weights, latent, preferred_element_type=F32)
            for k in range(list_len):
                number_here = b * list_len + k
                mask = places_ref[2, number_here].astype(F32)
                masked = (part[k * tile_rows : (k + 1) * tile_rows] * mask).astype(BF16)
                near_ref[places_ref[0, number_here]] = masked
                far_ref[places_ref[1, number_here]] = masked


def add_entries(total, table_ref, group, slots, kept, other, groups, first):
    for slot in range(slots):
        place = group * slots + slot
        total[table_ref[0, place]] += kept[place].astype(F32)
        total[table_ref[1, groups * slots + place]] += other[place + first * slots].astype(F32)


def far_kernel(slots, groups, table_ref, kept, other, far, before, same, total):
    del same
    for group, out in ((groups - 1, far), (groups - 2, before)):
        total[...] = jnp.zeros_like(total)
        add_entries(total, table_ref, group, slots, kept, other, groups, 2 - groups)
        out[...] = total[...].astype(BF16)


def own_kernel(slots, groups, table_ref, kept, other, own):
    group = pl.program_id(0)
    total = own.at[group]
    total[...] = jnp.zeros_like(total)
    add_entries(total, table_ref, group, slots, kept, other, groups, groups)


def add_kernel(group, own, came, token, out):
    del token
    out[...] = (own[group] + came[...].astype(F32)).astype(BF16)


def mesh_kernel(
    latent_ref, up_ref, down_ref, gain_ref, own, came, neighbour, first_ref, second_ref
):
    total = own[0] + came[...].astype(F32) + neighbour[...].astype(F32)
    mesh_in = latent_ref[...].astype(F32) + total.reshape(latent_ref.shape)
    normed = layer_norm(mesh_in, gain_ref[...]).astype(BF16)
    hidden = silu(jnp.dot(normed, up_ref[...], preferred_element_type=F32)).astype(BF16)
    out = (mesh_in + jnp.dot(hidden, down_ref[...], preferred_element_type=F32)).astype(BF16)
    first_ref[...] = out
    second_ref[...] = out


def order_kernel(*refs):
    del refs


def pick_kernel(chosen, slots, groups, tile_rows, table_ref, *refs):
    pieces, outs, copied = refs[: len(chosen)], refs[-2:], refs[len(chosen) : -2]
    for source, target in zip(copied[::2], copied[1::2]):
        target[...] = source[...]
    for number, group in enumerate(chosen):
        for slot in range(slots):
            for way, out in enumerate(outs):
                tile = table_ref[way, (way * groups + group) * slots + slot]
                rows = pl.ds(pl.multiple_of(tile * tile_rows, tile_rows), tile_rows)
                into = (number * slots + slot) * tile_rows
                out[into : into + tile_rows] = pieces[number][rows]


def turn_kernel(interp_ref, token, out_ref):
    del token
    for b in range(interp_ref.shape[0]):
        out_ref[b] = interp_ref[b].reshape(out_ref.shape[2], out_ref.shape[1]).T


def join_kernel(*refs):
    pieces, out = refs[:-1], refs[-1]
    start = 0
    for piece in pieces:
        out[start : start + piece.shape[0]] = piece[...]
        start += piece.shape[0]


def back_kernel(
    list_len, table_ref, weights_ref, near_ref, mine_ref, theirs_ref, latent_any,
    out_any, latent_ref, total, out_ref, sems,
):
    blk_count, block_rows, listed = weights_ref.shape
    tile_rows = listed // list_len
    part_rows = BACK_PART * block_rows
    parts = [pl.ds(i * part_rows, part_rows) for i in range(blk_count // BACK_PART)]
    latent_in, outs = [], []
    for i, rows in enumerate(parts):
        latent_in.append(
            pltpu.make_async_copy(latent_any.at[rows], latent_ref.at[rows], sems.at[i])
        )
        outs.append(
            pltpu.make_async_copy(out_ref.at[rows], out_any.at[rows], sems.at[len(parts) + i])
        )
    for copy in latent_in:
        copy.start()

    def rows_at(tile):
        return pl.ds(pl.multiple_of(tile * tile_rows, tile_rows), tile_rows)

    for block in range(blk_count):
        values = []
        for k in range(list_len):
            entry = block * list_len + k
            place, kind = table_ref[2, entry], table_ref[3, entry]
            here = jnp.where(kind > 1, 0, place)
            beyond = jnp.where(kind > 1, place, 0)
            value = near_ref[rows_at(here)]
            value = jnp.where(kind == 2, mine_ref[rows_at(beyond)], value)
            value = jnp.where(kind == 3, theirs_ref[rows_at(beyond)], value)
            values.append(jnp.where(kind > 0, value, jnp.zeros_like(value)))
        value = jnp.concatenate(values, axis=0)
        rows = slice(block * block_rows, (block + 1) * block_rows)
        total[rows] = jnp.dot(weights_ref[block], value, preferred_element_type=F32)
        if block % BACK_PART == 0:
            latent_in[block // BACK_PART].wait()
        for strip in strips(rows):
            out_ref[strip] = (latent_ref[strip].astype(F32) + total[strip]).astype(BF16)
        if block % BACK_PART == BACK_PART - 1:
            outs[block // BACK_PART].start()
    for copy in outs:
        copy.wait()


def whole(array):
    zeros = (0,) * array.ndim
    return pl.BlockSpec(array.shape, lambda *_: zeros)


def params(mib):
    return pltpu.CompilerParams(vmem_limit_bytes=mib * 1024 * 1024)


def cost(flops, *arrays):
    size = sum(a.size * a.dtype.itemsize for a in arrays)
    return pl.CostEstimate(flops=int(flops), bytes_accessed=int(size), transcendentals=0)


def shape(dims, kind=BF16):
    return jax.ShapeDtypeStruct(dims, kind)


def on_device(
    n_y,
    grid_features,
    mesh_latent,
    embed_in,
    embed_out,
    embed_gain,
    interp,
    block_mask,
    tile_list,
    mesh_up,
    mesh_down,
    mesh_gain,
):
    n_band = lax.axis_size("band")
    blk_count, list_len, tile_rows, block_rows = interp.shape
    channels, width = embed_in.shape
    node_rows = mesh_latent.shape[0]
    tiles = node_rows // tile_rows
    entries = blk_count * list_len
    slots = entries // n_band
    ring = Ring(n_band, n_y, tiles)
    chips, far = ring.chips, ring.far
    lists = (lax.axis_index("band").reshape(1), tile_list.T, block_mask.T)

    def in_hbm(array):
        return pltpu.with_memory_space_constraint(array, pltpu.HBM)

    gain = embed_gain.reshape(1, width)
    in_vmem = pl.BlockSpec(memory_space=pltpu.VMEM)
    in_any = pl.BlockSpec(memory_space=pl.ANY)
    grid_rows = blk_count * block_rows
    per_step = 4
    rows = per_step * block_rows
    counts = ((2 * chips - 2) * slots, 2 * slots)
    latent, near, sent_far, table = pl.pallas_call(
        functools.partial(embed_kernel, ring, per_step, slots),
        out_shape=[pltpu.HBM((blk_count * block_rows, width), BF16)]
        + [shape((count + 1, tile_rows, width)) for count in counts]
        + [shape((4, entries), jnp.int32)],
        grid_spec=pltpu.PrefetchScalarGridSpec(
            num_scalar_prefetch=3,
            grid=(blk_count // per_step,),
            in_specs=[
                pl.BlockSpec((channels, rows), lambda i, *_: (0, i)),
                whole(embed_in),
                whole(embed_out),
                whole(gain),
                pl.BlockSpec((per_step,) + interp.shape[1:], lambda i, *_: (i, 0, 0, 0)),
            ],
            out_specs=[pl.BlockSpec((rows, width), lambda i, *_: (i, 0))]
            + [pl.BlockSpec(memory_space=pltpu.VMEM)] * len(counts)
            + [pl.BlockSpec(memory_space=pltpu.SMEM)],
            scratch_shapes=[
                pltpu.VMEM((rows, width), F32),
                pltpu.VMEM((rows, width), BF16),
                pltpu.SMEM((2, n_band), jnp.int32),
                pltpu.SMEM((3, per_step * list_len), jnp.int32),
            ],
        ),
        compiler_params=params(24),
        cost_estimate=cost(
            2 * blk_count * block_rows * width * (channels + width + list_len * tile_rows),
            grid_features,
            interp,
        ),
        name="embed",
    )(lists[0], *map(in_hbm, lists[1:] + (grid_features.T, embed_in, embed_out, gain, interp)))
    other_far = ring.over_core(sent_far)

    dense = (tiles, tile_rows, width)

    def in_order(value, token):
        return pl.pallas_call(
            order_kernel,
            out_shape=shape(value.shape),
            in_specs=[in_any] * 2,
            out_specs=in_any,
            input_output_aliases={0: 0},
            compiler_params=params(1),
            cost_estimate=cost(0),
            name="in_order",
        )(value, token)

    first, second, near = pl.pallas_call(
        functools.partial(far_kernel, slots, chips),
        out_shape=[shape(dense)] * 2 + [shape(near.shape)],
        grid_spec=pltpu.PrefetchScalarGridSpec(
            num_scalar_prefetch=1,
            grid=(1,),
            in_specs=[in_vmem] * 2,
            out_specs=[in_vmem] * 3,
            scratch_shapes=[pltpu.VMEM(dense, F32)],
        ),
        input_output_aliases={1: 2},
        compiler_params=params(8),
        cost_estimate=cost(0, near),
        name="far_sums",
    )(table, near, other_far)
    other = ring.over_core(near)
    own = pl.pallas_call(
        functools.partial(own_kernel, slots, chips),
        out_shape=shape((chips - 2,) + dense, F32),
        grid_spec=pltpu.PrefetchScalarGridSpec(
            num_scalar_prefetch=1,
            grid=(chips - 2,),
            in_specs=[in_vmem] * 2,
            out_specs=in_vmem,
        ),
        compiler_params=params(8 if n_band <= 16 else 24),
        cost_estimate=cost(0, near, near),
        name="own_sums",
    )(table, near, other)

    def add_own(group, value, token):
        return pl.pallas_call(
            functools.partial(add_kernel, group),
            out_shape=shape(dense),
            in_specs=[in_vmem] * 2 + [in_any],
            out_specs=in_vmem,
            compiler_params=params(8),
            cost_estimate=cost(0),
            name=f"add_{group}",
        )(own, value, token)

    first, second = ring.over_first(first, far), ring.over_second(second, far - 1)
    turned = (blk_count, block_rows, list_len * tile_rows)
    per_step = 4
    token = weights = pl.pallas_call(
        turn_kernel,
        out_shape=shape(turned),
        grid=(blk_count // per_step,),
        in_specs=[pl.BlockSpec((per_step,) + interp.shape[1:], lambda i: (i, 0, 0, 0)), in_any],
        out_specs=pl.BlockSpec((per_step,) + turned[1:], lambda i: (i, 0, 0)),
        compiler_params=params(8),
        cost_estimate=cost(0, interp, interp),
        name="turn",
    )(interp, own)
    for group in range(chips - 3, 0, -1):
        distance = (group + 1) // 2
        if group % 2:
            token = add_own(group, first, token)
            first = ring.over_first(token, distance)
        else:
            token = add_own(group, second, token)
            second = ring.over_second(token, distance)

    mesh_gain = mesh_gain.reshape(1, width)
    piece, again = pl.pallas_call(
        mesh_kernel,
        out_shape=[shape((node_rows, width))] * 2,
        in_specs=[in_vmem] * 7,
        out_specs=[in_vmem] * 2,
        compiler_params=params(16),
        cost_estimate=cost(4 * node_rows * width * width, mesh_up, mesh_down),
        name="mesh_step",
    )(mesh_latent, mesh_up, mesh_down, mesh_gain, own, first, second)

    mine, theirs = [], []

    def pick(chosen, values, *copied):
        outs = [shape(v.shape) for v in copied]
        outs += [shape((len(chosen) * slots * tile_rows, width))] * 2
        picked = pl.pallas_call(
            functools.partial(pick_kernel, chosen, slots, chips, tile_rows),
            out_shape=outs,
            grid_spec=pltpu.PrefetchScalarGridSpec(
                num_scalar_prefetch=1,
                grid=(1,),
                in_specs=[in_vmem] * (len(values) + len(copied)),
                out_specs=[in_vmem] * len(outs),
            ),
            compiler_params=params(8),
            cost_estimate=cost(0, *values),
            name=f"pick_{chosen[0]}",
        )(table, *values, *copied)
        mine.append(picked[-2])
        theirs.append(ring.over_core(picked[-1]))
        return picked[:-2]

    first = ring.over_first(piece, 1)
    pick([0], [piece])
    second = ring.over_second(in_order(again, theirs[0]), 1)
    token = mine[0]
    for distance in range(1, far):
        first = in_order(first, token)
        onward = ring.over_first(first, distance + 1)
        second = in_order(second, first)
        if distance < far - 1:
            after = ring.over_second(second, distance + 1)
        copied = pick(
            [2 * distance - 1, 2 * distance], [first, second], *[piece] * (distance == 1)
        )
        if copied:
            mesh_out = copied[0]
        token = mine[-1]
        first, second = onward, after
    tiles_far = [first, ring.over_core(first)]
    parts = mine + theirs
    joined = pl.pallas_call(
        join_kernel,
        out_shape=shape((sum(part.shape[0] for part in parts), width)),
        in_specs=[in_vmem] * len(parts),
        out_specs=in_vmem,
        compiler_params=params(8),
        cost_estimate=cost(0, *parts),
        name="join",
    )(*parts)

    grid_out = pl.pallas_call(
        functools.partial(back_kernel, list_len),
        out_shape=shape((grid_rows, width)),
        grid_spec=pltpu.PrefetchScalarGridSpec(
            num_scalar_prefetch=1,
            grid=(1,),
            in_specs=[in_vmem] * 4 + [in_any],
            out_specs=in_any,
            scratch_shapes=[
                pltpu.VMEM((grid_rows, width), BF16),
                pltpu.VMEM((grid_rows, width), F32),
                pltpu.VMEM((grid_rows, width), BF16),
                pltpu.SemaphoreType.DMA((2 * (blk_count // BACK_PART),)),
            ],
        ),
        compiler_params=params(32),
        cost_estimate=cost(2 * grid_rows * width * list_len * tile_rows, latent, latent, interp),
        name="back",
    )(table, weights, joined, *tiles_far, in_hbm(latent))
    return (grid_out, mesh_out)


def solution(mesh):
    placed = (
        P(("groups", "band"), None),
        P(("groups", "band"), None),
        P(),
        P(),
        P(),
        P("band", None, None, None),
        P(),
        P(),
        P(),
        P(),
        P(),
    )
    n_y = max(1, 4 // mesh.shape["groups"])
    return jax.shard_map(
        functools.partial(on_device, n_y),
        mesh=mesh,
        in_specs=placed,
        out_specs=(P(("groups", "band"), None), P(("groups", "band"), None)),
        check_vma=False,
    )
```

```python
import functools

import jax
import jax.numpy as jnp
from jax import lax
from jax.experimental import pallas as pl
from jax.experimental.pallas import tpu as pltpu
from jax.sharding import PartitionSpec as P

F32 = jnp.float32
BF16 = jnp.bfloat16
N_CORE = 2
STRIP = 32
PART = 2
BACK_PART = 4


def silu(values):
    half = 0.5 * values
    return half * (1.0 + jnp.tanh(half))


def layer_norm(values, gain):
    centred = values - jnp.mean(values, axis=-1, keepdims=True)
    spread = jnp.mean(centred * centred, axis=-1, keepdims=True)
    return centred * lax.rsqrt(spread + 1e-05) * gain


def split(value, size):
    if size & (size - 1) == 0:
        return lax.shift_right_logical(value, size.bit_length() - 1), value & (size - 1)
    return lax.div(value, size), lax.rem(value, size)


class Ring:
    def __init__(self, n_band, n_y, tiles):
        self.n_band, self.n_y, self.tiles = n_band, n_y, tiles
        self.chips = n_band // N_CORE
        self.far = self.chips // 2

    def place(self, index):
        chip, core = split(index, N_CORE)
        z, y = split(chip, self.n_y)
        return z + y * (self.chips - 1 - 2 * z), core

    def index(self, ring, core):
        ring = ring % self.chips
        n_z = self.chips // self.n_y
        z, y = (ring, 0) if ring < n_z else (self.chips - 1 - ring, 1)
        return (z * self.n_y + y) * N_CORE + core

    def over_core(self, value):
        return lax.ppermute(value, "band", [(i, i ^ 1) for i in range(self.n_band)])

    def over(self, value, right):
        pairs = []
        for i in range(self.n_band):
            chip, core = divmod(i, N_CORE)
            z, y = divmod(chip, self.n_y)
            ring = z if y == 0 else self.chips - 1 - z
            pairs.append((i, self.index(ring + (1 if core == right else -1), 1 - core)))
        return lax.ppermute(value, "band", pairs)

    def over_first(self, value, distance):
        return self.over(value, distance % 2)

    def over_second(self, value, distance):
        return self.over(value, (distance + 1) % 2)

    def seen(self, owner, me):
        ring, core = self.place(owner)
        my_ring, my_core = self.place(me)
        ahead = split(ring - my_ring + self.chips, self.chips)[1]
        left = (ahead > self.far).astype(jnp.int32)
        distance = jnp.where(ahead > self.far, self.chips - ahead, ahead)
        shared = (ahead == 0) | (ahead == self.far)
        stream = jnp.where(shared, 0, core ^ left)
        group = jnp.maximum(2 * distance - 1 + stream, 0)
        return ((distance + core) & 1) ^ my_core, group


def strips(rows):
    return [slice(r, r + STRIP) for r in range(rows.start, rows.stop, STRIP)]


def embed_kernel(
    ring, per_step, slots, me_ref, lists_ref, mask_ref,
    x_ref, w1_ref, w2_ref, gain_ref, interp_ref,
    latent_ref, near_ref, far_ref, table_ref, wide, hidden, owners_ref, places_ref,
):
    step = pl.program_id(0)
    me = me_ref[0]
    list_len, tile_rows, block_rows = interp_ref.shape[1:]
    blk_count = pl.num_programs(0) * per_step
    groups = ring.chips

    @pl.when(step == 0)
    def _():
        def note(owner, carry):
            across, group = ring.seen(owner, me)
            owners_ref[0, owner] = (across * groups + group) * slots
            owners_ref[1, owner] = ((across ^ 1) * groups + group) * slots
            return carry

        lax.fori_loop(0, ring.n_band, note, 0)

    def spot(who, block, k):
        owner, tile = split(lists_ref[k, (me ^ who) * blk_count + block], ring.tiles)
        slot = split(block * list_len + k, ring.n_band)[0]
        return owners_ref[who, owner] + slot, tile

    near_spare, far_spare = near_ref.shape[0] - 1, far_ref.shape[0] - 1
    for b in range(per_step):
        block = step * per_step + b
        for k in range(list_len):
            entry = block * list_len + k
            place, tile = spot(0, block, k)
            mask = mask_ref[k, me * blk_count + block]
            table_ref[0, place] = tile
            across = (place >= groups * slots).astype(jnp.int32)
            near = place - across * slots
            beyond = place - across * groups * slots >= (groups - 1) * slots
            table_ref[2, entry] = jnp.where(beyond, tile, near)
            table_ref[3, entry] = mask * jnp.where(beyond, 2 + across, 1)
            there, its_tile = spot(1, block, k)
            table_ref[1, there] = its_tile
            places_ref[0, b * list_len + k] = jnp.minimum(place, near_spare)
            places_ref[1, b * list_len + k] = jnp.where(
                place < near_spare, far_spare, place - near_spare
            )
            places_ref[2, b * list_len + k] = mask

    part_rows = PART * block_rows
    spans = [slice(i * part_rows, (i + 1) * part_rows) for i in range(per_step // PART)]
    for rows in spans:
        wide[rows] = lax.dot_general(
            x_ref[:, rows], w1_ref[...], (((0,), (0,)), ((), ())), preferred_element_type=F32
        )
    for rows in spans:
        for strip in strips(rows):
            hidden[strip] = silu(wide[strip]).astype(BF16)
        wide[rows] = jnp.dot(hidden[rows], w2_ref[...], preferred_element_type=F32)
    for number, rows in enumerate(spans):
        for strip in strips(rows):
            latent_ref[strip] = layer_norm(wide[strip], gain_ref[...]).astype(BF16)
        for b in range(number * PART, (number + 1) * PART):
            weights = interp_ref[b].reshape(list_len * tile_rows, block_rows)
            latent = latent_ref[b * block_rows : (b + 1) * block_rows]
            part = jnp.dot(weights, latent, preferred_element_type=F32)
            for k in range(list_len):
                number_here = b * list_len + k
                mask = places_ref[2, number_here].astype(F32)
                masked = (part[k * tile_rows : (k + 1) * tile_rows] * mask).astype(BF16)
                near_ref[places_ref[0, number_here]] = masked
                far_ref[places_ref[1, number_here]] = masked


def add_entries(total, table_ref, group, slots, kept, other, groups, first):
    for slot in range(slots):
        place = group * slots + slot
        total[table_ref[0, place]] += kept[place].astype(F32)
        total[table_ref[1, groups * slots + place]] += other[place + first * slots].astype(F32)


def far_kernel(slots, groups, table_ref, kept, other, far, before, same, total):
    del same
    for group, out in ((groups - 1, far), (groups - 2, before)):
        total[...] = jnp.zeros_like(total)
        add_entries(total, table_ref, group, slots, kept, other, groups, 2 - groups)
        out[...] = total[...].astype(BF16)


def own_kernel(slots, groups, table_ref, kept, other, own):
    group = pl.program_id(0)
    total = own.at[group]
    total[...] = jnp.zeros_like(total)
    add_entries(total, table_ref, group, slots, kept, other, groups, groups)


def add_kernel(group, own, came, token, out):
    del token
    out[...] = (own[group] + came[...].astype(F32)).astype(BF16)


def mesh_kernel(
    latent_ref, up_ref, down_ref, gain_ref, own, came, neighbour, first_ref, second_ref
):
    total = own[0] + came[...].astype(F32) + neighbour[...].astype(F32)
    mesh_in = latent_ref[...].astype(F32) + total.reshape(latent_ref.shape)
    normed = layer_norm(mesh_in, gain_ref[...]).astype(BF16)
    hidden = silu(jnp.dot(normed, up_ref[...], preferred_element_type=F32)).astype(BF16)
    out = (mesh_in + jnp.dot(hidden, down_ref[...], preferred_element_type=F32)).astype(BF16)
    first_ref[...] = out
    second_ref[...] = out


def order_kernel(*refs):
    del refs


def pick_kernel(chosen, slots, groups, tile_rows, table_ref, *refs):
    pieces, outs = refs[: len(chosen)], refs[len(chosen) :]
    for out in outs[2:]:
        out[...] = pieces[0][...]
    for number, group in enumerate(chosen):
        for slot in range(slots):
            for way, out in enumerate(outs[:2]):
                tile = table_ref[way, (way * groups + group) * slots + slot]
                rows = pl.ds(pl.multiple_of(tile * tile_rows, tile_rows), tile_rows)
                into = (number * slots + slot) * tile_rows
                out[into : into + tile_rows] = pieces[number][rows]


def turn_kernel(interp_ref, token, out_ref):
    del token
    for b in range(interp_ref.shape[0]):
        out_ref[b] = interp_ref[b].reshape(out_ref.shape[2], out_ref.shape[1]).T


def join_kernel(*refs):
    pieces, out = refs[:-1], refs[-1]
    start = 0
    for piece in pieces:
        out[start : start + piece.shape[0]] = piece[...]
        start += piece.shape[0]


def back_kernel(
    list_len, table_ref, weights_ref, near_ref, mine_ref, theirs_ref, latent_any,
    out_any, latent_ref, total, out_ref, sems,
):
    blk_count, block_rows, listed = weights_ref.shape
    tile_rows = listed // list_len
    part_rows = BACK_PART * block_rows
    parts = [pl.ds(i * part_rows, part_rows) for i in range(blk_count // BACK_PART)]
    latent_in, outs = [], []
    for i, rows in enumerate(parts):
        latent_in.append(
            pltpu.make_async_copy(latent_any.at[rows], latent_ref.at[rows], sems.at[i])
        )
        outs.append(
            pltpu.make_async_copy(out_ref.at[rows], out_any.at[rows], sems.at[len(parts) + i])
        )
    for copy in latent_in:
        copy.start()

    def rows_at(tile):
        return pl.ds(pl.multiple_of(tile * tile_rows, tile_rows), tile_rows)

    for block in range(blk_count):
        values = []
        for k in range(list_len):
            entry = block * list_len + k
            place, kind = table_ref[2, entry], table_ref[3, entry]
            here = jnp.where(kind > 1, 0, place)
            beyond = jnp.where(kind > 1, place, 0)
            value = near_ref[rows_at(here)]
            value = jnp.where(kind == 2, mine_ref[rows_at(beyond)], value)
            value = jnp.where(kind == 3, theirs_ref[rows_at(beyond)], value)
            values.append(jnp.where(kind > 0, value, jnp.zeros_like(value)))
        value = jnp.concatenate(values, axis=0)
        rows = slice(block * block_rows, (block + 1) * block_rows)
        total[rows] = jnp.dot(weights_ref[block], value, preferred_element_type=F32)
        if block % BACK_PART == 0:
            latent_in[block // BACK_PART].wait()
        for strip in strips(rows):
            out_ref[strip] = (latent_ref[strip].astype(F32) + total[strip]).astype(BF16)
        if block % BACK_PART == BACK_PART - 1:
            outs[block // BACK_PART].start()
    for copy in outs:
        copy.wait()


def whole(array):
    zeros = (0,) * array.ndim
    return pl.BlockSpec(array.shape, lambda *_: zeros)


def params(mib):
    return pltpu.CompilerParams(vmem_limit_bytes=mib * 1024 * 1024)


def cost(flops, *arrays):
    size = sum(a.size * a.dtype.itemsize for a in arrays)
    return pl.CostEstimate(flops=int(flops), bytes_accessed=int(size), transcendentals=0)


def shape(dims, kind=BF16):
    return jax.ShapeDtypeStruct(dims, kind)


def on_device(
    n_y,
    grid_features,
    mesh_latent,
    embed_in,
    embed_out,
    embed_gain,
    interp,
    block_mask,
    tile_list,
    mesh_up,
    mesh_down,
    mesh_gain,
):
    n_band = lax.axis_size("band")
    blk_count, list_len, tile_rows, block_rows = interp.shape
    channels, width = embed_in.shape
    node_rows = mesh_latent.shape[0]
    tiles = node_rows // tile_rows
    entries = blk_count * list_len
    slots = entries // n_band
    ring = Ring(n_band, n_y, tiles)
    chips, far = ring.chips, ring.far
    lists = (lax.axis_index("band").reshape(1), tile_list.T, block_mask.T)

    def in_hbm(array):
        return pltpu.with_memory_space_constraint(array, pltpu.HBM)

    gain = embed_gain.reshape(1, width)
    in_vmem = pl.BlockSpec(memory_space=pltpu.VMEM)
    in_any = pl.BlockSpec(memory_space=pl.ANY)
    grid_rows = blk_count * block_rows
    per_step = 8
    rows = per_step * block_rows
    counts = ((2 * chips - 2) * slots, 2 * slots)
    latent, near, sent_far, table = pl.pallas_call(
        functools.partial(embed_kernel, ring, per_step, slots),
        out_shape=[pltpu.HBM((blk_count * block_rows, width), BF16)]
        + [shape((count + 1, tile_rows, width)) for count in counts]
        + [shape((4, entries), jnp.int32)],
        grid_spec=pltpu.PrefetchScalarGridSpec(
            num_scalar_prefetch=3,
            grid=(blk_count // per_step,),
            in_specs=[
                pl.BlockSpec((channels, rows), lambda i, *_: (0, i)),
                whole(embed_in),
                whole(embed_out),
                whole(gain),
                pl.BlockSpec((per_step,) + interp.shape[1:], lambda i, *_: (i, 0, 0, 0)),
            ],
            out_specs=[pl.BlockSpec((rows, width), lambda i, *_: (i, 0))]
            + [pl.BlockSpec(memory_space=pltpu.VMEM)] * len(counts)
            + [pl.BlockSpec(memory_space=pltpu.SMEM)],
            scratch_shapes=[
                pltpu.VMEM((rows, width), F32),
                pltpu.VMEM((rows, width), BF16),
                pltpu.SMEM((2, n_band), jnp.int32),
                pltpu.SMEM((3, per_step * list_len), jnp.int32),
            ],
        ),
        compiler_params=params(32),
        cost_estimate=cost(
            2 * blk_count * block_rows * width * (channels + width + list_len * tile_rows),
            grid_features,
            interp,
        ),
        name="embed",
    )(lists[0], *map(in_hbm, lists[1:] + (grid_features.T, embed_in, embed_out, gain, interp)))
    other_far = ring.over_core(sent_far)

    dense = (tiles, tile_rows, width)

    def in_order(value, token):
        return pl.pallas_call(
            order_kernel,
            out_shape=shape(value.shape),
            in_specs=[in_any] * 2,
            out_specs=in_any,
            input_output_aliases={0: 0},
            compiler_params=params(1),
            cost_estimate=cost(0),
            name="in_order",
        )(value, token)

    first, second, near = pl.pallas_call(
        functools.partial(far_kernel, slots, chips),
        out_shape=[shape(dense)] * 2 + [shape(near.shape)],
        grid_spec=pltpu.PrefetchScalarGridSpec(
            num_scalar_prefetch=1,
            grid=(1,),
            in_specs=[in_vmem] * 2,
            out_specs=[in_vmem] * 3,
            scratch_shapes=[pltpu.VMEM(dense, F32)],
        ),
        input_output_aliases={1: 2},
        compiler_params=params(8),
        cost_estimate=cost(0, near),
        name="far_sums",
    )(table, near, other_far)
    other = ring.over_core(near)
    own = pl.pallas_call(
        functools.partial(own_kernel, slots, chips),
        out_shape=shape((chips - 2,) + dense, F32),
        grid_spec=pltpu.PrefetchScalarGridSpec(
            num_scalar_prefetch=1,
            grid=(chips - 2,),
            in_specs=[in_vmem] * 2,
            out_specs=in_vmem,
        ),
        compiler_params=params(8 if n_band <= 16 else 24),
        cost_estimate=cost(0, near, near),
        name="own_sums",
    )(table, near, other)

    def add_own(group, value, token):
        return pl.pallas_call(
            functools.partial(add_kernel, group),
            out_shape=shape(dense),
            in_specs=[in_vmem] * 2 + [in_any],
            out_specs=in_vmem,
            compiler_params=params(8),
            cost_estimate=cost(0),
            name=f"add_{group}",
        )(own, value, token)

    first, second = ring.over_first(first, far), ring.over_second(second, far - 1)
    turned = (blk_count, block_rows, list_len * tile_rows)
    per_step = 4
    token = weights = pl.pallas_call(
        turn_kernel,
        out_shape=shape(turned),
        grid=(blk_count // per_step,),
        in_specs=[pl.BlockSpec((per_step,) + interp.shape[1:], lambda i: (i, 0, 0, 0)), in_any],
        out_specs=pl.BlockSpec((per_step,) + turned[1:], lambda i: (i, 0, 0)),
        compiler_params=params(8),
        cost_estimate=cost(0, interp, interp),
        name="turn",
    )(interp, own)
    for group in range(chips - 3, 0, -1):
        distance = (group + 1) // 2
        if group % 2:
            token = add_own(group, first, token)
            first = ring.over_first(token, distance)
        else:
            token = add_own(group, second, token)
            second = ring.over_second(token, distance)

    mesh_gain = mesh_gain.reshape(1, width)
    piece, again = pl.pallas_call(
        mesh_kernel,
        out_shape=[shape((node_rows, width))] * 2,
        in_specs=[in_vmem] * 7,
        out_specs=[in_vmem] * 2,
        compiler_params=params(16),
        cost_estimate=cost(4 * node_rows * width * width, mesh_up, mesh_down),
        name="mesh_step",
    )(mesh_latent, mesh_up, mesh_down, mesh_gain, own, first, second)

    mine, theirs = [], []

    def pick(chosen, values):
        outs = [shape((len(chosen) * slots * tile_rows, width))] * 2
        if chosen == [0]:
            outs.append(shape((node_rows, width)))
        picked = pl.pallas_call(
            functools.partial(pick_kernel, chosen, slots, chips, tile_rows),
            out_shape=outs,
            grid_spec=pltpu.PrefetchScalarGridSpec(
                num_scalar_prefetch=1,
                grid=(1,),
                in_specs=[in_vmem] * len(values),
                out_specs=[in_vmem] * len(outs),
            ),
            compiler_params=params(8),
            cost_estimate=cost(0, *values),
            name=f"pick_{chosen[0]}",
        )(table, *values)
        mine.append(picked[0])
        theirs.append(ring.over_core(picked[1]))
        return picked[-1]

    first = ring.over_first(piece, 1)
    mesh_out = pick([0], [piece])
    second = ring.over_second(in_order(again, theirs[0]), 1)
    token = mine[0]
    for distance in range(1, far):
        first = in_order(first, token)
        onward = ring.over_first(first, distance + 1)
        second = in_order(second, first)
        if distance < far - 1:
            after = ring.over_second(second, distance + 1)
        pick([2 * distance - 1, 2 * distance], [first, second])
        token = mine[-1]
        first, second = onward, after
    tiles_far = [first, ring.over_core(first)]
    parts = mine + theirs
    joined = pl.pallas_call(
        join_kernel,
        out_shape=shape((sum(part.shape[0] for part in parts), width)),
        in_specs=[in_vmem] * len(parts),
        out_specs=in_vmem,
        compiler_params=params(8),
        cost_estimate=cost(0, *parts),
        name="join",
    )(*parts)

    grid_out = pl.pallas_call(
        functools.partial(back_kernel, list_len),
        out_shape=shape((grid_rows, width)),
        grid_spec=pltpu.PrefetchScalarGridSpec(
            num_scalar_prefetch=1,
            grid=(1,),
            in_specs=[in_vmem] * 4 + [in_any],
            out_specs=in_any,
            scratch_shapes=[
                pltpu.VMEM((grid_rows, width), BF16),
                pltpu.VMEM((grid_rows, width), F32),
                pltpu.VMEM((grid_rows, width), BF16),
                pltpu.SemaphoreType.DMA((2 * (blk_count // BACK_PART),)),
            ],
        ),
        compiler_params=params(32),
        cost_estimate=cost(2 * grid_rows * width * list_len * tile_rows, latent, latent, interp),
        name="back",
    )(table, weights, joined, *tiles_far, in_hbm(latent))
    return (grid_out, mesh_out)


def solution(mesh):
    placed = (
        P(("groups", "band"), None),
        P(("groups", "band"), None),
        P(),
        P(),
        P(),
        P("band", None, None, None),
        P(),
        P(),
        P(),
        P(),
        P(),
    )
    n_y = max(1, 4 // mesh.shape["groups"])
    return jax.shard_map(
        functools.partial(on_device, n_y),
        mesh=mesh,
        in_specs=placed,
        out_specs=(P(("groups", "band"), None), P(("groups", "band"), None)),
        check_vma=False,
    )
```
